32 devices in a mesh: user: 32 (over z, y, x, core).
Axes of the slice: x: 2, y: 2, z: 4, core: 2. Of those that a mesh axis runs over, the one named last changes fastest.
Arguments:
- ratings: bfloat16 [32, 3, 6, 128, 128], P('user'), may hold values from -6 to 6
- tile_index: int32 [32, 3, 6], P('user'), may hold values from 0 to 8, as said below
- tile_count: int32 [32, 3], P('user'), may hold values from 1 to 6, as said below
- side_features: bfloat16 [12288, 1024], P('user'), may hold values from -6 to 6
- user_factors: float32 [12288, 256], P('user'), may hold values from -3 to 3
- item_factors: float32 [12288, 256], P('user'), may hold values from -3 to 3
- prior_weights: float32 [1024, 256], replicated, may hold values from -0.1875 to 0.1875
- user_noise: bfloat16 [3, 12288, 256], P(None, 'user'), may hold values from -6 to 6
- item_noise: bfloat16 [3, 12288, 256], P(None, 'user'), may hold values from -6 to 6
Outputs:
- users_out: float32 [12288, 256], P('user')
- items_held: float32 [12288, 256], P('user')
- weights_out: float32 [1024, 256], P('user')
The draws below stay inside these ranges and needn't reach their ends.
Inputs may be any that keep to these rules, and one draw needn't show every extreme that they name: `tile_index`: code r * 3 + c of a tile; the codes of one device and stratum are distinct. `tile_count`: live slots are the first ones; in every stratum some device has 6.
All inputs are finite; a program needn't handle non-finite values.
Results may differ from the reference program's by a relative error of at most 0.0013.
The reference program's roundings to bfloat16 on the way (of `offset` and `errb`) count: a program that leaves them out, or rounds other values in their place, can miss the bound.
Values sent between devices are 32-bit elements; how exact they have to be, the bound alone decides.
No kernel may reach another device: no remote copies, remote signals or barrier semaphores. Data moves between devices by JAX's collectives and lax.ppermute only.
A program may use at most 64 MiB of HBM per device.

```python
import math
import jax
import jax.numpy as jnp
from jax import lax

RANK = 256
FEAT = 1024
TILE = 128
STRATA = 3
USR_DEV = 384
MAXT = 6
USERS = 12288
ITEMS = 12288
N_USER = 32


def draw_tile_index(key, part):
    grid = USR_DEV // TILE
    cells = grid * grid
    scores = jax.random.randint(key, (N_USER, STRATA, cells), 0, 1 << 18) * 4096 + jnp.arange(cells, dtype=jnp.int32)
    order = jnp.argsort(scores, axis=-1, stable=True)
    return order[:, :, :MAXT].astype(jnp.int32)


def draw_tile_count(key, part):
    first, second = jax.random.split(jax.random.fold_in(key, 7))
    counts = jax.random.randint(first, (N_USER, STRATA), 1, MAXT + 1)
    heavy = jax.random.randint(second, (STRATA,), 0, N_USER)
    place = jnp.arange(N_USER, dtype=jnp.int32)[:, None] == heavy[None, :]
    return jnp.where(place, MAXT, counts).astype(jnp.int32)


def draw_side_features(key, part):
    inner = jax.random.fold_in(key, 11)
    values = jnp.clip(jax.random.normal(inner, (USERS, FEAT), jnp.float32), -6.0, 6.0)
    return values.astype(jnp.bfloat16)


def block_levels(stream_key, dims, cuts, least, largest):
    def one(dim, shards_of):
        draws = jax.random.uniform(jax.random.fold_in(jax.random.fold_in(stream_key, 6), dim), (shards_of,), jnp.float32, least / len(cuts), largest / len(cuts))
        return jnp.repeat(jnp.exp(draws), dims[dim] // shards_of).reshape((-1,) + (1,) * (len(dims) - dim - 1))

    level = one(*cuts[0])
    for cut in cuts[1:]:
        level = level * one(*cut)
    return level


def gaussian(own_key, dims, scale, reach, pieces=(), held_as=jnp.bfloat16):
    array = scale * jax.random.normal(own_key, dims, jnp.float32)
    if pieces:
        array = array * block_levels(own_key, dims, pieces, -0.22, 0.18)
    return jnp.clip(array, -reach, reach).astype(held_as)


def setup_inputs(seed: int = 0) -> dict:
    seeds = jax.random.split(jax.random.key(seed), 10)
    return {
        "ratings": gaussian(seeds[0], (N_USER, STRATA, MAXT, TILE, TILE), 1.0, 6.0, ((0, 32),)),
        "tile_index": draw_tile_index(jax.random.fold_in(seeds[9], 71), 0),
        "tile_count": draw_tile_count(jax.random.fold_in(seeds[9], 71), 0),
        "side_features": draw_side_features(jax.random.fold_in(seeds[9], 71), 0),
        "user_factors": gaussian(seeds[4], (USERS, RANK), 0.5, 3.0, ((0, 32),), jnp.float32),
        "item_factors": gaussian(seeds[5], (ITEMS, RANK), 0.5, 3.0, ((0, 32),), jnp.float32),
        "prior_weights": gaussian(seeds[6], (FEAT, RANK), FEAT ** -0.5, 0.1875, (), jnp.float32),
        "user_noise": gaussian(seeds[7], (STRATA, USERS, RANK), 1.0, 6.0, ((1, 32),)),
        "item_noise": gaussian(seeds[8], (STRATA, ITEMS, RANK), 1.0, 6.0, ((1, 32),)),
    }


step_size = 0.01
prior_prec = 8.0
item_prec = 1.0
weight_decay = 1.0
rate_scale = 0.04

def reference(ratings, tile_index, tile_count, side_features, user_factors, item_factors, prior_weights, user_noise, item_noise):
    grid = USR_DEV // TILE
    rate = rate_scale / (USR_DEV * N_USER)
    noise_scale = math.sqrt(2.0 * step_size)
    users = user_factors
    items = item_factors
    weights = prior_weights
    slot = jnp.arange(MAXT, dtype=jnp.int32)
    for stratum in range(STRATA):
        mean = jnp.dot(side_features, weights.astype(jnp.bfloat16), preferred_element_type=jnp.float32)
        offset = (users - mean).astype(jnp.bfloat16)
        user_b = lax.optimization_barrier(users.astype(jnp.bfloat16)).reshape(N_USER, grid, TILE, RANK)
        item_b = lax.optimization_barrier(items.astype(jnp.bfloat16)).reshape(N_USER, grid, TILE, RANK)
        codes = tile_index[:, stratum]
        live = (slot[None, :] < tile_count[:, stratum][:, None]).astype(jnp.float32)

        def one(inputs):
            tiles, code, mask, ub, vb = inputs
            rows = code // grid
            cols = code % grid
            urows = ub[rows].astype(jnp.float32)
            vrows = vb[cols].astype(jnp.float32)
            err = tiles.astype(jnp.float32) - jnp.einsum('tak,tbk->tab', urows, vrows)
            err = err * mask[:, None, None]
            sse = jnp.sum(err * err)
            errb = lax.optimization_barrier(err.astype(jnp.bfloat16)).astype(jnp.float32)
            gu = jnp.einsum('tab,tbk->tak', errb, vrows)
            gv = jnp.einsum('tab,tak->tbk', errb, urows)
            grad_u = jnp.zeros((grid, TILE, RANK), jnp.float32).at[rows].add(gu)
            grad_v = jnp.zeros((grid, TILE, RANK), jnp.float32).at[cols].add(gv)
            return (sse, grad_u, grad_v)
        sse, grad_u, grad_v = lax.map(one, (ratings[:, stratum], codes, live, user_b, item_b))
        total_sse = jnp.sum(sse)
        total_count = jnp.sum(tile_count[:, stratum].astype(jnp.float32)) * float(TILE * TILE)
        precision = (1.0 + total_count / 2.0) / (1.0 + total_sse / 2.0)
        grad_u = grad_u.reshape(USERS, RANK)
        grad_v = grad_v.reshape(ITEMS, RANK)
        grad_w = lax.dot_general(side_features, offset, (((0,), (0,)), ((), ())), preferred_element_type=jnp.float32)
        new_users = users + step_size * (precision * grad_u - prior_prec * (users - mean)) + noise_scale * user_noise[stratum].astype(jnp.float32)
        new_items = items + step_size * (precision * grad_v - item_prec * items) + noise_scale * item_noise[stratum].astype(jnp.float32)
        weights = weights + rate * (prior_prec * grad_w - weight_decay * weights)
        users = new_users
        if stratum + 1 < STRATA:
            items = jnp.roll(new_items, USR_DEV, axis=0)
        else:
            items = new_items
    return (users, items, weights)
```

```python
import functools
import math

import jax
import jax.numpy as jnp
from jax import lax
from jax.experimental import pallas as pl
from jax.experimental.pallas import tpu as pltpu
from jax.sharding import PartitionSpec as P

step_size = 0.01
prior_prec = 8.0
item_prec = 1.0
weight_decay = 1.0
rate_scale = 0.04

NT = (((1,), (1,)), ((), ()))
TN = (((0,), (0,)), ((), ()))
VMEM = pl.BlockSpec(memory_space=pltpu.VMEM)
SMEM = pl.BlockSpec(memory_space=pltpu.SMEM)


def dot(a, b, dims=(((1,), (0,)), ((), ()))):
    return lax.dot_general(a, b, dims, preferred_element_type=jnp.float32)


def tile_kernel(codes, count, tiles, users, items, grad_u, grad_v, stats, pred, err_b):
    slots, tile, _ = tiles.shape
    grid = items.shape[0] // tile
    user_b = users[...].astype(jnp.bfloat16)
    item_b = items[...].astype(jnp.bfloat16)
    pred[...] = dot(user_b, item_b, NT)
    err_b[...] = jnp.zeros_like(err_b)
    live_slots = count[0]
    sse = jnp.zeros((tile, tile), jnp.float32)
    for slot in range(slots):
        code = codes[slot]
        rows = pl.ds(pl.multiple_of(code // grid * tile, tile), tile)
        cols = pl.ds(pl.multiple_of(code % grid * tile, tile), tile)
        live = (slot < live_slots).astype(jnp.float32)
        err = (tiles[slot].astype(jnp.float32) - pred[rows, cols]) * live
        sse = sse + err * err
        err_b[rows, cols] = err.astype(jnp.bfloat16)
    err_all = err_b[...]
    grad_u[...] = dot(err_all, item_b)
    grad_v[...] = dot(err_all, user_b, TN)
    total = jnp.sum(sse)
    counted = live_slots.astype(jnp.float32) * float(tile * tile)
    lane = lax.broadcasted_iota(jnp.int32, stats.shape, 1)
    stats[...] = jnp.where(lane == 0, total, jnp.where(lane == 1, counted, 0.0))


def tile_pass(codes, count, tiles, users, items):
    rows, rank = users.shape
    f32 = jnp.float32
    return pl.pallas_call(
        tile_kernel,
        out_shape=(
            jax.ShapeDtypeStruct((rows, rank), f32),
            jax.ShapeDtypeStruct((rows, rank), f32),
            jax.ShapeDtypeStruct((8, rank), f32),
        ),
        in_specs=[SMEM, SMEM, VMEM, VMEM, VMEM],
        out_specs=(VMEM, VMEM, VMEM),
        scratch_shapes=[
            pltpu.VMEM((rows, rows), f32),
            pltpu.VMEM((rows, rows), jnp.bfloat16),
        ],
        compiler_params=pltpu.CompilerParams(vmem_limit_bytes=16 << 20),
        cost_estimate=pl.CostEstimate(
            flops=6 * rows * rows * rank, bytes_accessed=4 * rows * rank * 4, transcendentals=0
        ),
        name="tile_pass",
    )(codes, count, tiles, users, items)


def prior_kernel(order, feats, weights, users, mean, grad_w):
    weights_b = weights[...].astype(jnp.bfloat16)
    mean_now = dot(feats[...], weights_b)
    mean[...] = mean_now
    offset = (users[...] - mean_now).astype(jnp.bfloat16)
    full = dot(feats[...], offset, TN)
    if order is None:
        grad_w[...] = full
    else:
        block = full.shape[0] // len(order)
        for place, source in enumerate(order):
            grad_w[place * block : (place + 1) * block, :] = full[
                source * block : (source + 1) * block, :
            ]


def prior_pass(feats, weights, users, order=None):
    rows, rank = users.shape
    feat = weights.shape[0]
    return pl.pallas_call(
        functools.partial(prior_kernel, order),
        out_shape=(
            jax.ShapeDtypeStruct((rows, rank), jnp.float32),
            jax.ShapeDtypeStruct((feat, rank), jnp.float32),
        ),
        in_specs=[VMEM, VMEM, VMEM],
        out_specs=(VMEM, VMEM),
        compiler_params=pltpu.CompilerParams(vmem_limit_bytes=16 << 20),
        cost_estimate=pl.CostEstimate(
            flops=4 * rows * feat * rank, bytes_accessed=8 * feat * rank, transcendentals=0
        ),
        name="prior_pass",
    )(feats, weights, users)


def bit_orders(devices):
    bits = devices.bit_length() - 1
    high = list(range(3, bits))
    return [1, 2] + high[::-1], [2, 1] + high


def exchange(array, devices, stage):
    first, second = bit_orders(devices)
    if stage == 0:
        pairs = [(i, i ^ 1) for i in range(devices)]
    else:
        pairs = [(i, i ^ (1 << (second if i & 1 else first)[stage - 1])) for i in range(devices)]
    return lax.ppermute(array, "user", pairs)


def final_order(devices):
    orders = bit_orders(devices)
    bits = devices.bit_length() - 1
    result = []
    for place in range(devices):
        core = place >> (bits - 1)
        index = core
        for stage, bit in enumerate(orders[core]):
            index |= ((place >> (bits - 2 - stage)) & 1) << bit
        result.append(index)
    return result


def local(
    ratings,
    tile_index,
    tile_count,
    side_features,
    user_factors,
    item_factors,
    prior_weights,
    user_noise,
    item_noise,
):
    devices = lax.axis_size("user")
    own = lax.axis_index("user")
    stages = devices.bit_length() - 1
    strata = ratings.shape[1]
    rows_dev = user_factors.shape[0]
    feat, rank = prior_weights.shape
    feat_rows = feat // devices
    rate = rate_scale / (rows_dev * devices)
    noise_scale = math.sqrt(2.0 * step_size)
    core = own & 1
    first, second = bit_orders(devices)

    def my_bit(stage):
        if stage == 0:
            return core
        return jnp.where(core == 0, own >> first[stage - 1], own >> second[stage - 1]) & 1

    def halve(array, stage, rider=None):
        half = array.shape[0] // 2
        bit = my_bit(stage)
        send = lax.dynamic_slice_in_dim(array, (1 - bit) * half, half, 0)
        keep = lax.dynamic_slice_in_dim(array, bit * half, half, 0)
        if rider is None:
            return keep + exchange(send, devices, stage), None
        got = exchange(jnp.concatenate([send, rider], 0), devices, stage)
        return keep + got[:half], rider + got[half:]

    def whole(array, stage, rider):
        got = exchange(jnp.concatenate([array, rider], 0), devices, stage)
        return array + got[: array.shape[0]], rider + got[array.shape[0] :]

    def gather(array, stage):
        got = exchange(array, devices, stage)
        return jnp.where(
            my_bit(stage) == 0,
            jnp.concatenate([array, got], 0),
            jnp.concatenate([got, array], 0),
        )

    users = user_factors
    items = item_factors
    weights = prior_weights
    final_rows = None
    piece = feat // 8
    piece_start = core * (feat // 2) + my_bit(1) * (feat // 4) + my_bit(2) * piece
    for stratum in range(strata):
        last = stratum + 1 == strata
        mean, grad_w = prior_pass(
            side_features, weights, users, final_order(devices) if last else None
        )
        grad_u, grad_v, stats = tile_pass(
            tile_index[0, stratum], tile_count[0, stratum : stratum + 1], ratings[0, stratum], users, items
        )
        part, _ = halve(grad_w, 0)
        for stage in (1, 2):
            part, stats = halve(part, stage, stats)
        for stage in range(3, stages):
            part, stats = (halve if last else whole)(part, stage, stats)
        stats = stats + exchange(stats, devices, 0)
        precision = (1.0 + stats[0, 1] / 2.0) / (1.0 + stats[0, 0] / 2.0)
        new_items = (
            items
            + step_size * (precision * grad_v - item_prec * items)
            + noise_scale * item_noise[stratum].astype(jnp.float32)
        )
        new_users = (
            users
            + step_size * (precision * grad_u - prior_prec * (users - mean))
            + noise_scale * user_noise[stratum].astype(jnp.float32)
        )
        start = own * feat_rows if last else piece_start
        old = lax.dynamic_slice_in_dim(weights, start, part.shape[0], 0)
        part = old + rate * (prior_prec * part - weight_decay * old)
        if last:
            final_rows = part
            items = new_items
        else:
            items = lax.ppermute(
                new_items, "user", [(i, (i + 1) % devices) for i in range(devices)]
            )
            for stage in (2, 1, 0):
                part = gather(part, stage)
            weights = part
        users = new_users
    return (users, items, final_rows)


def solution(mesh):
    return jax.shard_map(
        local,
        mesh=mesh,
        in_specs=(
            P("user", None, None, None, None),
            P("user", None, None),
            P("user", None),
            P("user", None),
            P("user", None),
            P("user", None),
            P(),
            P(None, "user", None),
            P(None, "user", None),
        ),
        out_specs=(P("user", None), P("user", None), P("user", None)),
        check_vma=False,
    )
```

```python
import functools
import math

import jax
import jax.numpy as jnp
from jax import lax
from jax.experimental import pallas as pl
from jax.experimental.pallas import tpu as pltpu
from jax.sharding import PartitionSpec as P

step_size = 0.01
prior_prec = 8.0
item_prec = 1.0
weight_decay = 1.0
rate_scale = 0.04

CHUNKS = 2
NT = (((1,), (1,)), ((), ()))
TN = (((0,), (0,)), ((), ()))
VMEM = pl.BlockSpec(memory_space=pltpu.VMEM)
SMEM = pl.BlockSpec(memory_space=pltpu.SMEM)


def dot(a, b, dims=(((1,), (0,)), ((), ()))):
    return lax.dot_general(a, b, dims, preferred_element_type=jnp.float32)


def tile_kernel(codes, count, tiles, users, items, grad_u, grad_v, stats, pred, err_b):
    slots, tile, _ = tiles.shape
    grid = items.shape[0] // tile
    user_b = users[...].astype(jnp.bfloat16)
    item_b = items[...].astype(jnp.bfloat16)
    pred[...] = dot(user_b, item_b, NT)
    err_b[...] = jnp.zeros_like(err_b)
    live_slots = count[0]
    sse = jnp.zeros((tile, tile), jnp.float32)
    for slot in range(slots):
        code = codes[slot]
        rows = pl.ds(pl.multiple_of(code // grid * tile, tile), tile)
        cols = pl.ds(pl.multiple_of(code % grid * tile, tile), tile)
        live = (slot < live_slots).astype(jnp.float32)
        err = (tiles[slot].astype(jnp.float32) - pred[rows, cols]) * live
        sse = sse + err * err
        err_b[rows, cols] = err.astype(jnp.bfloat16)
    err_all = err_b[...]
    total = jnp.sum(sse)
    counted = live_slots.astype(jnp.float32) * float(tile * tile)
    row = lax.broadcasted_iota(jnp.int32, stats.shape, 0)
    stats[...] = jnp.where(row == 0, total, jnp.where(row == 1, counted, 0.0))
    grad_u[...] = dot(err_all, item_b)
    grad_v[...] = dot(err_all, user_b, TN)


def tile_pass(codes, count, tiles, users, items):
    rows, rank = users.shape
    f32 = jnp.float32
    return pl.pallas_call(
        tile_kernel,
        out_shape=(
            jax.ShapeDtypeStruct((rows, rank), f32),
            jax.ShapeDtypeStruct((rows, rank), f32),
            jax.ShapeDtypeStruct((8, rank // CHUNKS), f32),
        ),
        in_specs=[SMEM, SMEM, VMEM, VMEM, VMEM],
        out_specs=(VMEM, VMEM, VMEM),
        scratch_shapes=[
            pltpu.VMEM((rows, rows), f32),
            pltpu.VMEM((rows, rows), jnp.bfloat16),
        ],
        compiler_params=pltpu.CompilerParams(vmem_limit_bytes=16 << 20),
        cost_estimate=pl.CostEstimate(
            flops=6 * rows * rows * rank, bytes_accessed=4 * rows * rank * 4, transcendentals=0
        ),
        name="tile_pass",
    )(codes, count, tiles, users, items)


def prior_kernel(places, core, feats, weights, users, mean, send, keep, *full):
    half = send.shape[0]
    weights_b = weights[...].astype(jnp.bfloat16)
    mean_now = dot(feats[...], weights_b)
    mean[...] = mean_now
    offset = (users[...] - mean_now).astype(jnp.bfloat16)
    here = core[0]
    if places is None:
        for ref, which in ((send, 1 - here), (keep, here)):
            ref[...] = dot(feats[:, pl.ds(pl.multiple_of(which * half, half), half)], offset, TN)
    else:
        full[0][...] = dot(feats[...], offset, TN)
        block = half // len(places[0])
        for ref, which in ((send, 1 - here), (keep, here)):
            for place, (zero, one) in enumerate(zip(*places, strict=True)):
                source = jnp.where(which == 0, zero, one) * block
                if block % 8 == 0:
                    source = pl.multiple_of(source, block)
                ref[pl.ds(place * block, block), :] = full[0][pl.ds(source, block), :]


def prior_pass(core, feats, weights, users, places=None):
    rows, rank = users.shape
    feat = weights.shape[0]
    f32 = jnp.float32
    return pl.pallas_call(
        functools.partial(prior_kernel, places),
        out_shape=(
            jax.ShapeDtypeStruct((rows, rank), f32),
            jax.ShapeDtypeStruct((feat // 2, rank), f32),
            jax.ShapeDtypeStruct((feat // 2, rank), f32),
        ),
        in_specs=[SMEM, VMEM, VMEM, VMEM],
        out_specs=(VMEM, VMEM, VMEM),
        scratch_shapes=[] if places is None else [pltpu.VMEM((feat, rank), f32)],
        compiler_params=pltpu.CompilerParams(vmem_limit_bytes=16 << 20),
        cost_estimate=pl.CostEstimate(
            flops=4 * rows * feat * rank, bytes_accessed=8 * feat * rank, transcendentals=0
        ),
        name="prior_pass",
    )(core, feats, weights, users)


def bit_order(devices, core, chunk):
    bits = devices.bit_length() - 1
    near = [1, 2] if core == chunk % 2 else [2, 1]
    far = list(range(3, bits))
    return near + (far if chunk % 2 == 0 else far[::-1])


def exchange(array, devices, chunk, stage):
    if stage == 0:
        pairs = [(i, i ^ 1) for i in range(devices)]
    else:
        orders = [bit_order(devices, core, chunk) for core in (0, 1)]
        pairs = [(i, i ^ (1 << orders[i & 1][stage - 1])) for i in range(devices)]
    return lax.ppermute(array, "user", pairs)


def final_places(devices, chunk):
    bits = devices.bit_length() - 1
    result = []
    for core in (0, 1):
        order = bit_order(devices, core, chunk)
        result.append(
            [
                core
                | sum(((place >> (bits - 2 - n)) & 1) << bit for n, bit in enumerate(order))
                for place in range(devices // 2)
            ]
        )
    return result


def local(
    ratings,
    tile_index,
    tile_count,
    side_features,
    user_factors,
    item_factors,
    prior_weights,
    user_noise,
    item_noise,
):
    devices = lax.axis_size("user")
    own = lax.axis_index("user")
    stages = devices.bit_length() - 1
    strata = ratings.shape[1]
    rows_dev = user_factors.shape[0]
    feat, rank = prior_weights.shape
    feat_rows = feat // devices
    width = rank // CHUNKS
    rate = rate_scale / (rows_dev * devices)
    noise_scale = math.sqrt(2.0 * step_size)
    core = own & 1
    core_ref = core.reshape(1)

    def my_bit(chunk, stage):
        if stage == 0:
            return core
        zero, one = (bit_order(devices, c, chunk)[stage - 1] for c in (0, 1))
        return jnp.where(core == 0, own >> zero, own >> one) & 1

    def add(send, keep, chunk, stage, rider):
        if rider is None:
            return keep + exchange(send, devices, chunk, stage), None
        got = exchange(jnp.concatenate([send, rider], 0), devices, chunk, stage)
        return keep + got[: keep.shape[0]], rider + got[keep.shape[0] :]

    def halve(array, chunk, stage, rider):
        half = array.shape[0] // 2
        bit = my_bit(chunk, stage)
        send = lax.dynamic_slice_in_dim(array, (1 - bit) * half, half, 0)
        keep = lax.dynamic_slice_in_dim(array, bit * half, half, 0)
        return add(send, keep, chunk, stage, rider)

    def gather(array, chunk, stage):
        got = exchange(array, devices, chunk, stage)
        return jnp.where(
            my_bit(chunk, stage) == 0,
            jnp.concatenate([array, got], 0),
            jnp.concatenate([got, array], 0),
        )

    users = user_factors
    items = item_factors
    weights = [prior_weights[:, c * width : (c + 1) * width] for c in range(CHUNKS)]
    both = range(CHUNKS)
    for stratum in range(strata):
        last = stratum + 1 == strata
        means, parts = [], []
        for c in both:
            mean, send, keep = prior_pass(
                core_ref,
                side_features,
                weights[c],
                users[:, c * width : (c + 1) * width],
                final_places(devices, c) if last else None,
            )
            means.append(mean)
            parts.append(add(send, keep, c, 0, None)[0])
        grad_u, grad_v, stats = tile_pass(
            tile_index[0, stratum], tile_count[0, stratum : stratum + 1], ratings[0, stratum], users, items
        )
        stats = stats + exchange(stats, devices, 0, 0)
        for stage in range(1, stages):
            for c in both:
                rider = stats if c == CHUNKS - 1 else None
                if stage < 3 or last:
                    parts[c], rider = halve(parts[c], c, stage, rider)
                else:
                    parts[c], rider = add(parts[c], parts[c], c, stage, rider)
                if c == CHUNKS - 1:
                    stats = rider
        precision = (1.0 + stats[1:2, :] / 2.0) / (1.0 + stats[0:1, :] / 2.0)
        precision = jnp.concatenate([precision] * CHUNKS, 1)
        new_items = (
            items
            + step_size * (precision * grad_v - item_prec * items)
            + noise_scale * item_noise[stratum].astype(jnp.float32)
        )
        mean = jnp.concatenate(means, 1)
        new_users = (
            users
            + step_size * (precision * grad_u - prior_prec * (users - mean))
            + noise_scale * user_noise[stratum].astype(jnp.float32)
        )
        for c in both:
            if last:
                start = own * feat_rows
            else:
                start = core * (feat // 2) + my_bit(c, 1) * (feat // 4) + my_bit(c, 2) * (feat // 8)
            old = lax.dynamic_slice_in_dim(weights[c], start, parts[c].shape[0], 0)
            parts[c] = old + rate * (prior_prec * parts[c] - weight_decay * old)
        if last:
            items = new_items
        else:
            items = lax.ppermute(
                new_items, "user", [(i, (i + 1) % devices) for i in range(devices)]
            )
            for stage in (2, 1, 0):
                for c in both:
                    parts[c] = gather(parts[c], c, stage)
        weights = list(parts)
        users = new_users
    return (users, items, jnp.concatenate(weights, 1))


def solution(mesh):
    return jax.shard_map(
        local,
        mesh=mesh,
        in_specs=(
            P("user", None, None, None, None),
            P("user", None, None),
            P("user", None),
            P("user", None),
            P("user", None),
            P("user", None),
            P(),
            P(None, "user", None),
            P(None, "user", None),
        ),
        out_specs=(P("user", None), P("user", None), P("user", None)),
        check_vma=False,
    )
```

```python
import functools
import math

import jax
import jax.numpy as jnp
from jax import lax
from jax.experimental import pallas as pl
from jax.experimental.pallas import tpu as pltpu
from jax.sharding import PartitionSpec as P

step_size = 0.01
prior_prec = 8.0
item_prec = 1.0
weight_decay = 1.0
rate_scale = 0.04

CHUNKS = 2
CORES = 2
NT = (((1,), (1,)), ((), ()))
TN = (((0,), (0,)), ((), ()))
VMEM = pl.BlockSpec(memory_space=pltpu.VMEM)
SMEM = pl.BlockSpec(memory_space=pltpu.SMEM)


def dot(a, b, dims=(((1,), (0,)), ((), ()))):
    return lax.dot_general(a, b, dims, preferred_element_type=jnp.float32)


def tile_kernel(codes, count, tiles, users, items, grad_u, grad_v, stats, pred, err_b):
    slots, tile, _ = tiles.shape
    grid = items.shape[0] // tile
    user_b = users[...].astype(jnp.bfloat16)
    item_b = items[...].astype(jnp.bfloat16)
    pred[...] = dot(user_b, item_b, NT)
    err_b[...] = jnp.zeros_like(err_b)
    live_slots = count[0]
    sse = jnp.zeros((tile, tile), jnp.float32)
    for slot in range(slots):
        code = codes[slot]
        rows = pl.ds(pl.multiple_of(code // grid * tile, tile), tile)
        cols = pl.ds(pl.multiple_of(code % grid * tile, tile), tile)
        live = (slot < live_slots).astype(jnp.float32)
        err = (tiles[slot].astype(jnp.float32) - pred[rows, cols]) * live
        sse = sse + err * err
        err_b[rows, cols] = err.astype(jnp.bfloat16)
    err_all = err_b[...]
    total = jnp.sum(sse)
    counted = live_slots.astype(jnp.float32) * float(tile * tile)
    row = lax.broadcasted_iota(jnp.int32, stats.shape, 0)
    stats[...] = jnp.where(row == 0, total, jnp.where(row == 1, counted, 0.0))
    grad_u[...] = dot(err_all, item_b)
    grad_v[...] = dot(err_all, user_b, TN)


def tile_pass(codes, count, tiles, users, items):
    rows, rank = users.shape
    f32 = jnp.float32
    return pl.pallas_call(
        tile_kernel,
        out_shape=(
            jax.ShapeDtypeStruct((rows, rank), f32),
            jax.ShapeDtypeStruct((rows, rank), f32),
            jax.ShapeDtypeStruct((8, rank // CORES), f32),
        ),
        in_specs=[SMEM, SMEM, VMEM, VMEM, VMEM],
        out_specs=(VMEM, VMEM, VMEM),
        scratch_shapes=[
            pltpu.VMEM((rows, rows), f32),
            pltpu.VMEM((rows, rows), jnp.bfloat16),
        ],
        compiler_params=pltpu.CompilerParams(vmem_limit_bytes=16 << 20),
        cost_estimate=pl.CostEstimate(
            flops=6 * rows * rows * rank, bytes_accessed=4 * rows * rank * 4, transcendentals=0
        ),
        name="tile_pass",
    )(codes, count, tiles, users, items)


def half_of(ref, core, count=CORES):
    width = ref.shape[1] // count
    return ref[:, pl.ds(pl.multiple_of(core * width, width), width)]


def first_kernel(core, feats, weights, users, mean, *outs):
    mean_now = dot(feats[...], weights[...].astype(jnp.bfloat16))
    mean[...] = mean_now
    here = core[0]
    width = outs[0].shape[1]
    rows = outs[0].shape[0]
    for group, which in ((outs[:CHUNKS], 1 - here), (outs[CHUNKS:], here)):
        offset = (half_of(users, which) - half_of(mean, which)).astype(jnp.bfloat16)
        for chunk, ref in enumerate(group):
            ref[...] = dot(feats[:, chunk * rows : (chunk + 1) * rows], offset, TN)


def first_pass(core, feats, weights, users):
    rows, rank = users.shape
    feat = weights.shape[0]
    f32 = jnp.float32
    return pl.pallas_call(
        first_kernel,
        out_shape=(jax.ShapeDtypeStruct((rows, rank), f32),)
        + (jax.ShapeDtypeStruct((feat // CHUNKS, rank // CORES), f32),) * (2 * CHUNKS),
        in_specs=[SMEM, VMEM, VMEM, VMEM],
        out_specs=(VMEM,) * (1 + 2 * CHUNKS),
        compiler_params=pltpu.CompilerParams(vmem_limit_bytes=8 << 20),
        cost_estimate=pl.CostEstimate(
            flops=4 * rows * feat * rank, bytes_accessed=8 * feat * rank, transcendentals=0
        ),
        name="first_pass",
    )(core, feats, weights, users)


def widen_kernel(narrow, wide):
    wide[...] = narrow[...].astype(jnp.float32)


def join_kernel(own, other, both):
    rows = own.shape[0]
    both[:rows, :] = own[...]
    both[rows:, :] = other[...].astype(jnp.bfloat16)


def part_kernel(feats, weights, part):
    part[...] = dot(feats[:, : weights.shape[0]], weights[...].astype(jnp.bfloat16))


def part_pass(feats, weights):
    rows = feats.shape[0]
    depth, width = weights.shape
    return pl.pallas_call(
        part_kernel,
        out_shape=jax.ShapeDtypeStruct((rows, width), jnp.float32),
        in_specs=[VMEM, VMEM],
        out_specs=VMEM,
        compiler_params=pltpu.CompilerParams(vmem_limit_bytes=8 << 20),
        cost_estimate=pl.CostEstimate(
            flops=2 * rows * depth * width, bytes_accessed=2 * rows * depth, transcendentals=0
        ),
        name="part_pass",
    )(feats, weights)


def prior_kernel(places, core, feats, weights, part, users, others, own_mean, other_mean, offset, *outs):
    depth = weights.shape[0]
    rows = users.shape[0]
    mean = part[...] + dot(feats[:, depth:], weights[...].astype(jnp.bfloat16))
    own_mean[...] = mean[:rows]
    other_mean[...] = mean[rows:]
    offset[:rows, :] = (half_of(users, core[0]) - mean[:rows]).astype(jnp.bfloat16)
    offset[rows:, :] = (others[...] - mean[rows:]).astype(jnp.bfloat16)
    if places is None:
        outs[0][...] = dot(feats[:, :depth], offset[...], TN)
        return
    full = outs[-1]
    full[...] = dot(feats[...], offset[...], TN)
    for ref, (zero, one) in zip(outs[:-1], places, strict=True):
        block = depth // len(zero)
        for place, (first, second) in enumerate(zip(zero, one, strict=True)):
            source = jnp.where(core[0] == 0, first, second) * block
            if block % 8 == 0:
                source = pl.multiple_of(source, block)
            ref[place * block : (place + 1) * block, :] = full[pl.ds(source, block), :]


def prior_pass(core, feats, weights, part, users, others, places=None):
    rows = users.shape[0]
    depth, width = weights.shape
    f32 = jnp.float32
    chunks = 1 if places is None else CHUNKS
    return pl.pallas_call(
        functools.partial(prior_kernel, places),
        out_shape=(
            jax.ShapeDtypeStruct((rows, width), f32),
            jax.ShapeDtypeStruct((rows, width), f32),
            jax.ShapeDtypeStruct((CORES * rows, width), jnp.bfloat16),
        )
        + (jax.ShapeDtypeStruct((depth, width), f32),) * chunks,
        in_specs=[SMEM] + [VMEM] * 5,
        out_specs=(VMEM,) * (3 + chunks),
        scratch_shapes=[] if places is None else [pltpu.VMEM((CHUNKS * depth, width), f32)],
        compiler_params=pltpu.CompilerParams(vmem_limit_bytes=8 << 20),
        cost_estimate=pl.CostEstimate(
            flops=8 * rows * depth * width, bytes_accessed=8 * rows * depth, transcendentals=0
        ),
        name="prior_pass",
    )(core, feats, weights, part, users, others)


def rest_kernel(feats, offset, grad):
    grad[...] = dot(feats[:, grad.shape[0] :], offset[...], TN)


def rest_pass(feats, offset):
    rows, width = offset.shape
    depth = feats.shape[1] // CHUNKS
    return pl.pallas_call(
        rest_kernel,
        out_shape=jax.ShapeDtypeStruct((depth, width), jnp.float32),
        in_specs=[VMEM, VMEM],
        out_specs=VMEM,
        compiler_params=pltpu.CompilerParams(vmem_limit_bytes=8 << 20),
        cost_estimate=pl.CostEstimate(
            flops=2 * rows * depth * width, bytes_accessed=2 * rows * depth, transcendentals=0
        ),
        name="rest_pass",
    )(feats, offset)


def bit_order(devices, core, chunk):
    bits = devices.bit_length() - 1
    near = [1, 2] if core == chunk % 2 else [2, 1]
    far = list(range(3, bits))
    return near + (far if chunk % 2 == 0 else far[::-1])


def swap(array, devices):
    return lax.ppermute(array, "user", [(i, i ^ 1) for i in range(devices)])


def roll(array, devices):
    return lax.ppermute(array, "user", [(i, (i + 1) % devices) for i in range(devices)])


def exchange(array, devices, chunk, stage):
    orders = [bit_order(devices, core, chunk) for core in range(CORES)]
    pairs = [(i, i ^ (1 << orders[i & 1][stage])) for i in range(devices)]
    return lax.ppermute(array, "user", pairs)


def final_places(devices, chunk):
    bits = devices.bit_length() - 1
    result = []
    for core in range(CORES):
        order = bit_order(devices, core, chunk)
        result.append(
            [
                chunk
                | sum(((place >> (bits - 2 - n)) & 1) << bit for n, bit in enumerate(order))
                for place in range(devices // 2)
            ]
        )
    return result


def local(
    ratings,
    tile_index,
    tile_count,
    side_features,
    user_factors,
    item_factors,
    prior_weights,
    user_noise,
    item_noise,
):
    devices = lax.axis_size("user")
    own = lax.axis_index("user")
    stages = devices.bit_length() - 2
    strata = ratings.shape[1]
    rows_dev = user_factors.shape[0]
    feat, rank = prior_weights.shape
    feat_rows = feat // devices
    depth = feat // CHUNKS
    width = rank // CORES
    rate = rate_scale / (rows_dev * devices)
    noise_scale = math.sqrt(2.0 * step_size)
    core = own & 1
    core_ref = core.reshape(1)
    f32 = jnp.float32
    both = range(CHUNKS)

    def my_bit(chunk, stage):
        zero, one = (bit_order(devices, c, chunk)[stage] for c in range(CORES))
        return jnp.where(core == 0, own >> zero, own >> one) & 1

    def columns(array, which):
        return jnp.where(which == 0, array[:, :width], array[:, width:])

    def across(mine, other):
        return jnp.where(
            core == 0, jnp.concatenate([mine, other], 1), jnp.concatenate([other, mine], 1)
        )

    def add(send, keep, chunk, stage, rider):
        if rider is None:
            return keep + exchange(send, devices, chunk, stage), None
        got = exchange(jnp.concatenate([send, rider], 0), devices, chunk, stage)
        return keep + got[: keep.shape[0]], rider + got[keep.shape[0] :]

    def halve(array, chunk, stage, rider):
        half = array.shape[0] // 2
        bit = my_bit(chunk, stage)
        send = lax.dynamic_slice_in_dim(array, (1 - bit) * half, half, 0)
        keep = lax.dynamic_slice_in_dim(array, bit * half, half, 0)
        return add(send, keep, chunk, stage, rider)

    def gather(array, chunk, stage):
        got = exchange(array, devices, chunk, stage)
        return jnp.where(
            my_bit(chunk, stage) == 0,
            jnp.concatenate([array, got], 0),
            jnp.concatenate([got, array], 0),
        )

    def tiles_of(stratum, users, items):
        grad_u, grad_v, stats = tile_pass(
            tile_index[0, stratum], tile_count[0, stratum : stratum + 1], ratings[0, stratum], users, items
        )
        return grad_u, grad_v, stats + swap(stats, devices)

    users = user_factors
    items = item_factors
    mean, *outs = first_pass(core_ref, side_features, prior_weights, users)
    parts = [outs[CHUNKS + c] + swap(outs[c], devices) for c in both]
    grad_u, grad_v, stats = tiles_of(0, users, items)
    mine = columns(prior_weights, core)
    weights = [mine[c * depth : (c + 1) * depth] for c in both]
    wide = pl.pallas_call(
        widen_kernel,
        out_shape=jax.ShapeDtypeStruct(side_features.shape, f32),
        in_specs=[VMEM],
        out_specs=VMEM,
        compiler_params=pltpu.CompilerParams(vmem_limit_bytes=8 << 20),
        name="widen",
    )(side_features)
    feats = pl.pallas_call(
        join_kernel,
        out_shape=jax.ShapeDtypeStruct((CORES * rows_dev, feat), jnp.bfloat16),
        in_specs=[VMEM, VMEM],
        out_specs=VMEM,
        compiler_params=pltpu.CompilerParams(vmem_limit_bytes=8 << 20),
        name="join",
    )(side_features, swap(wide, devices))
    others = None
    for stratum in range(strata):
        last = stratum + 1 == strata
        if stratum:
            part = part_pass(feats, weights[0])
            own_mean, other_mean, offset, *parts = prior_pass(
                core_ref,
                feats,
                weights[1],
                part,
                users,
                others,
                [final_places(devices, c) for c in both] if last else None,
            )
            if not last:
                parts.append(rest_pass(feats, offset))
            mean = across(own_mean, swap(other_mean, devices))
        base = (
            items
            - (step_size * item_prec) * items
            + noise_scale * item_noise[stratum].astype(f32)
        )
        push = step_size * grad_v
        if not last:
            base = roll(base, devices)
            push = roll(push, devices)
        for stage in range(stages):
            for c in both:
                rider = stats if c == CHUNKS - 1 else None
                if stage < 2 or last:
                    parts[c], rider = halve(parts[c], c, stage, rider)
                else:
                    parts[c], rider = add(parts[c], parts[c], c, stage, rider)
                if c == CHUNKS - 1:
                    stats = rider
        precision = (1.0 + stats[1:2, :] / 2.0) / (1.0 + stats[0:1, :] / 2.0)
        precision = jnp.concatenate([precision] * CORES, 1)
        items = base + precision * push
        users = (
            users
            + step_size * (precision * grad_u - prior_prec * (users - mean))
            + noise_scale * user_noise[stratum].astype(f32)
        )
        if not last:
            others = swap(columns(users, 1 - core), devices)
            grad_u, grad_v, stats = tiles_of(stratum + 1, users, items)
        for c in both:
            if last:
                old = jnp.concatenate(weights, 0)
                start = ((own & -2) + c) * feat_rows
            else:
                old = weights[c]
                start = my_bit(c, 0) * (depth // 2) + my_bit(c, 1) * (depth // 4)
            old = lax.dynamic_slice_in_dim(old, start, parts[c].shape[0], 0)
            parts[c] = old + rate * (prior_prec * parts[c] - weight_decay * old)
        if not last:
            for stage in (1, 0):
                for c in both:
                    parts[c] = gather(parts[c], c, stage)
        weights = list(parts)
    zero, one = weights
    rows = across(jnp.where(core == 0, zero, one), swap(jnp.where(core == 0, one, zero), devices))
    return (users, items, rows)


def solution(mesh):
    return jax.shard_map(
        local,
        mesh=mesh,
        in_specs=(
            P("user", None, None, None, None),
            P("user", None, None),
            P("user", None),
            P("user", None),
            P("user", None),
            P("user", None),
            P(),
            P(None, "user", None),
            P(None, "user", None),
        ),
        out_specs=(P("user", None), P("user", None), P("user", None)),
        check_vma=False,
    )
```

```python
import functools
import math

import jax
import jax.numpy as jnp
from jax import lax
from jax.experimental import pallas as pl
from jax.experimental.pallas import tpu as pltpu
from jax.sharding import PartitionSpec as P

step_size = 0.01
prior_prec = 8.0
item_prec = 1.0
weight_decay = 1.0
rate_scale = 0.04

CORES = 2
NN = (((1,), (0,)), ((), ()))
NT = (((1,), (1,)), ((), ()))
TN = (((0,), (0,)), ((), ()))
VMEM = pl.BlockSpec(memory_space=pltpu.VMEM)
SMEM = pl.BlockSpec(memory_space=pltpu.SMEM)
HBM = pl.BlockSpec(memory_space=pltpu.HBM)
ANY = pl.BlockSpec(memory_space=pl.ANY)
PARAMS = pltpu.CompilerParams(vmem_limit_bytes=8 << 20)
f32 = jnp.float32
bf16 = jnp.bfloat16


def dot(a, b, dims=NN):
    return lax.dot_general(a, b, dims, preferred_element_type=f32)


def shape(*dims, dtype=f32):
    return jax.ShapeDtypeStruct(dims, dtype)


def cost(flops, size):
    return pl.CostEstimate(flops=flops, bytes_accessed=size, transcendentals=0)


def half_of(ref, core):
    width = ref.shape[1] // CORES
    return ref[:, pl.ds(pl.multiple_of(core * width, width), width)]


def precision_of(stats):
    return (1.0 + stats[1:2, :] / 2.0) / (1.0 + stats[0:1, :] / 2.0)


def tile_kernel(stratum, noise_scale, core, codes, count, ratings, user_noise, item_noise, *refs):
    if stratum == 0:
        users_in, items_in = refs[:2]
        base_u, grad_u, pushed, stats = refs[2:6]
        refs = refs[6:]
    else:
        old_base, old_grad, own_mean, other_mean, old_stats, pulled = refs[:6]
        base_u, grad_u, pushed, stats, own_cols, other_cols = refs[6:12]
        refs = refs[12:]
    tiles, noise_u, noise_v, users, items, pred, err_b, sems = refs
    rows, rank = users.shape
    width = rank // CORES
    tile = tiles.shape[-1]
    grid = rows // tile
    copies = [
        pltpu.make_async_copy(source, target, sems.at[n])
        for n, (source, target) in enumerate(
            [
                (ratings.at[0, stratum], tiles),
                (user_noise.at[stratum], noise_u),
                (item_noise.at[stratum], noise_v),
            ]
            + ([(users_in, users), (items_in, items)] if stratum == 0 else [])
        )
    ]
    for copy in copies[::-1]:
        copy.start()
    if stratum == 0:
        copies[4].wait()
        copies[3].wait()
    else:
        precision = precision_of(old_stats[...])
        precision = jnp.concatenate([precision] * CORES, 1)
        items[...] = pulled[:rows, :] + precision * pulled[rows:, :]
        new = old_base[...] + precision * old_grad[...]
        here = core[0] == 0
        pull = step_size * prior_prec
        left = jnp.where(here, own_mean[...], other_mean[...])
        right = jnp.where(here, other_mean[...], own_mean[...])
        users[:, :width] = new[:, :width] + pull * left
        users[:, width:] = new[:, width:] + pull * right
        own_cols[...] = half_of(users, core[0])
        other_cols[...] = half_of(users, 1 - core[0])
    user_b = users[...].astype(bf16)
    item_b = items[...].astype(bf16)
    pred[...] = dot(user_b, item_b, NT)
    err_b[...] = jnp.zeros_like(err_b)
    live_slots = count[0, stratum]
    sse = jnp.zeros((tile, tile), f32)
    copies[0].wait()
    for slot in range(tiles.shape[0]):
        code = codes[0, stratum, slot]
        at_rows = pl.ds(pl.multiple_of(code // grid * tile, tile), tile)
        at_cols = pl.ds(pl.multiple_of(code % grid * tile, tile), tile)
        live = (slot < live_slots).astype(f32)
        err = (tiles[slot].astype(f32) - pred[at_rows, at_cols]) * live
        sse = sse + err * err
        err_b[at_rows, at_cols] = err.astype(bf16)
    err_all = err_b[...]
    total = jnp.sum(sse)
    counted = live_slots.astype(f32) * float(tile * tile)
    row = lax.broadcasted_iota(jnp.int32, stats.shape, 0)
    stats[...] = jnp.where(row == 0, total, jnp.where(row == 1, counted, 0.0))
    grad_u[...] = step_size * dot(err_all, item_b)
    pushed[rows:, :] = step_size * dot(err_all, user_b, TN)
    copies[2].wait()
    pushed[:rows, :] = (1.0 - step_size * item_prec) * items[...] + noise_scale * noise_v[
        ...
    ].astype(f32)
    copies[1].wait()
    base_u[...] = (1.0 - step_size * prior_prec) * users[...] + noise_scale * noise_u[...].astype(
        f32
    )


def tile_pass(stratum, core, codes, count, ratings, user_noise, item_noise, *state):
    slots, tile = ratings.shape[2:4]
    rows, rank = user_noise.shape[1:]
    noise_scale = math.sqrt(2.0 * step_size)
    width = rank // CORES
    outs = [shape(rows, rank), shape(rows, rank), shape(2 * rows, rank), shape(8, width)]
    if stratum:
        outs += [shape(rows, width)] * 2
    return pl.pallas_call(
        functools.partial(tile_kernel, stratum, noise_scale),
        out_shape=tuple(outs),
        in_specs=[SMEM] * 3 + [HBM] * 3 + [VMEM if stratum else HBM] * len(state),
        out_specs=(VMEM,) * len(outs),
        scratch_shapes=[
            pltpu.VMEM((slots, tile, tile), bf16),
            pltpu.VMEM((rows, rank), bf16),
            pltpu.VMEM((rows, rank), bf16),
            pltpu.VMEM((rows, rank), f32),
            pltpu.VMEM((rows, rank), f32),
            pltpu.VMEM((rows, rows), f32),
            pltpu.VMEM((rows, rows), bf16),
            pltpu.SemaphoreType.DMA((5,)),
        ],
        compiler_params=PARAMS,
        cost_estimate=cost(6 * rows * rows * rank, 16 * rows * rank),
        name="tile_pass",
    )(core, codes, count, ratings, user_noise, item_noise, *state)


def first_kernel(core, feats_in, weights_in, users_in, mean, send, keep, mine, wide, feats, weights, users, sems):
    copies = [
        pltpu.make_async_copy(source, target, sems.at[n])
        for n, (source, target) in enumerate(
            [(weights_in, weights), (feats_in, feats), (users_in, users)]
        )
    ]
    for copy in copies:
        copy.start()
    here = core[0]
    copies[0].wait()
    weights_b = weights[...].astype(bf16)
    copies[1].wait()
    mean[...] = dot(feats[...], weights_b)
    copies[2].wait()
    for ref, which in ((send, 1 - here), (keep, here)):
        offset = (half_of(users, which) - half_of(mean, which)).astype(bf16)
        ref[...] = dot(feats[...], offset, TN)
    mine[...] = half_of(weights, here)
    wide[...] = feats[...].astype(f32)


def first_pass(core, feats, weights, users):
    rows, rank = users.shape
    feat = weights.shape[0]
    width = rank // CORES
    return pl.pallas_call(
        first_kernel,
        out_shape=(shape(rows, rank),) + (shape(feat, width),) * 3 + (shape(rows, feat),),
        in_specs=[SMEM] + [HBM] * 3,
        out_specs=(VMEM,) * 5,
        scratch_shapes=[
            pltpu.VMEM(feats.shape, bf16),
            pltpu.VMEM(weights.shape, f32),
            pltpu.VMEM(users.shape, f32),
            pltpu.SemaphoreType.DMA((3,)),
        ],
        compiler_params=PARAMS,
        cost_estimate=cost(4 * rows * feat * rank, 8 * feat * rank),
        name="first_pass",
    )(core, feats, weights, users)


def join_kernel(own, other, both, sem):
    rows = other.shape[0]
    copy = pltpu.make_async_copy(own, both.at[:rows], sem.at[0])
    copy.start()
    both[rows:, :] = other[...].astype(bf16)
    copy.wait()


def join_pass(own, other):
    rows, feat = own.shape
    return pl.pallas_call(
        join_kernel,
        out_shape=shape(CORES * rows, feat, dtype=bf16),
        in_specs=[HBM, VMEM],
        out_specs=VMEM,
        scratch_shapes=[pltpu.SemaphoreType.DMA((1,))],
        compiler_params=PARAMS,
        name="join_pass",
    )(own, other)


def prior_kernel(places, place, feats, weights, own_cols, other_cols, stats, more_stats, own_mean, other_mean, send, keep, offset, *full):
    rows = own_cols.shape[0]
    half = keep.shape[0]
    mean = dot(feats[...], weights[...].astype(bf16))
    own_mean[...] = mean[:rows]
    other_mean[...] = mean[rows:]
    offset[:rows, :] = (own_cols[...] - mean[:rows]).astype(bf16)
    offset[rows:, :] = (other_cols[...] - mean[rows:]).astype(bf16)
    send[half:, :] = stats[...] + more_stats[...]
    core, bit = place[0], place[1]
    if places is None:
        for ref, which in ((send, 1 - bit), (keep, bit)):
            at = pl.ds(pl.multiple_of(which * half, half), half)
            ref[:half, :] = dot(feats[:, at], offset[...], TN)
        return
    full = full[0]
    full[...] = dot(feats[...], offset[...], TN)
    blocks = len(places[0])
    block = 2 * half // blocks
    for ref, which in ((send, 1 - bit), (keep, bit)):
        for n in range(blocks // 2):
            source = jnp.int32(0)
            for c, order in enumerate(places):
                for b in range(2):
                    source = jnp.where((core == c) & (which == b), order[b * blocks // 2 + n], source)
            source = source * block
            if block % 8 == 0:
                source = pl.multiple_of(source, block)
            ref[n * block : (n + 1) * block, :] = full[pl.ds(source, block), :]


def prior_pass(place, feats, weights, own_cols, other_cols, stats, more_stats, places=None):
    rows, width = own_cols.shape
    feat = weights.shape[0]
    return pl.pallas_call(
        functools.partial(prior_kernel, places),
        out_shape=(
            shape(rows, width),
            shape(rows, width),
            shape(feat // 2 + stats.shape[0], width),
            shape(feat // 2, width),
        ),
        in_specs=[SMEM] + [VMEM] * 6,
        out_specs=(VMEM,) * 4,
        scratch_shapes=[pltpu.VMEM((CORES * rows, width), bf16)]
        + ([] if places is None else [pltpu.VMEM((feat, width), f32)]),
        compiler_params=PARAMS,
        cost_estimate=cost(8 * rows * feat * width, 8 * rows * feat),
        name="prior_pass",
    )(place, feats, weights, own_cols, other_cols, stats, more_stats)


def update_kernel(rate, start, part, got, stats, weights, later, new, new_stats):
    rows = part.shape[0]
    old = weights[pl.ds(pl.multiple_of(start[0], rows), rows), :]
    total = part[...] + got[:rows, :]
    new[...] = old + rate * (prior_prec * total - weight_decay * old)
    new_stats[...] = stats[...] + got[rows:, :]


def update_pass(rate, start, part, got, stats, weights, later):
    return pl.pallas_call(
        functools.partial(update_kernel, rate),
        out_shape=(shape(*part.shape), shape(*stats.shape)),
        in_specs=[SMEM] + [VMEM] * 4 + [ANY],
        out_specs=(VMEM,) * 2,
        compiler_params=PARAMS,
        cost_estimate=cost(4 * part.size, 16 * part.size),
        name="update_pass",
    )(start, part, got, stats, weights, later)


def bit_order(devices, core):
    bits = devices.bit_length() - 1
    far = list(range(3, bits))
    return [1, 2] + far if core == 0 else [2, 1] + far[::-1]


def swap(array, devices):
    return lax.ppermute(array, "user", [(i, i ^ 1) for i in range(devices)])


def roll(array, devices):
    return lax.ppermute(array, "user", [(i, (i + 1) % devices) for i in range(devices)])


def exchange(array, devices, stage):
    orders = [bit_order(devices, core) for core in range(CORES)]
    pairs = [(i, i ^ (1 << orders[i & 1][stage])) for i in range(devices)]
    return lax.ppermute(array, "user", pairs)


def final_places(devices):
    bits = devices.bit_length() - 1
    return [
        [
            sum(
                ((place >> (bits - 2 - n)) & 1) << (bit - 1)
                for n, bit in enumerate(bit_order(devices, core))
            )
            for place in range(devices // 2)
        ]
        for core in range(CORES)
    ]


def local(
    ratings,
    tile_index,
    tile_count,
    side_features,
    user_factors,
    item_factors,
    prior_weights,
    user_noise,
    item_noise,
):
    devices = lax.axis_size("user")
    own = lax.axis_index("user")
    stages = devices.bit_length() - 2
    strata = ratings.shape[1]
    rows_dev = user_factors.shape[0]
    feat = prior_weights.shape[0]
    feat_rows = feat // devices
    rate = rate_scale / (rows_dev * devices)
    core = own & 1

    def my_bit(stage):
        zero, one = (bit_order(devices, c)[stage] for c in range(CORES))
        return jnp.where(core == 0, own >> zero, own >> one) & 1

    def across(mine, other):
        return jnp.where(
            core == 0, jnp.concatenate([mine, other], 1), jnp.concatenate([other, mine], 1)
        )

    def add(send, keep, stage, rider):
        got = exchange(jnp.concatenate([send, rider], 0), devices, stage)
        return keep + got[: keep.shape[0]], rider + got[keep.shape[0] :]

    def halve(array, stage, rider):
        half = array.shape[0] // 2
        bit = my_bit(stage)
        send = lax.dynamic_slice_in_dim(array, (1 - bit) * half, half, 0)
        keep = lax.dynamic_slice_in_dim(array, bit * half, half, 0)
        return add(send, keep, stage, rider)

    def gather(array, stage):
        got = exchange(array, devices, stage)
        return jnp.where(
            my_bit(stage) == 0,
            jnp.concatenate([array, got], 0),
            jnp.concatenate([got, array], 0),
        )

    core_ref = core.reshape(1)
    place = jnp.stack([core, my_bit(0)])
    tables = (core_ref, tile_index, tile_count, ratings, user_noise, item_noise)
    mean, send, part, weights, wide = first_pass(
        core_ref, side_features, prior_weights, user_factors
    )
    width = weights.shape[1]
    part = part + swap(send, devices)
    base, grad, pushed, stats = tile_pass(0, *tables, user_factors, item_factors)
    stats = stats + swap(stats, devices)
    part, stats = halve(part, 0, stats)
    feats = join_pass(side_features, swap(wide, devices))
    own_mean = jnp.where(core == 0, mean[:, :width], mean[:, width:])
    other_mean = jnp.where(core == 0, mean[:, width:], mean[:, :width])
    for stratum in range(strata):
        last = stratum + 1 == strata
        pulled = pushed if last else roll(pushed, devices)
        for stage in range(1, stages if last else stages - 1):
            if stage < 2 or last:
                part, stats = halve(part, stage, stats)
            else:
                part, stats = add(part, part, stage, stats)
        if last:
            start = (own >> 1) * (CORES * feat_rows)
            old = lax.dynamic_slice_in_dim(weights, start, part.shape[0], 0)
            part = old + rate * (prior_prec * part - weight_decay * old)
            break
        start = my_bit(0) * (feat // 2) + my_bit(1) * (feat // 4)
        got = exchange(jnp.concatenate([part, stats], 0), devices, stages - 1)
        part, stats = update_pass(rate, start.reshape(1), part, got, stats, weights, pulled)
        base, grad, pushed, new_stats, own_cols, other_cols = tile_pass(
            stratum + 1, *tables, base, grad, own_mean, other_mean, stats, pulled
        )
        more_stats = swap(new_stats, devices)
        other_cols = swap(other_cols, devices)
        for stage in (1, 0):
            part = gather(part, stage)
        weights = part
        own_mean, other_mean, send, keep = prior_pass(
            place,
            feats,
            weights,
            own_cols,
            other_cols,
            new_stats,
            more_stats,
            final_places(devices) if stratum + 2 == strata else None,
        )
        other_mean = swap(other_mean, devices)
        got = exchange(send, devices, 0)
        part = keep + got[: keep.shape[0]]
        stats = send[keep.shape[0] :] + got[keep.shape[0] :]
    precision = precision_of(stats)
    precision = jnp.concatenate([precision] * CORES, 1)
    items = pulled[:rows_dev] + precision * pulled[rows_dev:]
    users = base + precision * grad + (step_size * prior_prec) * across(own_mean, other_mean)
    first, second = part[:feat_rows], part[feat_rows:]
    rows = across(
        jnp.where(core == 0, first, second), swap(jnp.where(core == 0, second, first), devices)
    )
    return (users, items, rows)


def solution(mesh):
    return jax.shard_map(
        local,
        mesh=mesh,
        in_specs=(
            P("user", None, None, None, None),
            P("user", None, None),
            P("user", None),
            P("user", None),
            P("user", None),
            P("user", None),
            P(),
            P(None, "user", None),
            P(None, "user", None),
        ),
        out_specs=(P("user", None), P("user", None), P("user", None)),
        check_vma=False,
    )
```

```python
import functools
import math

import jax
import jax.numpy as jnp
from jax import lax
from jax.experimental import pallas as pl
from jax.experimental.pallas import tpu as pltpu
from jax.sharding import PartitionSpec as P

step_size = 0.01
prior_prec = 8.0
item_prec = 1.0
weight_decay = 1.0
rate_scale = 0.04

CORES = 2
RIDERS = 8
NN = (((1,), (0,)), ((), ()))
NT = (((1,), (1,)), ((), ()))
TN = (((0,), (0,)), ((), ()))
VMEM = pl.BlockSpec(memory_space=pltpu.VMEM)
SMEM = pl.BlockSpec(memory_space=pltpu.SMEM)
HBM = pl.BlockSpec(memory_space=pltpu.HBM)
ANY = pl.BlockSpec(memory_space=pl.ANY)
PARAMS = pltpu.CompilerParams(vmem_limit_bytes=8 << 20)
f32 = jnp.float32
bf16 = jnp.bfloat16


def dot(a, b, dims=NN):
    return lax.dot_general(a, b, dims, preferred_element_type=f32)


def shape(*dims, dtype=f32):
    return jax.ShapeDtypeStruct(dims, dtype)


def cost(flops, size):
    return pl.CostEstimate(flops=flops, bytes_accessed=size, transcendentals=0)


def half_of(ref, core):
    width = ref.shape[1] // CORES
    return ref[:, pl.ds(pl.multiple_of(core * width, width), width)]


def precision_of(stats):
    return (1.0 + stats[1:2, :] / 2.0) / (1.0 + stats[0:1, :] / 2.0)


def tile_kernel(stratum, noise_scale, place, codes, count, ratings, user_noise, item_noise, *refs):
    if stratum == 0:
        users_in, items_in = refs[:2]
        base_u, grad_u, base_v, grad_v, stats = refs[2:7]
        refs = refs[7:]
    else:
        old_base, old_grad, own_mean, other_mean, old_stats, old_base_v, old_grad_v = refs[:7]
        base_u, grad_u, base_v, grad_v, stats, own_cols, other_cols = refs[7:14]
        refs = refs[14:]
    tiles, noise_u, noise_v, users, items, pred, err_b, sems = refs
    rows, rank = users.shape
    width = rank // CORES
    tile = tiles.shape[-1]
    grid = rows // tile
    copies = [
        pltpu.make_async_copy(source, target, sems.at[n])
        for n, (source, target) in enumerate(
            [
                (ratings.at[0, stratum], tiles),
                (user_noise.at[stratum], noise_u),
                (item_noise.at[stratum], noise_v),
            ]
            + ([(users_in, users), (items_in, items)] if stratum == 0 else [])
        )
    ]
    for copy in copies[::-1]:
        copy.start()
    if stratum == 0:
        copies[4].wait()
        copies[3].wait()
    else:
        precision = precision_of(old_stats[...])
        precision = jnp.concatenate([precision] * CORES, 1)
        items[...] = old_base_v[...] + precision * old_grad_v[...]
        new = old_base[...] + precision * old_grad[...]
        here = place[0] == 0
        pull = step_size * prior_prec
        left = jnp.where(here, own_mean[...], other_mean[...])
        right = jnp.where(here, other_mean[...], own_mean[...])
        users[:, :width] = new[:, :width] + pull * left
        users[:, width:] = new[:, width:] + pull * right
        own_cols[...] = half_of(users, place[0])
        other_cols[...] = half_of(users, 1 - place[0])
    user_b = users[...].astype(bf16)
    item_b = items[...].astype(bf16)
    pred[...] = dot(user_b, item_b, NT)
    err_b[...] = jnp.zeros_like(err_b)
    live_slots = count[0, stratum]
    sse = jnp.zeros((tile, tile), f32)
    copies[0].wait()
    for slot in range(tiles.shape[0]):
        code = codes[0, stratum, slot]
        at_rows = pl.ds(pl.multiple_of(code // grid * tile, tile), tile)
        at_cols = pl.ds(pl.multiple_of(code % grid * tile, tile), tile)
        live = (slot < live_slots).astype(f32)
        err = (tiles[slot].astype(f32) - pred[at_rows, at_cols]) * live
        sse = sse + err * err
        err_b[at_rows, at_cols] = err.astype(bf16)
    err_all = err_b[...]
    total = jnp.sum(sse)
    counted = live_slots.astype(f32) * float(tile * tile)
    row = lax.broadcasted_iota(jnp.int32, stats.shape, 0)
    stats[...] = jnp.where(row == 0, total, jnp.where(row == 1, counted, 0.0))
    grad_u[...] = step_size * dot(err_all, item_b)
    grad_v[...] = step_size * dot(err_all, user_b, TN)
    copies[2].wait()
    base_v[...] = (1.0 - step_size * item_prec) * items[...] + noise_scale * noise_v[...].astype(
        f32
    )
    copies[1].wait()
    base_u[...] = (1.0 - step_size * prior_prec) * users[...] + noise_scale * noise_u[...].astype(
        f32
    )


def tile_pass(stratum, place, codes, count, ratings, user_noise, item_noise, *state):
    slots, tile = ratings.shape[2:4]
    rows, rank = user_noise.shape[1:]
    noise_scale = math.sqrt(2.0 * step_size)
    width = rank // CORES
    outs = [shape(rows, rank)] * 4 + [shape(RIDERS, width)]
    if stratum:
        outs += [shape(rows, width)] * 2
    return pl.pallas_call(
        functools.partial(tile_kernel, stratum, noise_scale),
        out_shape=tuple(outs),
        in_specs=[SMEM] * 3 + [HBM] * 3 + [VMEM if stratum else HBM] * len(state),
        out_specs=(VMEM,) * len(outs),
        scratch_shapes=[
            pltpu.VMEM((slots, tile, tile), bf16),
            pltpu.VMEM((rows, rank), bf16),
            pltpu.VMEM((rows, rank), bf16),
            pltpu.VMEM((rows, rank), f32),
            pltpu.VMEM((rows, rank), f32),
            pltpu.VMEM((rows, rows), f32),
            pltpu.VMEM((rows, rows), bf16),
            pltpu.SemaphoreType.DMA((5,)),
        ],
        compiler_params=PARAMS,
        cost_estimate=cost(6 * rows * rows * rank, 16 * rows * rank),
        name="tile_pass",
    )(place, codes, count, ratings, user_noise, item_noise, *state)


def first_kernel(place, feats_in, weights_in, users_in, own_mean, other_mean, send, keep, old, mean, feats, weights, users, sems):
    copies = [
        pltpu.make_async_copy(source, target, sems.at[n])
        for n, (source, target) in enumerate(
            [(weights_in, weights), (feats_in, feats), (users_in, users)]
        )
    ]
    for copy in copies:
        copy.start()
    here = place[0]
    copies[0].wait()
    weights_b = weights[...].astype(bf16)
    copies[1].wait()
    mean[...] = dot(feats[...], weights_b)
    copies[2].wait()
    for grad, means, which in ((send, other_mean, 1 - here), (keep, own_mean, here)):
        mean_now = half_of(mean, which)
        means[...] = mean_now
        offset = (half_of(users, which) - mean_now).astype(bf16)
        grad[...] = dot(feats[...], offset, TN)
    rows, width = old.shape
    start = place[1] * (weights.shape[0] // 2) + place[2] * rows
    cols = pl.ds(pl.multiple_of(here * width, width), width)
    old[...] = weights[pl.ds(pl.multiple_of(start, rows), rows), cols]


def first_pass(place, feats, weights, users):
    rows, rank = users.shape
    feat = weights.shape[0]
    width = rank // CORES
    return pl.pallas_call(
        first_kernel,
        out_shape=(shape(rows, width),) * 2 + (shape(feat, width),) * 2 + (shape(feat // 4, width),),
        in_specs=[SMEM] + [HBM] * 3,
        out_specs=(VMEM,) * 5,
        scratch_shapes=[
            pltpu.VMEM(users.shape, f32),
            pltpu.VMEM(feats.shape, bf16),
            pltpu.VMEM(weights.shape, f32),
            pltpu.VMEM(users.shape, f32),
            pltpu.SemaphoreType.DMA((3,)),
        ],
        compiler_params=PARAMS,
        cost_estimate=cost(4 * rows * feat * rank, 8 * feat * rank),
        name="first_pass",
    )(place, feats, weights, users)


def widen_kernel(narrow_in, wide, narrow, sem):
    copy = pltpu.make_async_copy(narrow_in, narrow, sem.at[0])
    copy.start()
    copy.wait()
    wide[...] = narrow[...].astype(f32)


def widen_pass(narrow):
    return pl.pallas_call(
        widen_kernel,
        out_shape=shape(*narrow.shape),
        in_specs=[HBM],
        out_specs=VMEM,
        scratch_shapes=[pltpu.VMEM(narrow.shape, bf16), pltpu.SemaphoreType.DMA((1,))],
        compiler_params=PARAMS,
        name="widen_pass",
    )(narrow)


def join_kernel(own, other, both, sem):
    rows = other.shape[0]
    copy = pltpu.make_async_copy(own, both.at[:rows], sem.at[0])
    copy.start()
    both[rows:, :] = other[...].astype(bf16)
    copy.wait()


def join_pass(own, other):
    rows, feat = own.shape
    return pl.pallas_call(
        join_kernel,
        out_shape=shape(CORES * rows, feat, dtype=bf16),
        in_specs=[HBM, VMEM],
        out_specs=VMEM,
        scratch_shapes=[pltpu.SemaphoreType.DMA((1,))],
        compiler_params=PARAMS,
        name="join_pass",
    )(own, other)


def prior_kernel(places, place, feats, part, got, own_cols, other_cols, stats, more_stats, own_mean, other_mean, send, keep, *refs):
    rows = own_cols.shape[0]
    half = keep.shape[0]
    core, bit = place[0], place[1]
    here = pl.ds(pl.multiple_of(bit * half, half), half)
    there = pl.ds(pl.multiple_of((1 - bit) * half, half), half)
    offset = refs[-1]
    mean = dot(feats[:, here], part[...].astype(bf16)) + dot(feats[:, there], got[...].astype(bf16))
    own_mean[...] = mean[:rows]
    other_mean[...] = mean[rows:]
    offset[:rows, :] = (own_cols[...] - mean[:rows]).astype(bf16)
    offset[rows:, :] = (other_cols[...] - mean[rows:]).astype(bf16)
    send[half:, :] = stats[...] + more_stats[...]
    if places is None:
        send[:half, :] = dot(feats[:, there], offset[...], TN)
        keep[...] = dot(feats[:, here], offset[...], TN)
        return
    old, full = refs[:2]
    full[here, :] = part[...]
    full[there, :] = got[...]
    start = place[place.shape[0] - 1] * old.shape[0]
    if old.shape[0] % 8 == 0:
        start = pl.multiple_of(start, old.shape[0])
    old[...] = full[pl.ds(start, old.shape[0]), :]
    full[...] = dot(feats[...], offset[...], TN)
    blocks = len(places[0])
    block = 2 * half // blocks
    for ref, which in ((send, 1 - bit), (keep, bit)):
        for n in range(blocks // 2):
            source = jnp.int32(0)
            for c, order in enumerate(places):
                for b in range(2):
                    source = jnp.where((core == c) & (which == b), order[b * blocks // 2 + n], source)
            source = source * block
            if block % 8 == 0:
                source = pl.multiple_of(source, block)
            ref[n * block : (n + 1) * block, :] = full[pl.ds(source, block), :]


def prior_pass(place, feats, part, got, own_cols, other_cols, stats, more_stats, places=None):
    rows, width = own_cols.shape
    half = part.shape[0]
    outs = [shape(rows, width)] * 2 + [shape(half + stats.shape[0], width), shape(half, width)]
    scratch = [pltpu.VMEM((CORES * rows, width), bf16)]
    if places is not None:
        outs.append(shape(2 * half // len(places[0]), width))
        scratch.insert(0, pltpu.VMEM((2 * half, width), f32))
    return pl.pallas_call(
        functools.partial(prior_kernel, places),
        out_shape=tuple(outs),
        in_specs=[SMEM] + [VMEM] * 7,
        out_specs=(VMEM,) * len(outs),
        scratch_shapes=scratch,
        compiler_params=PARAMS,
        cost_estimate=cost(16 * rows * half * width, 16 * rows * half),
        name="prior_pass",
    )(place, feats, part, got, own_cols, other_cols, stats, more_stats)


def step_kernel(halving, slot, place, held, got, sent, more, *refs):
    send = refs[-2] if halving else refs[-1]
    riders = sent.shape[0] - RIDERS, more.shape[0] - RIDERS
    rider = sent[riders[0] :, :] + more[riders[1] :, :]
    rows = send.shape[0] - RIDERS
    if halving:
        bit = place[slot]
        for ref, which in ((send, 1 - bit), (refs[-1], bit)):
            at = pl.ds(pl.multiple_of(which * rows, 8), rows) if rows % 8 == 0 else pl.ds(which * rows, rows)
            ref[:rows, :] = held[at, :] + got[at, :]
    else:
        send[:rows, :] = held[:rows, :] + got[:rows, :]
    send[rows:, :] = rider


def step_pass(halving, stage, place, held, got, sent, more, rows, later=()):
    width = held.shape[1]
    outs = [shape(rows // 2 + RIDERS, width), shape(rows // 2, width)] if halving else [shape(rows + RIDERS, width)]
    return pl.pallas_call(
        functools.partial(step_kernel, halving, 1 + stage),
        out_shape=tuple(outs),
        in_specs=[SMEM] + [VMEM] * 4 + [ANY] * len(later),
        out_specs=(VMEM,) * len(outs),
        compiler_params=PARAMS,
        cost_estimate=cost(rows * width, 12 * rows * width),
        name="step_pass",
    )(place, held, got, sent, more, *later)


def update_kernel(rate, held, got, sent, old, *refs):
    new, stats = refs[-2:]
    rows = old.shape[0]
    total = held[:rows, :] + got[:rows, :]
    before = old[...]
    new[...] = before + rate * (prior_prec * total - weight_decay * before)
    stats[...] = sent[sent.shape[0] - RIDERS :, :] + got[rows:, :]


def update_pass(rate, held, got, sent, old, later=()):
    return pl.pallas_call(
        functools.partial(update_kernel, rate),
        out_shape=(shape(*old.shape), shape(RIDERS, old.shape[1])),
        in_specs=[VMEM] * 4 + [ANY] * len(later),
        out_specs=(VMEM,) * 2,
        compiler_params=PARAMS,
        cost_estimate=cost(4 * old.size, 16 * old.size),
        name="update_pass",
    )(held, got, sent, old, *later)


def gather_kernel(slot, place, part, got, both):
    rows = part.shape[0]
    bit = place[slot]
    both[pl.ds(pl.multiple_of(bit * rows, rows), rows), :] = part[...]
    both[pl.ds(pl.multiple_of((1 - bit) * rows, rows), rows), :] = got[...]


def gather_pass(stage, place, part, got):
    rows, width = part.shape
    return pl.pallas_call(
        functools.partial(gather_kernel, 1 + stage),
        out_shape=shape(2 * rows, width),
        in_specs=[SMEM, VMEM, VMEM],
        out_specs=VMEM,
        compiler_params=PARAMS,
        cost_estimate=cost(rows * width, 16 * rows * width),
        name="gather_pass",
    )(place, part, got)


def split_kernel(place, both, mine, other):
    rows = mine.shape[0]
    for ref, which in ((mine, place[0]), (other, 1 - place[0])):
        at = pl.ds(pl.multiple_of(which * rows, 8), rows) if rows % 8 == 0 else pl.ds(which * rows, rows)
        ref[...] = both[at, :]


def split_pass(place, both):
    rows, width = both.shape
    return pl.pallas_call(
        split_kernel,
        out_shape=(shape(rows // CORES, width),) * 2,
        in_specs=[SMEM, VMEM],
        out_specs=(VMEM,) * 2,
        compiler_params=PARAMS,
        name="split_pass",
    )(place, both)


def across_kernel(place, mine, other, both):
    width = mine.shape[1]
    both[:, pl.ds(pl.multiple_of(place[0] * width, width), width)] = mine[...]
    both[:, pl.ds(pl.multiple_of((1 - place[0]) * width, width), width)] = other[...]


def across_pass(place, mine, other):
    rows, width = mine.shape
    return pl.pallas_call(
        across_kernel,
        out_shape=shape(rows, CORES * width),
        in_specs=[SMEM, VMEM, VMEM],
        out_specs=VMEM,
        compiler_params=PARAMS,
        name="across_pass",
    )(place, mine, other)


def last_kernel(place, stats, base, grad, own_mean, other_mean, base_v, grad_v, users, items):
    width = own_mean.shape[1]
    precision = precision_of(stats[...])
    precision = jnp.concatenate([precision] * CORES, 1)
    items[...] = base_v[...] + precision * grad_v[...]
    users[...] = base[...] + precision * grad[...]
    pull = step_size * prior_prec
    for mean, which in ((own_mean, place[0]), (other_mean, 1 - place[0])):
        at = pl.ds(pl.multiple_of(which * width, width), width)
        users[:, at] = users[:, at] + pull * mean[...]


def last_pass(place, stats, base, *state):
    return pl.pallas_call(
        last_kernel,
        out_shape=(shape(*base.shape),) * 2,
        in_specs=[SMEM] + [VMEM] * 7,
        out_specs=(VMEM,) * 2,
        compiler_params=PARAMS,
        cost_estimate=cost(8 * base.size, 32 * base.size),
        name="last_pass",
    )(place, stats, base, *state)


def bit_order(devices, core):
    bits = devices.bit_length() - 1
    far = list(range(3, bits))
    return [1, 2] + far if core == 0 else [2, 1] + far[::-1]


def swap(array, devices):
    return lax.ppermute(array, "user", [(i, i ^ 1) for i in range(devices)])


def roll(array, devices):
    return lax.ppermute(array, "user", [(i, (i + 1) % devices) for i in range(devices)])


def exchange(array, devices, stage):
    orders = [bit_order(devices, core) for core in range(CORES)]
    pairs = [(i, i ^ (1 << orders[i & 1][stage])) for i in range(devices)]
    return lax.ppermute(array, "user", pairs)


def final_places(devices):
    bits = devices.bit_length() - 1
    return [
        [
            sum(
                ((place >> (bits - 2 - n)) & 1) << (bit - 1)
                for n, bit in enumerate(bit_order(devices, core))
            )
            for place in range(devices // 2)
        ]
        for core in range(CORES)
    ]


def local(
    ratings,
    tile_index,
    tile_count,
    side_features,
    user_factors,
    item_factors,
    prior_weights,
    user_noise,
    item_noise,
):
    devices = lax.axis_size("user")
    own = lax.axis_index("user")
    stages = devices.bit_length() - 2
    strata = ratings.shape[1]
    feat = prior_weights.shape[0]
    rate = rate_scale / (user_factors.shape[0] * devices)
    core = own & 1
    zero, one = (bit_order(devices, c) for c in range(CORES))
    bits = [jnp.where(core == 0, own >> z, own >> o) & 1 for z, o in zip(zero, one, strict=True)]
    place = jnp.stack([core, *bits, own >> 1])
    tables = (place, tile_index, tile_count, ratings, user_noise, item_noise)

    own_mean, other_mean, send, held, old = first_pass(
        place, side_features, prior_weights, user_factors
    )
    got = swap(send, devices)
    base, grad, base_v, grad_v, stats = tile_pass(0, *tables, user_factors, item_factors)
    more = swap(stats, devices)
    send, held = step_pass(True, 0, place, held, got, stats, more, feat)
    feats = join_pass(side_features, swap(widen_pass(side_features), devices))
    for stratum in range(strata):
        last = stratum + 1 == strata
        if not last:
            base_v, grad_v = roll(base_v, devices), roll(grad_v, devices)
        got = exchange(send, devices, 0)
        send, held = step_pass(True, 1, place, held, got, send, got, feat // 2)
        for stage in range(1, stages - 1):
            got = exchange(send, devices, stage)
            rows = got.shape[0] - RIDERS
            if last:
                send, held = step_pass(True, stage + 1, place, held, got, send, got, rows)
            else:
                later = (base_v, grad_v) if stage == 2 else ()
                (send,) = step_pass(False, 0, place, held, got, send, got, rows, later)
                held = send
        got = exchange(send, devices, stages - 1)
        part, stats = update_pass(rate, held, got, send, old)
        if last:
            break
        old = part
        got = exchange(part, devices, 1)
        part = gather_pass(1, place, part, got)
        got = exchange(part, devices, 0)
        base, grad, base_v, grad_v, stats, own_cols, other_cols = tile_pass(
            stratum + 1, *tables, base, grad, own_mean, other_mean, stats, base_v, grad_v
        )
        more = swap(stats, devices)
        other_cols = swap(other_cols, devices)
        outs = prior_pass(
            place,
            feats,
            part,
            got,
            own_cols,
            other_cols,
            stats,
            more,
            final_places(devices) if stratum + 2 == strata else None,
        )
        own_mean, other_mean, send, held = outs[:4]
        if len(outs) > 4:
            old = outs[4]
        other_mean = swap(other_mean, devices)
    mine, other = split_pass(place, part)
    got = swap(other, devices)
    users, items = last_pass(place, stats, base, grad, own_mean, other_mean, base_v, grad_v)
    return (users, items, across_pass(place, mine, got))


def solution(mesh):
    return jax.shard_map(
        local,
        mesh=mesh,
        in_specs=(
            P("user", None, None, None, None),
            P("user", None, None),
            P("user", None),
            P("user", None),
            P("user", None),
            P("user", None),
            P(),
            P(None, "user", None),
            P(None, "user", None),
        ),
        out_specs=(P("user", None), P("user", None), P("user", None)),
        check_vma=False,
    )
```

```python
import functools
import math

import jax
import jax.numpy as jnp
from jax import lax
from jax.experimental import pallas as pl
from jax.experimental.pallas import tpu as pltpu
from jax.sharding import PartitionSpec as P

step_size = 0.01
prior_prec = 8.0
item_prec = 1.0
weight_decay = 1.0
rate_scale = 0.04

CORES = 2
RIDERS = 8
NN = (((1,), (0,)), ((), ()))
NT = (((1,), (1,)), ((), ()))
TN = (((0,), (0,)), ((), ()))
VMEM = pl.BlockSpec(memory_space=pltpu.VMEM)
SMEM = pl.BlockSpec(memory_space=pltpu.SMEM)
HBM = pl.BlockSpec(memory_space=pltpu.HBM)
ANY = pl.BlockSpec(memory_space=pl.ANY)
PARAMS = pltpu.CompilerParams(vmem_limit_bytes=8 << 20)
f32 = jnp.float32
bf16 = jnp.bfloat16


def dot(a, b, dims=NN):
    return lax.dot_general(a, b, dims, preferred_element_type=f32)


def shape(*dims, dtype=f32):
    return jax.ShapeDtypeStruct(dims, dtype)


def cost(flops, size):
    return pl.CostEstimate(flops=flops, bytes_accessed=size, transcendentals=0)


def where_am_i(devices):
    own = lax.axis_index("user")
    core = own & 1
    zero, one = (bit_order(devices, c) for c in range(CORES))
    bits = [jnp.where(core == 0, own >> z, own >> o) & 1 for z, o in zip(zero, one, strict=True)]
    return [core, *bits, own >> 1]


def half_of(ref, core):
    width = ref.shape[1] // CORES
    return ref[:, pl.ds(pl.multiple_of(core * width, width), width)]


def precision_of(stats):
    return (1.0 + stats[1:2, :] / 2.0) / (1.0 + stats[0:1, :] / 2.0)


def tile_kernel(stratum, noise_scale, devices, codes, count, ratings, user_noise, item_noise, *refs):
    if stratum == 0:
        users_in, items_in = refs[:2]
        base_u, grad_u, base_v, grad_v, stats = refs[2:7]
        refs = refs[7:]
    else:
        old_base, old_grad, own_mean, other_mean, old_stats, old_base_v, old_grad_v = refs[:7]
        base_u, grad_u, base_v, grad_v, stats, own_cols, other_cols = refs[7:14]
        refs = refs[14:]
    tiles, noise_u, noise_v, users, items, pred, err_b, sems = refs
    core = where_am_i(devices)[0]
    rows, rank = users.shape
    width = rank // CORES
    tile = tiles.shape[-1]
    grid = rows // tile
    copies = [
        pltpu.make_async_copy(source, target, sems.at[n])
        for n, (source, target) in enumerate(
            [
                (ratings.at[0, stratum], tiles),
                (user_noise.at[stratum], noise_u),
                (item_noise.at[stratum], noise_v),
            ]
            + ([(users_in, users), (items_in, items)] if stratum == 0 else [])
        )
    ]
    for copy in copies[::-1]:
        copy.start()
    if stratum == 0:
        copies[4].wait()
        copies[3].wait()
    else:
        precision = precision_of(old_stats[...])
        precision = jnp.concatenate([precision] * CORES, 1)
        items[...] = old_base_v[...] + precision * old_grad_v[...]
        new = old_base[...] + precision * old_grad[...]
        here = core == 0
        pull = step_size * prior_prec
        left = jnp.where(here, own_mean[...], other_mean[...])
        right = jnp.where(here, other_mean[...], own_mean[...])
        users[:, :width] = new[:, :width] + pull * left
        users[:, width:] = new[:, width:] + pull * right
        own_cols[...] = half_of(users, core)
        other_cols[...] = half_of(users, 1 - core)
    user_b = users[...].astype(bf16)
    item_b = items[...].astype(bf16)
    pred[...] = dot(user_b, item_b, NT)
    err_b[...] = jnp.zeros_like(err_b)
    live_slots = count[0, stratum]
    sse = jnp.zeros((tile, tile), f32)
    copies[0].wait()
    for slot in range(tiles.shape[0]):
        code = codes[0, stratum, slot]
        at_rows = pl.ds(pl.multiple_of(code // grid * tile, tile), tile)
        at_cols = pl.ds(pl.multiple_of(code % grid * tile, tile), tile)
        live = (slot < live_slots).astype(f32)
        err = (tiles[slot].astype(f32) - pred[at_rows, at_cols]) * live
        sse = sse + err * err
        err_b[at_rows, at_cols] = err.astype(bf16)
    err_all = err_b[...]
    total = jnp.sum(sse)
    counted = live_slots.astype(f32) * float(tile * tile)
    row = lax.broadcasted_iota(jnp.int32, stats.shape, 0)
    stats[...] = jnp.where(row == 0, total, jnp.where(row == 1, counted, 0.0))
    grad_u[...] = step_size * dot(err_all, item_b)
    grad_v[...] = step_size * dot(err_all, user_b, TN)
    copies[2].wait()
    base_v[...] = (1.0 - step_size * item_prec) * items[...] + noise_scale * noise_v[...].astype(
        f32
    )
    copies[1].wait()
    base_u[...] = (1.0 - step_size * prior_prec) * users[...] + noise_scale * noise_u[...].astype(
        f32
    )


def tile_pass(stratum, devices, codes, count, ratings, user_noise, item_noise, *state):
    slots, tile = ratings.shape[2:4]
    rows, rank = user_noise.shape[1:]
    noise_scale = math.sqrt(2.0 * step_size)
    width = rank // CORES
    outs = [shape(rows, rank)] * 4 + [shape(RIDERS, width)]
    if stratum:
        outs += [shape(rows, width)] * 2
    return pl.pallas_call(
        functools.partial(tile_kernel, stratum, noise_scale, devices),
        out_shape=tuple(outs),
        in_specs=[SMEM] * 2 + [HBM] * 3 + [VMEM if stratum else HBM] * len(state),
        out_specs=(VMEM,) * len(outs),
        scratch_shapes=[
            pltpu.VMEM((slots, tile, tile), bf16),
            pltpu.VMEM((rows, rank), bf16),
            pltpu.VMEM((rows, rank), bf16),
            pltpu.VMEM((rows, rank), f32),
            pltpu.VMEM((rows, rank), f32),
            pltpu.VMEM((rows, rows), f32),
            pltpu.VMEM((rows, rows), bf16),
            pltpu.SemaphoreType.DMA((5,)),
        ],
        compiler_params=PARAMS,
        cost_estimate=cost(6 * rows * rows * rank, 16 * rows * rank),
        name="tile_pass",
    )(codes, count, ratings, user_noise, item_noise, *state)


def first_kernel(devices, feats_in, weights_in, users_in, own_mean, other_mean, send, keep, old, mean, feats, weights, users, sems):
    copies = [
        pltpu.make_async_copy(source, target, sems.at[n])
        for n, (source, target) in enumerate(
            [(weights_in, weights), (feats_in, feats), (users_in, users)]
        )
    ]
    for copy in copies:
        copy.start()
    place = where_am_i(devices)
    here = place[0]
    copies[0].wait()
    weights_b = weights[...].astype(bf16)
    copies[1].wait()
    mean[...] = dot(feats[...], weights_b)
    copies[2].wait()
    for grad, means, which in ((send, other_mean, 1 - here), (keep, own_mean, here)):
        mean_now = half_of(mean, which)
        means[...] = mean_now
        offset = (half_of(users, which) - mean_now).astype(bf16)
        grad[...] = dot(feats[...], offset, TN)
    rows, width = old.shape
    start = place[1] * (weights.shape[0] // 2) + place[2] * rows
    cols = pl.ds(pl.multiple_of(here * width, width), width)
    old[...] = weights[pl.ds(pl.multiple_of(start, rows), rows), cols]


def first_pass(devices, feats, weights, users):
    rows, rank = users.shape
    feat = weights.shape[0]
    width = rank // CORES
    return pl.pallas_call(
        functools.partial(first_kernel, devices),
        out_shape=(shape(rows, width),) * 2 + (shape(feat, width),) * 2 + (shape(feat // 4, width),),
        in_specs=[HBM] * 3,
        out_specs=(VMEM,) * 5,
        scratch_shapes=[
            pltpu.VMEM(users.shape, f32),
            pltpu.VMEM(feats.shape, bf16),
            pltpu.VMEM(weights.shape, f32),
            pltpu.VMEM(users.shape, f32),
            pltpu.SemaphoreType.DMA((3,)),
        ],
        compiler_params=PARAMS,
        cost_estimate=cost(4 * rows * feat * rank, 8 * feat * rank),
        name="first_pass",
    )(feats, weights, users)


def widen_kernel(narrow_in, wide, narrow, sem):
    copy = pltpu.make_async_copy(narrow_in, narrow, sem.at[0])
    copy.start()
    copy.wait()
    wide[...] = narrow[...].astype(f32)


def widen_pass(narrow):
    return pl.pallas_call(
        widen_kernel,
        out_shape=shape(*narrow.shape),
        in_specs=[HBM],
        out_specs=VMEM,
        scratch_shapes=[pltpu.VMEM(narrow.shape, bf16), pltpu.SemaphoreType.DMA((1,))],
        compiler_params=PARAMS,
        name="widen_pass",
    )(narrow)


def join_kernel(own, other, both, turned):
    rows = other.shape[0]
    both[:rows, :] = own[...]
    both[rows:, :] = other[...].astype(bf16)
    turned[:, :rows] = own[...].T
    turned[:, rows:] = other[...].T.astype(bf16)


def join_pass(own, other):
    rows, feat = own.shape
    return pl.pallas_call(
        join_kernel,
        out_shape=(shape(CORES * rows, feat, dtype=bf16), shape(feat, CORES * rows, dtype=bf16)),
        in_specs=[VMEM, VMEM],
        out_specs=(VMEM, VMEM),
        compiler_params=PARAMS,
        cost_estimate=cost(rows * feat, 12 * rows * feat),
        name="join_pass",
    )(own, other)


def part_kernel(devices, feats, part, mean):
    half = part.shape[0]
    bit = where_am_i(devices)[1]
    here = pl.ds(pl.multiple_of(bit * half, half), half)
    mean[...] = dot(feats[:, here], part[...].astype(bf16))


def part_pass(devices, feats, part):
    rows = feats.shape[0]
    half, width = part.shape
    return pl.pallas_call(
        functools.partial(part_kernel, devices),
        out_shape=shape(rows, width),
        in_specs=[VMEM, VMEM],
        out_specs=VMEM,
        compiler_params=PARAMS,
        cost_estimate=cost(2 * rows * half * width, 4 * rows * half),
        name="part_pass",
    )(feats, part)


def prior_kernel(places, devices, feats, turned, begun, part, got, own_cols, other_cols, stats, more_stats, own_mean, other_mean, send, keep, *refs):
    rows = own_cols.shape[0]
    half = keep.shape[0]
    place = where_am_i(devices)
    core, bit = place[0], place[1]
    here = pl.ds(pl.multiple_of(bit * half, half), half)
    there = pl.ds(pl.multiple_of((1 - bit) * half, half), half)
    offset = refs[-1]
    mean = begun[...] + dot(feats[:, there], got[...].astype(bf16))
    own_mean[...] = mean[:rows]
    other_mean[...] = mean[rows:]
    offset[:rows, :] = (own_cols[...] - mean[:rows]).astype(bf16)
    offset[rows:, :] = (other_cols[...] - mean[rows:]).astype(bf16)
    send[half:, :] = stats[...] + more_stats[...]
    if places is None:
        send[:half, :] = dot(turned[there, :], offset[...])
        keep[...] = dot(turned[here, :], offset[...])
        return
    old, full = refs[:2]
    full[here, :] = part[...]
    full[there, :] = got[...]
    start = place[-1] * old.shape[0]
    if old.shape[0] % 8 == 0:
        start = pl.multiple_of(start, old.shape[0])
    old[...] = full[pl.ds(start, old.shape[0]), :]
    full[...] = dot(turned[...], offset[...])
    blocks = len(places[0])
    block = 2 * half // blocks
    for ref, which in ((send, 1 - bit), (keep, bit)):
        for n in range(blocks // 2):
            source = jnp.int32(0)
            for c, order in enumerate(places):
                for b in range(2):
                    source = jnp.where((core == c) & (which == b), order[b * blocks // 2 + n], source)
            source = source * block
            if block % 8 == 0:
                source = pl.multiple_of(source, block)
            ref[n * block : (n + 1) * block, :] = full[pl.ds(source, block), :]


def prior_pass(devices, feats, turned, begun, part, got, own_cols, other_cols, stats, more_stats, places=None):
    rows, width = own_cols.shape
    half = part.shape[0]
    outs = [shape(rows, width)] * 2 + [shape(half + stats.shape[0], width), shape(half, width)]
    scratch = [pltpu.VMEM((CORES * rows, width), bf16)]
    if places is not None:
        outs.append(shape(2 * half // len(places[0]), width))
        scratch.insert(0, pltpu.VMEM((2 * half, width), f32))
    return pl.pallas_call(
        functools.partial(prior_kernel, places, devices),
        out_shape=tuple(outs),
        in_specs=[VMEM] * 9,
        out_specs=(VMEM,) * len(outs),
        scratch_shapes=scratch,
        compiler_params=PARAMS,
        cost_estimate=cost(16 * rows * half * width, 16 * rows * half),
        name="prior_pass",
    )(feats, turned, begun, part, got, own_cols, other_cols, stats, more_stats)


def step_kernel(halving, slot, devices, held, got, sent, more, *refs):
    send = refs[-2] if halving else refs[-1]
    riders = sent.shape[0] - RIDERS, more.shape[0] - RIDERS
    rider = sent[riders[0] :, :] + more[riders[1] :, :]
    rows = send.shape[0] - RIDERS
    if halving:
        bit = where_am_i(devices)[slot]
        for ref, which in ((send, 1 - bit), (refs[-1], bit)):
            at = pl.ds(pl.multiple_of(which * rows, 8), rows) if rows % 8 == 0 else pl.ds(which * rows, rows)
            ref[:rows, :] = held[at, :] + got[at, :]
    else:
        send[:rows, :] = held[:rows, :] + got[:rows, :]
    send[rows:, :] = rider


def step_pass(halving, stage, devices, held, got, sent, more, rows, later=()):
    width = held.shape[1]
    outs = [shape(rows // 2 + RIDERS, width), shape(rows // 2, width)] if halving else [shape(rows + RIDERS, width)]
    return pl.pallas_call(
        functools.partial(step_kernel, halving, 1 + stage, devices),
        out_shape=tuple(outs),
        in_specs=[VMEM] * 4 + [ANY] * len(later),
        out_specs=(VMEM,) * len(outs),
        compiler_params=PARAMS,
        cost_estimate=cost(rows * width, 12 * rows * width),
        name="step_pass",
    )(held, got, sent, more, *later)


def update_kernel(rate, held, got, sent, old, *refs):
    new, stats = refs[-2:]
    rows = old.shape[0]
    total = held[:rows, :] + got[:rows, :]
    before = old[...]
    new[...] = before + rate * (prior_prec * total - weight_decay * before)
    stats[...] = sent[sent.shape[0] - RIDERS :, :] + got[rows:, :]


def update_pass(rate, held, got, sent, old, later=()):
    return pl.pallas_call(
        functools.partial(update_kernel, rate),
        out_shape=(shape(*old.shape), shape(RIDERS, old.shape[1])),
        in_specs=[VMEM] * 4 + [ANY] * len(later),
        out_specs=(VMEM,) * 2,
        compiler_params=PARAMS,
        cost_estimate=cost(4 * old.size, 16 * old.size),
        name="update_pass",
    )(held, got, sent, old, *later)


def gather_kernel(slot, devices, part, got, both):
    rows = part.shape[0]
    bit = where_am_i(devices)[slot]
    both[pl.ds(pl.multiple_of(bit * rows, rows), rows), :] = part[...]
    both[pl.ds(pl.multiple_of((1 - bit) * rows, rows), rows), :] = got[...]


def gather_pass(stage, devices, part, got):
    rows, width = part.shape
    return pl.pallas_call(
        functools.partial(gather_kernel, 1 + stage, devices),
        out_shape=shape(2 * rows, width),
        in_specs=[VMEM, VMEM],
        out_specs=VMEM,
        compiler_params=PARAMS,
        cost_estimate=cost(rows * width, 16 * rows * width),
        name="gather_pass",
    )(part, got)


def split_kernel(devices, both, mine, other):
    place = where_am_i(devices)
    rows = mine.shape[0]
    for ref, which in ((mine, place[0]), (other, 1 - place[0])):
        at = pl.ds(pl.multiple_of(which * rows, 8), rows) if rows % 8 == 0 else pl.ds(which * rows, rows)
        ref[...] = both[at, :]


def split_pass(devices, both):
    rows, width = both.shape
    return pl.pallas_call(
        functools.partial(split_kernel, devices),
        out_shape=(shape(rows // CORES, width),) * 2,
        in_specs=[VMEM],
        out_specs=(VMEM,) * 2,
        compiler_params=PARAMS,
        name="split_pass",
    )(both)


def across_kernel(devices, mine, other, both):
    place = where_am_i(devices)
    width = mine.shape[1]
    both[:, pl.ds(pl.multiple_of(place[0] * width, width), width)] = mine[...]
    both[:, pl.ds(pl.multiple_of((1 - place[0]) * width, width), width)] = other[...]


def across_pass(devices, mine, other):
    rows, width = mine.shape
    return pl.pallas_call(
        functools.partial(across_kernel, devices),
        out_shape=shape(rows, CORES * width),
        in_specs=[VMEM, VMEM],
        out_specs=VMEM,
        compiler_params=PARAMS,
        name="across_pass",
    )(mine, other)


def last_kernel(devices, stats, base, grad, own_mean, other_mean, base_v, grad_v, users, items):
    place = where_am_i(devices)
    width = own_mean.shape[1]
    precision = precision_of(stats[...])
    precision = jnp.concatenate([precision] * CORES, 1)
    items[...] = base_v[...] + precision * grad_v[...]
    users[...] = base[...] + precision * grad[...]
    pull = step_size * prior_prec
    for mean, which in ((own_mean, place[0]), (other_mean, 1 - place[0])):
        at = pl.ds(pl.multiple_of(which * width, width), width)
        users[:, at] = users[:, at] + pull * mean[...]


def last_pass(devices, stats, base, *state):
    return pl.pallas_call(
        functools.partial(last_kernel, devices),
        out_shape=(shape(*base.shape),) * 2,
        in_specs=[VMEM] * 7,
        out_specs=(VMEM,) * 2,
        compiler_params=PARAMS,
        cost_estimate=cost(8 * base.size, 32 * base.size),
        name="last_pass",
    )(stats, base, *state)


def bit_order(devices, core):
    bits = devices.bit_length() - 1
    far = list(range(3, bits))
    return [1, 2] + far if core == 0 else [2, 1] + far[::-1]


def swap(array, devices):
    return lax.ppermute(array, "user", [(i, i ^ 1) for i in range(devices)])


def roll(array, devices):
    return lax.ppermute(array, "user", [(i, (i + 1) % devices) for i in range(devices)])


def exchange(array, devices, stage):
    orders = [bit_order(devices, core) for core in range(CORES)]
    pairs = [(i, i ^ (1 << orders[i & 1][stage])) for i in range(devices)]
    return lax.ppermute(array, "user", pairs)


def final_places(devices):
    bits = devices.bit_length() - 1
    return [
        [
            sum(
                ((place >> (bits - 2 - n)) & 1) << (bit - 1)
                for n, bit in enumerate(bit_order(devices, core))
            )
            for place in range(devices // 2)
        ]
        for core in range(CORES)
    ]


def local(
    ratings,
    tile_index,
    tile_count,
    side_features,
    user_factors,
    item_factors,
    prior_weights,
    user_noise,
    item_noise,
):
    devices = lax.axis_size("user")
    stages = devices.bit_length() - 2
    strata = ratings.shape[1]
    feat = prior_weights.shape[0]
    rate = rate_scale / (user_factors.shape[0] * devices)
    tables = (devices, tile_index, tile_count, ratings, user_noise, item_noise)

    own_mean, other_mean, send, held, old = first_pass(
        devices, side_features, prior_weights, user_factors
    )
    got = swap(send, devices)
    base, grad, base_v, grad_v, stats = tile_pass(0, *tables, user_factors, item_factors)
    more = swap(stats, devices)
    send, held = step_pass(True, 0, devices, held, got, stats, more, feat)
    feats, turned = join_pass(side_features, swap(widen_pass(side_features), devices))
    for stratum in range(strata):
        last = stratum + 1 == strata
        if not last:
            base_v, grad_v = roll(base_v, devices), roll(grad_v, devices)
        got = exchange(send, devices, 0)
        send, held = step_pass(True, 1, devices, held, got, send, got, feat // 2)
        for stage in range(1, stages - 1):
            got = exchange(send, devices, stage)
            rows = got.shape[0] - RIDERS
            if last:
                send, held = step_pass(True, stage + 1, devices, held, got, send, got, rows)
            else:
                later = (base_v,) if stage == 1 else ()
                (send,) = step_pass(False, 0, devices, held, got, send, got, rows, later)
                held = send
        got = exchange(send, devices, stages - 1)
        part, stats = update_pass(rate, held, got, send, old, () if last else (grad_v,))
        if last:
            break
        old = part
        got = exchange(part, devices, 1)
        part = gather_pass(1, devices, part, got)
        got = exchange(part, devices, 0)
        begun = part_pass(devices, feats, part)
        base, grad, base_v, grad_v, stats, own_cols, other_cols = tile_pass(
            stratum + 1, *tables, base, grad, own_mean, other_mean, stats, base_v, grad_v
        )
        more = swap(stats, devices)
        other_cols = swap(other_cols, devices)
        outs = prior_pass(
            devices,
            feats,
            turned,
            begun,
            part,
            got,
            own_cols,
            other_cols,
            stats,
            more,
            final_places(devices) if stratum + 2 == strata else None,
        )
        own_mean, other_mean, send, held = outs[:4]
        if len(outs) > 4:
            old = outs[4]
        other_mean = swap(other_mean, devices)
    mine, other = split_pass(devices, part)
    got = swap(other, devices)
    users, items = last_pass(devices, stats, base, grad, own_mean, other_mean, base_v, grad_v)
    return (users, items, across_pass(devices, mine, got))


def solution(mesh):
    return jax.shard_map(
        local,
        mesh=mesh,
        in_specs=(
            P("user", None, None, None, None),
            P("user", None, None),
            P("user", None),
            P("user", None),
            P("user", None),
            P("user", None),
            P(),
            P(None, "user", None),
            P(None, "user", None),
        ),
        out_specs=(P("user", None), P("user", None), P("user", None)),
        check_vma=False,
    )
```

```python
import functools
import math

import jax
import jax.numpy as jnp
from jax import lax
from jax.experimental import pallas as pl
from jax.experimental.pallas import tpu as pltpu
from jax.sharding import PartitionSpec as P

step_size = 0.01
prior_prec = 8.0
item_prec = 1.0
weight_decay = 1.0
rate_scale = 0.04

CORES = 2
CHUNKS = 2
RIDERS = 8
NN = (((1,), (0,)), ((), ()))
NT = (((1,), (1,)), ((), ()))
TN = (((0,), (0,)), ((), ()))
VMEM = pl.BlockSpec(memory_space=pltpu.VMEM)
SMEM = pl.BlockSpec(memory_space=pltpu.SMEM)
HBM = pl.BlockSpec(memory_space=pltpu.HBM)
ANY = pl.BlockSpec(memory_space=pl.ANY)
PARAMS = pltpu.CompilerParams(vmem_limit_bytes=8 << 20)
f32 = jnp.float32
bf16 = jnp.bfloat16


def dot(a, b, dims=NN):
    return lax.dot_general(a, b, dims, preferred_element_type=f32)


def shape(*dims, dtype=f32):
    return jax.ShapeDtypeStruct(dims, dtype)


def cost(flops, size):
    return pl.CostEstimate(flops=flops, bytes_accessed=size, transcendentals=0)


def where_am_i(devices, chunk=0):
    own = lax.axis_index("user")
    core = own & 1
    zero, one = (bit_order(devices, c, chunk) for c in range(CORES))
    bits = [jnp.where(core == 0, own >> z, own >> o) & 1 for z, o in zip(zero, one, strict=True)]
    return [core, *bits, own >> 1]


def rows_at(which, rows):
    start = which * rows
    return pl.ds(pl.multiple_of(start, rows) if rows % 8 == 0 else start, rows)


def half_of(ref, core):
    width = ref.shape[1] // CORES
    return ref[:, pl.ds(pl.multiple_of(core * width, width), width)]


def precision_of(stats):
    return (1.0 + stats[1:2, :] / 2.0) / (1.0 + stats[0:1, :] / 2.0)


def tile_kernel(stratum, noise_scale, devices, codes, count, ratings, user_noise, item_noise, *refs):
    if stratum == 0:
        users_in, items_in = refs[:2]
        base_u, grad_u, base_v, grad_v, stats = refs[2:7]
        refs = refs[7:]
    else:
        old_base, old_grad, own_mean, other_mean, old_stats, old_base_v, old_grad_v = refs[:7]
        base_u, grad_u, base_v, grad_v, stats, own_cols, other_cols = refs[7:14]
        refs = refs[14:]
    tiles, noise_u, noise_v, users, items, pred, err_b, sems = refs
    core = where_am_i(devices)[0]
    rows, rank = users.shape
    width = rank // CORES
    tile = tiles.shape[-1]
    grid = rows // tile
    copies = [
        pltpu.make_async_copy(source, target, sems.at[n])
        for n, (source, target) in enumerate(
            [
                (ratings.at[0, stratum], tiles),
                (user_noise.at[stratum], noise_u),
                (item_noise.at[stratum], noise_v),
            ]
            + ([(users_in, users), (items_in, items)] if stratum == 0 else [])
        )
    ]
    for copy in copies[::-1]:
        copy.start()
    if stratum == 0:
        copies[4].wait()
        copies[3].wait()
    else:
        precision = precision_of(old_stats[...])
        precision = jnp.concatenate([precision] * CORES, 1)
        items[...] = old_base_v[...] + precision * old_grad_v[...]
        new = old_base[...] + precision * old_grad[...]
        here = core == 0
        pull = step_size * prior_prec
        left = jnp.where(here, own_mean[...], other_mean[...])
        right = jnp.where(here, other_mean[...], own_mean[...])
        users[:, :width] = new[:, :width] + pull * left
        users[:, width:] = new[:, width:] + pull * right
        own_cols[...] = half_of(users, core)
        other_cols[...] = half_of(users, 1 - core)
    user_b = users[...].astype(bf16)
    item_b = items[...].astype(bf16)
    pred[...] = dot(user_b, item_b, NT)
    err_b[...] = jnp.zeros_like(err_b)
    live_slots = count[0, stratum]
    sse = jnp.zeros((tile, tile), f32)
    copies[0].wait()
    for slot in range(tiles.shape[0]):
        code = codes[0, stratum, slot]
        at_rows = pl.ds(pl.multiple_of(code // grid * tile, tile), tile)
        at_cols = pl.ds(pl.multiple_of(code % grid * tile, tile), tile)
        live = (slot < live_slots).astype(f32)
        err = (tiles[slot].astype(f32) - pred[at_rows, at_cols]) * live
        sse = sse + err * err
        err_b[at_rows, at_cols] = err.astype(bf16)
    err_all = err_b[...]
    total = jnp.sum(sse)
    counted = live_slots.astype(f32) * float(tile * tile)
    row = lax.broadcasted_iota(jnp.int32, stats.shape, 0)
    stats[...] = jnp.where(row == 0, total, jnp.where(row == 1, counted, 0.0))
    grad_u[...] = step_size * dot(err_all, item_b)
    grad_v[...] = step_size * dot(err_all, user_b, TN)
    copies[2].wait()
    base_v[...] = (1.0 - step_size * item_prec) * items[...] + noise_scale * noise_v[...].astype(
        f32
    )
    copies[1].wait()
    base_u[...] = (1.0 - step_size * prior_prec) * users[...] + noise_scale * noise_u[...].astype(
        f32
    )


def tile_pass(stratum, devices, codes, count, ratings, user_noise, item_noise, *state):
    slots, tile = ratings.shape[2:4]
    rows, rank = user_noise.shape[1:]
    noise_scale = math.sqrt(2.0 * step_size)
    width = rank // CORES
    outs = [shape(rows, rank)] * 4 + [shape(RIDERS, width)]
    if stratum:
        outs += [shape(rows, width)] * 2
    return pl.pallas_call(
        functools.partial(tile_kernel, stratum, noise_scale, devices),
        out_shape=tuple(outs),
        in_specs=[SMEM] * 2 + [HBM] * 3 + [VMEM if stratum else HBM] * len(state),
        out_specs=(VMEM,) * len(outs),
        scratch_shapes=[
            pltpu.VMEM((slots, tile, tile), bf16),
            pltpu.VMEM((rows, rank), bf16),
            pltpu.VMEM((rows, rank), bf16),
            pltpu.VMEM((rows, rank), f32),
            pltpu.VMEM((rows, rank), f32),
            pltpu.VMEM((rows, rows), f32),
            pltpu.VMEM((rows, rows), bf16),
            pltpu.SemaphoreType.DMA((5,)),
        ],
        compiler_params=PARAMS,
        cost_estimate=cost(6 * rows * rows * rank, 16 * rows * rank),
        name="tile_pass",
    )(codes, count, ratings, user_noise, item_noise, *state)


def first_kernel(devices, feats_in, weights_in, users_in, own_mean, other_mean, *refs):
    sends, keeps, olds = refs[:CHUNKS], refs[CHUNKS : 2 * CHUNKS], refs[2 * CHUNKS : 3 * CHUNKS]
    mean, feats, weights, users, sems = refs[3 * CHUNKS :]
    copies = [
        pltpu.make_async_copy(source, target, sems.at[n])
        for n, (source, target) in enumerate(
            [(weights_in, weights), (feats_in, feats), (users_in, users)]
        )
    ]
    for copy in copies:
        copy.start()
    here = where_am_i(devices)[0]
    copies[0].wait()
    weights_b = weights[...].astype(bf16)
    copies[1].wait()
    mean[...] = dot(feats[...], weights_b)
    copies[2].wait()
    for grads, means, which in ((sends, other_mean, 1 - here), (keeps, own_mean, here)):
        mean_now = half_of(mean, which)
        means[...] = mean_now
        offset = (half_of(users, which) - mean_now).astype(bf16)
        for chunk, grad in enumerate(grads):
            depth = grad.shape[0]
            grad[...] = dot(feats[:, chunk * depth : (chunk + 1) * depth], offset, TN)
    for chunk, old in enumerate(olds):
        rows, width = old.shape
        _, first, second, *_ = where_am_i(devices, chunk)
        cols = pl.ds(pl.multiple_of(here * width, width), width)
        old[...] = weights[rows_at(chunk * 4 + first * 2 + second, rows), cols]


def first_pass(devices, feats, weights, users):
    rows, rank = users.shape
    feat = weights.shape[0]
    width = rank // CORES
    depth = feat // CHUNKS
    return pl.pallas_call(
        functools.partial(first_kernel, devices),
        out_shape=(shape(rows, width),) * 2
        + (shape(depth, width),) * (2 * CHUNKS)
        + (shape(depth // 4, width),) * CHUNKS,
        in_specs=[HBM] * 3,
        out_specs=(VMEM,) * (2 + 3 * CHUNKS),
        scratch_shapes=[
            pltpu.VMEM(users.shape, f32),
            pltpu.VMEM(feats.shape, bf16),
            pltpu.VMEM(weights.shape, f32),
            pltpu.VMEM(users.shape, f32),
            pltpu.SemaphoreType.DMA((3,)),
        ],
        compiler_params=PARAMS,
        cost_estimate=cost(4 * rows * feat * rank, 8 * feat * rank),
        name="first_pass",
    )(feats, weights, users)


def widen_kernel(narrow_in, wide, narrow, sem):
    copy = pltpu.make_async_copy(narrow_in, narrow, sem.at[0])
    copy.start()
    copy.wait()
    wide[...] = narrow[...].astype(f32)


def widen_pass(narrow):
    return pl.pallas_call(
        widen_kernel,
        out_shape=shape(*narrow.shape),
        in_specs=[HBM],
        out_specs=VMEM,
        scratch_shapes=[pltpu.VMEM(narrow.shape, bf16), pltpu.SemaphoreType.DMA((1,))],
        compiler_params=PARAMS,
        name="widen_pass",
    )(narrow)


def join_kernel(own, other, both, turned):
    rows = other.shape[0]
    both[:rows, :] = own[...]
    both[rows:, :] = other[...].astype(bf16)
    turned[:, :rows] = own[...].T
    turned[:, rows:] = other[...].T.astype(bf16)


def join_pass(own, other):
    rows, feat = own.shape
    return pl.pallas_call(
        join_kernel,
        out_shape=(shape(CORES * rows, feat, dtype=bf16), shape(feat, CORES * rows, dtype=bf16)),
        in_specs=[VMEM, VMEM],
        out_specs=(VMEM, VMEM),
        compiler_params=PARAMS,
        cost_estimate=cost(rows * feat, 12 * rows * feat),
        name="join_pass",
    )(own, other)


def halves_mean(feats, chunk, bit, part, got):
    half = part.shape[0]
    return dot(feats[:, rows_at(2 * chunk + bit, half)], part[...].astype(bf16)) + dot(
        feats[:, rows_at(2 * chunk + 1 - bit, half)], got[...].astype(bf16)
    )


def part_kernel(devices, feats, part, got, mean):
    mean[...] = halves_mean(feats, 0, where_am_i(devices)[1], part, got)


def part_pass(devices, feats, part, got):
    rows = feats.shape[0]
    half, width = part.shape
    return pl.pallas_call(
        functools.partial(part_kernel, devices),
        out_shape=shape(rows, width),
        in_specs=[VMEM] * 3,
        out_specs=VMEM,
        compiler_params=PARAMS,
        cost_estimate=cost(4 * rows * half * width, 4 * rows * half),
        name="part_pass",
    )(feats, part, got)


def find_offset(devices, feats, begun, part, got, own_cols, other_cols, own_mean, other_mean, offset):
    rows = own_cols.shape[0]
    mean = begun[...] + halves_mean(feats, 1, where_am_i(devices, 1)[1], part, got)
    own_mean[...] = mean[:rows]
    other_mean[...] = mean[rows:]
    offset[:rows, :] = (own_cols[...] - mean[:rows]).astype(bf16)
    offset[rows:, :] = (other_cols[...] - mean[rows:]).astype(bf16)


def prior_kernel(devices, feats, turned, begun, part, got, own_cols, other_cols, own_mean, other_mean, offset, send, keep):
    find_offset(devices, feats, begun, part, got, own_cols, other_cols, own_mean, other_mean, offset)
    bit = where_am_i(devices)[1]
    half = keep.shape[0]
    send[...] = dot(turned[rows_at(1 - bit, half), :], offset[...])
    keep[...] = dot(turned[rows_at(bit, half), :], offset[...])


def prior_pass(devices, feats, turned, begun, part, got, own_cols, other_cols):
    rows, width = own_cols.shape
    half = part.shape[0]
    return pl.pallas_call(
        functools.partial(prior_kernel, devices),
        out_shape=(shape(rows, width),) * 2
        + (shape(CORES * rows, width, dtype=bf16),)
        + (shape(half, width),) * 2,
        in_specs=[VMEM] * 7,
        out_specs=(VMEM,) * 5,
        compiler_params=PARAMS,
        cost_estimate=cost(16 * rows * half * width, 16 * rows * half),
        name="prior_pass",
    )(feats, turned, begun, part, got, own_cols, other_cols)


def rest_kernel(devices, turned, offset, stats, more_stats, send, keep):
    bit = where_am_i(devices, 1)[1]
    half = keep.shape[0]
    send[:half, :] = dot(turned[rows_at(2 + 1 - bit, half), :], offset[...])
    keep[...] = dot(turned[rows_at(2 + bit, half), :], offset[...])
    send[half:, :] = stats[...] + more_stats[...]


def rest_pass(devices, turned, offset, stats, more_stats):
    rows, width = offset.shape
    half = turned.shape[0] // (2 * CHUNKS)
    return pl.pallas_call(
        functools.partial(rest_kernel, devices),
        out_shape=(shape(half + RIDERS, width), shape(half, width)),
        in_specs=[VMEM] * 4,
        out_specs=(VMEM,) * 2,
        compiler_params=PARAMS,
        cost_estimate=cost(4 * rows * half * width, 4 * rows * half),
        name="rest_pass",
    )(turned, offset, stats, more_stats)


def final_kernel(places, devices, feats, turned, begun, part, got, first_part, first_got, own_cols, other_cols, stats, more_stats, own_mean, other_mean, send, keep, old, full, offset):
    find_offset(devices, feats, begun, part, got, own_cols, other_cols, own_mean, other_mean, offset)
    send[keep.shape[0] :, :] = stats[...] + more_stats[...]
    rows = part.shape[0]
    place = where_am_i(devices)
    for chunk, mine, theirs in ((0, first_part, first_got), (1, part, got)):
        bit = where_am_i(devices, chunk)[1]
        full[rows_at(2 * chunk + bit, rows), :] = mine[...]
        full[rows_at(2 * chunk + 1 - bit, rows), :] = theirs[...]
    old[...] = full[rows_at(place[-1], old.shape[0]), :]
    full[...] = dot(turned[...], offset[...])
    core, bit = place[0], place[1]
    blocks = len(places[0])
    block = full.shape[0] // blocks
    for ref, which in ((send, 1 - bit), (keep, bit)):
        for n in range(blocks // 2):
            source = jnp.int32(0)
            for c, order in enumerate(places):
                for b in range(2):
                    source = jnp.where((core == c) & (which == b), order[b * blocks // 2 + n], source)
            ref[n * block : (n + 1) * block, :] = full[rows_at(source, block), :]


def final_pass(places, devices, feats, turned, begun, part, got, first_part, first_got, own_cols, other_cols, stats, more_stats):
    rows, width = own_cols.shape
    feat = feats.shape[1]
    return pl.pallas_call(
        functools.partial(final_kernel, places, devices),
        out_shape=(shape(rows, width),) * 2
        + (shape(feat // 2 + RIDERS, width), shape(feat // 2, width), shape(feat // len(places[0]), width)),
        in_specs=[VMEM] * 11,
        out_specs=(VMEM,) * 5,
        scratch_shapes=[pltpu.VMEM((feat, width), f32), pltpu.VMEM((CORES * rows, width), bf16)],
        compiler_params=PARAMS,
        cost_estimate=cost(8 * rows * feat * width, 8 * rows * feat),
        name="final_pass",
    )(feats, turned, begun, part, got, first_part, first_got, own_cols, other_cols, stats, more_stats)


def step_kernel(halving, stage, chunk, riders, devices, held, got, *refs):
    send = refs[-2] if halving else refs[-1]
    rows = send.shape[0] - riders
    if halving:
        bit = where_am_i(devices, chunk)[1 + stage]
        for ref, which in ((send, 1 - bit), (refs[-1], bit)):
            at = rows_at(which, rows)
            ref[:rows, :] = held[at, :] + got[at, :]
    else:
        send[:rows, :] = held[:rows, :] + got[:rows, :]
    if riders:
        sent, more = refs[:2]
        send[rows:, :] = sent[sent.shape[0] - riders :, :] + more[more.shape[0] - riders :, :]


def step_pass(halving, stage, chunk, devices, held, got, rows, riders=(), later=()):
    width = held.shape[1]
    under = RIDERS if riders else 0
    outs = [shape(rows // 2 + under, width), shape(rows // 2, width)] if halving else [shape(rows + under, width)]
    return pl.pallas_call(
        functools.partial(step_kernel, halving, stage, chunk, under, devices),
        out_shape=tuple(outs),
        in_specs=[VMEM] * (2 + len(riders)) + [ANY] * len(later),
        out_specs=(VMEM,) * len(outs),
        compiler_params=PARAMS,
        cost_estimate=cost(rows * width, 12 * rows * width),
        name="step_pass",
    )(held, got, *riders, *later)


def update_kernel(rate, riding, held, got, old, *refs):
    rows = old.shape[0]
    new = refs[-2] if riding else refs[-1]
    total = held[:rows, :] + got[:rows, :]
    before = old[...]
    new[...] = before + rate * (prior_prec * total - weight_decay * before)
    if riding:
        refs[-1][...] = held_stats(refs[0]) + got[rows:, :]


def held_stats(sent):
    return sent[sent.shape[0] - RIDERS :, :]


def update_pass(rate, held, got, old, sent=None, later=()):
    riding = sent is not None
    out = shape(*old.shape)
    return pl.pallas_call(
        functools.partial(update_kernel, rate, riding),
        out_shape=(out, shape(RIDERS, old.shape[1])) if riding else out,
        in_specs=[VMEM] * (3 + riding) + [ANY] * len(later),
        out_specs=(VMEM,) * 2 if riding else VMEM,
        compiler_params=PARAMS,
        cost_estimate=cost(4 * old.size, 16 * old.size),
        name="update_pass",
    )(held, got, old, *([sent] if riding else []), *later)


def gather_kernel(stage, chunk, devices, part, got, both):
    rows = part.shape[0]
    bit = where_am_i(devices, chunk)[1 + stage]
    both[rows_at(bit, rows), :] = part[...]
    both[rows_at(1 - bit, rows), :] = got[...]


def gather_pass(stage, chunk, devices, part, got):
    rows, width = part.shape
    return pl.pallas_call(
        functools.partial(gather_kernel, stage, chunk, devices),
        out_shape=shape(2 * rows, width),
        in_specs=[VMEM, VMEM],
        out_specs=VMEM,
        compiler_params=PARAMS,
        cost_estimate=cost(rows * width, 16 * rows * width),
        name="gather_pass",
    )(part, got)


def split_kernel(devices, both, mine, other):
    place = where_am_i(devices)
    rows = mine.shape[0]
    for ref, which in ((mine, place[0]), (other, 1 - place[0])):
        at = pl.ds(pl.multiple_of(which * rows, 8), rows) if rows % 8 == 0 else pl.ds(which * rows, rows)
        ref[...] = both[at, :]


def split_pass(devices, both):
    rows, width = both.shape
    return pl.pallas_call(
        functools.partial(split_kernel, devices),
        out_shape=(shape(rows // CORES, width),) * 2,
        in_specs=[VMEM],
        out_specs=(VMEM,) * 2,
        compiler_params=PARAMS,
        name="split_pass",
    )(both)


def across_kernel(devices, mine, other, both):
    place = where_am_i(devices)
    width = mine.shape[1]
    both[:, pl.ds(pl.multiple_of(place[0] * width, width), width)] = mine[...]
    both[:, pl.ds(pl.multiple_of((1 - place[0]) * width, width), width)] = other[...]


def across_pass(devices, mine, other):
    rows, width = mine.shape
    return pl.pallas_call(
        functools.partial(across_kernel, devices),
        out_shape=shape(rows, CORES * width),
        in_specs=[VMEM, VMEM],
        out_specs=VMEM,
        compiler_params=PARAMS,
        name="across_pass",
    )(mine, other)


def last_kernel(devices, stats, base, grad, own_mean, other_mean, base_v, grad_v, users, items):
    place = where_am_i(devices)
    width = own_mean.shape[1]
    precision = precision_of(stats[...])
    precision = jnp.concatenate([precision] * CORES, 1)
    items[...] = base_v[...] + precision * grad_v[...]
    users[...] = base[...] + precision * grad[...]
    pull = step_size * prior_prec
    for mean, which in ((own_mean, place[0]), (other_mean, 1 - place[0])):
        at = pl.ds(pl.multiple_of(which * width, width), width)
        users[:, at] = users[:, at] + pull * mean[...]


def last_pass(devices, stats, base, *state):
    return pl.pallas_call(
        functools.partial(last_kernel, devices),
        out_shape=(shape(*base.shape),) * 2,
        in_specs=[VMEM] * 7,
        out_specs=(VMEM,) * 2,
        compiler_params=PARAMS,
        cost_estimate=cost(8 * base.size, 32 * base.size),
        name="last_pass",
    )(stats, base, *state)


def bit_order(devices, core, chunk=0):
    bits = devices.bit_length() - 1
    near = [1, 2] if core == chunk else [2, 1]
    far = list(range(3, bits))
    return near + (far if chunk == 0 else far[::-1])


def swap(array, devices):
    return lax.ppermute(array, "user", [(i, i ^ 1) for i in range(devices)])


def roll(array, devices):
    return lax.ppermute(array, "user", [(i, (i + 1) % devices) for i in range(devices)])


def exchange(array, devices, stage, chunk=0):
    orders = [bit_order(devices, core, chunk) for core in range(CORES)]
    pairs = [(i, i ^ (1 << orders[i & 1][stage])) for i in range(devices)]
    return lax.ppermute(array, "user", pairs)


def final_places(devices):
    bits = devices.bit_length() - 1
    return [
        [
            sum(
                ((place >> (bits - 2 - n)) & 1) << (bit - 1)
                for n, bit in enumerate(bit_order(devices, core))
            )
            for place in range(devices // 2)
        ]
        for core in range(CORES)
    ]


def local(
    ratings,
    tile_index,
    tile_count,
    side_features,
    user_factors,
    item_factors,
    prior_weights,
    user_noise,
    item_noise,
):
    devices = lax.axis_size("user")
    stages = devices.bit_length() - 2
    strata = ratings.shape[1]
    feat = prior_weights.shape[0]
    rate = rate_scale / (user_factors.shape[0] * devices)
    tables = (devices, tile_index, tile_count, ratings, user_noise, item_noise)

    both = range(CHUNKS)
    depth = feat // CHUNKS
    own_mean, other_mean, *outs = first_pass(
        devices, side_features, prior_weights, user_factors
    )
    helds, olds = outs[CHUNKS : 2 * CHUNKS], outs[2 * CHUNKS :]
    gots = [swap(send, devices) for send in outs[:CHUNKS]]
    base, grad, base_v, grad_v, stats = tile_pass(0, *tables, user_factors, item_factors)
    more = swap(stats, devices)
    sends = [None] * CHUNKS
    for c in both:
        riders = (stats, more) if c else ()
        sends[c], helds[c] = step_pass(True, 0, c, devices, helds[c], gots[c], depth, riders)
    feats, turned = join_pass(side_features, swap(widen_pass(side_features), devices))
    for stratum in range(strata - 1):
        base_v, grad_v = roll(base_v, devices), roll(grad_v, devices)
        for stage in range(stages - 1):
            for c in both:
                gots[c] = exchange(sends[c], devices, stage, c)
                riders = (sends[c], gots[c]) if c else ()
                rows = gots[c].shape[0] - RIDERS * c
                if stage < 1:
                    sends[c], helds[c] = step_pass(True, stage + 1, c, devices, helds[c], gots[c], rows, riders)
                else:
                    (sends[c],) = step_pass(False, 0, c, devices, helds[c], gots[c], rows, riders)
                    helds[c] = sends[c]
        for c in both:
            gots[c] = exchange(sends[c], devices, stages - 1, c)
            if c:
                olds[c], stats = update_pass(rate, helds[c], gots[c], olds[c], sends[c])
            else:
                olds[c] = update_pass(rate, helds[c], gots[c], olds[c])
        parts = list(olds)
        for c in both:
            parts[c] = gather_pass(1, c, devices, parts[c], exchange(parts[c], devices, 1, c))
        gots = [exchange(parts[c], devices, 0, c) for c in both]
        base, grad, base_v, grad_v, stats, own_cols, other_cols = tile_pass(
            stratum + 1, *tables, base, grad, own_mean, other_mean, stats, base_v, grad_v
        )
        more = swap(stats, devices)
        other_cols = swap(other_cols, devices)
        begun = part_pass(devices, feats, parts[0], gots[0])
        if stratum + 2 < strata:
            own_mean, other_mean, offset, sends[0], helds[0] = prior_pass(
                devices, feats, turned, begun, parts[1], gots[1], own_cols, other_cols
            )
            sends[1], helds[1] = rest_pass(devices, turned, offset, stats, more)
        else:
            own_mean, other_mean, send, held, old = final_pass(
                final_places(devices),
                devices,
                feats,
                turned,
                begun,
                parts[1],
                gots[1],
                parts[0],
                gots[0],
                own_cols,
                other_cols,
                stats,
                more,
            )
        other_mean = swap(other_mean, devices)
    for stage in range(stages - 1):
        got = exchange(send, devices, stage)
        send, held = step_pass(True, stage + 1, 0, devices, held, got, got.shape[0] - RIDERS, (send, got))
    got = exchange(send, devices, stages - 1)
    part, stats = update_pass(rate, held, got, old, send)
    mine, other = split_pass(devices, part)
    got = swap(other, devices)
    users, items = last_pass(devices, stats, base, grad, own_mean, other_mean, base_v, grad_v)
    return (users, items, across_pass(devices, mine, got))


def solution(mesh):
    return jax.shard_map(
        local,
        mesh=mesh,
        in_specs=(
            P("user", None, None, None, None),
            P("user", None, None),
            P("user", None),
            P("user", None),
            P("user", None),
            P("user", None),
            P(),
            P(None, "user", None),
            P(None, "user", None),
        ),
        out_specs=(P("user", None), P("user", None), P("user", None)),
        check_vma=False,
    )
```

```python
import functools
import math

import jax
import jax.numpy as jnp
from jax import lax
from jax.experimental import pallas as pl
from jax.experimental.pallas import tpu as pltpu
from jax.sharding import PartitionSpec as P

step_size = 0.01
prior_prec = 8.0
item_prec = 1.0
weight_decay = 1.0
rate_scale = 0.04

CORES = 2
CHUNKS = 2
RIDERS = 8
BASE_BY = 1
PULL_BY = 1
NN = (((1,), (0,)), ((), ()))
NT = (((1,), (1,)), ((), ()))
TN = (((0,), (0,)), ((), ()))
VMEM = pl.BlockSpec(memory_space=pltpu.VMEM)
SMEM = pl.BlockSpec(memory_space=pltpu.SMEM)
HBM = pl.BlockSpec(memory_space=pltpu.HBM)
ANY = pl.BlockSpec(memory_space=pl.ANY)
PARAMS = pltpu.CompilerParams(vmem_limit_bytes=8 << 20)
f32 = jnp.float32
bf16 = jnp.bfloat16


def dot(a, b, dims=NN):
    return lax.dot_general(a, b, dims, preferred_element_type=f32)


def shape(*dims, dtype=f32):
    return jax.ShapeDtypeStruct(dims, dtype)


def cost(flops, size):
    return pl.CostEstimate(flops=flops, bytes_accessed=size, transcendentals=0)


def where_am_i(devices, chunk=0):
    own = lax.axis_index("user")
    core = own & 1
    zero, one = (bit_order(devices, c, chunk) for c in range(CORES))
    bits = [jnp.where(core == 0, own >> z, own >> o) & 1 for z, o in zip(zero, one, strict=True)]
    return [core, *bits, own >> 1]


def rows_at(which, rows):
    start = which * rows
    return pl.ds(pl.multiple_of(start, rows) if rows % 8 == 0 else start, rows)


def half_of(ref, core):
    width = ref.shape[1] // CORES
    return ref[:, pl.ds(pl.multiple_of(core * width, width), width)]


def precision_of(stats):
    return (1.0 + stats[1:2, :] / 2.0) / (1.0 + stats[0:1, :] / 2.0)


def tile_kernel(stratum, noise_scale, devices, codes, count, ratings, user_noise, item_noise, *refs):
    if stratum == 0:
        users_in, items_in = refs[:2]
        base_u, grad_u, err_b, user_b, stats = refs[2:7]
        refs = refs[7:]
    else:
        old_base, old_grad, own_mean, other_mean, old_stats, old_base_v, old_grad_v = refs[:7]
        base_u, grad_u, err_b, user_b, stats, own_cols, other_cols, base_v = refs[8:16]
        refs = refs[16:]
    tiles, noise_u, noise_v, users, items, pred, sems = refs
    core = where_am_i(devices)[0]
    rows, rank = users.shape
    width = rank // CORES
    tile = tiles.shape[-1]
    grid = rows // tile
    copies = [
        pltpu.make_async_copy(source, target, sems.at[n])
        for n, (source, target) in enumerate(
            [
                (ratings.at[0, stratum], tiles),
                (user_noise.at[stratum], noise_u),
            ]
            + (
                [(users_in, users), (items_in, items)]
                if stratum == 0
                else [(item_noise.at[stratum], noise_v)]
            )
        )
    ]
    for copy in copies[::-1]:
        copy.start()
    if stratum == 0:
        copies[3].wait()
        copies[2].wait()
    else:
        precision = precision_of(old_stats[...])
        precision = jnp.concatenate([precision] * CORES, 1)
        items[...] = old_base_v[...] + precision * old_grad_v[...]
        new = old_base[...] + precision * old_grad[...]
        here = core == 0
        pull = step_size * prior_prec
        left = jnp.where(here, own_mean[...], other_mean[...])
        right = jnp.where(here, other_mean[...], own_mean[...])
        users[:, :width] = new[:, :width] + pull * left
        users[:, width:] = new[:, width:] + pull * right
        own_cols[...] = half_of(users, core)
        other_cols[...] = half_of(users, 1 - core)
    user_b[...] = users[...].astype(bf16)
    item_b = items[...].astype(bf16)
    pred[...] = dot(user_b[...], item_b, NT)
    err_b[...] = jnp.zeros_like(err_b)
    live_slots = count[0, stratum]
    sse = jnp.zeros((tile, tile), f32)
    copies[0].wait()
    for slot in range(tiles.shape[0]):
        code = codes[0, stratum, slot]
        at_rows = pl.ds(pl.multiple_of(code // grid * tile, tile), tile)
        at_cols = pl.ds(pl.multiple_of(code % grid * tile, tile), tile)
        live = (slot < live_slots).astype(f32)
        err = (tiles[slot].astype(f32) - pred[at_rows, at_cols]) * live
        sse = sse + err * err
        err_b[at_rows, at_cols] = err.astype(bf16)
    err_all = err_b[...]
    total = jnp.sum(sse)
    counted = live_slots.astype(f32) * float(tile * tile)
    row = lax.broadcasted_iota(jnp.int32, stats.shape, 0)
    stats[...] = jnp.where(row == 0, total, jnp.where(row == 1, counted, 0.0))
    grad_u[...] = step_size * dot(err_all, item_b)
    copies[1].wait()
    base_u[...] = (1.0 - step_size * prior_prec) * users[...] + noise_scale * noise_u[...].astype(
        f32
    )
    if stratum:
        copies[2].wait()
        base_v[...] = item_base(noise_scale, items, noise_v)


def item_base(noise_scale, items, noise):
    return (1.0 - step_size * item_prec) * items[...] + noise_scale * noise[...].astype(f32)


def base_kernel(noise_scale, items_in, noise_in, base, items, noise, sems):
    copies = [
        pltpu.make_async_copy(items_in, items, sems.at[0]),
        pltpu.make_async_copy(noise_in.at[0], noise, sems.at[1]),
    ]
    for copy in copies:
        copy.start()
    for copy in copies:
        copy.wait()
    base[...] = item_base(noise_scale, items, noise)


def base_pass(items, item_noise):
    return pl.pallas_call(
        functools.partial(base_kernel, math.sqrt(2.0 * step_size)),
        out_shape=shape(*items.shape),
        in_specs=[HBM] * 2,
        out_specs=VMEM,
        scratch_shapes=[
            pltpu.VMEM(items.shape, f32),
            pltpu.VMEM(items.shape, bf16),
            pltpu.SemaphoreType.DMA((2,)),
        ],
        compiler_params=PARAMS,
        cost_estimate=cost(2 * items.size, 10 * items.size),
        name="base_pass",
    )(items, item_noise)


def pull_kernel(err_b, user_b, *refs):
    refs[-1][...] = step_size * dot(err_b[...], user_b[...], TN)


def pull_pass(err_b, user_b, later):
    rows, rank = user_b.shape
    return pl.pallas_call(
        pull_kernel,
        out_shape=shape(rows, rank),
        in_specs=[VMEM] * 2 + [ANY] * len(later),
        out_specs=VMEM,
        compiler_params=PARAMS,
        cost_estimate=cost(2 * rows * rows * rank, 8 * rows * rank),
        name="pull_pass",
    )(err_b, user_b, *later)


def tile_pass(stratum, devices, codes, count, ratings, user_noise, item_noise, *state):
    slots, tile = ratings.shape[2:4]
    rows, rank = user_noise.shape[1:]
    noise_scale = math.sqrt(2.0 * step_size)
    width = rank // CORES
    outs = [
        shape(rows, rank),
        shape(rows, rank),
        shape(rows, rows, dtype=bf16),
        shape(rows, rank, dtype=bf16),
        shape(RIDERS, width),
    ]
    if stratum:
        outs += [shape(rows, width), shape(rows, width), shape(rows, rank)]
    return pl.pallas_call(
        functools.partial(tile_kernel, stratum, noise_scale, devices),
        out_shape=tuple(outs),
        in_specs=[SMEM] * 2 + [HBM] * 3 + ([VMEM] * 7 + [ANY] if stratum else [HBM] * 2),
        out_specs=(VMEM,) * len(outs),
        scratch_shapes=[
            pltpu.VMEM((slots, tile, tile), bf16),
            pltpu.VMEM((rows, rank), bf16),
            pltpu.VMEM((rows, rank), bf16),
            pltpu.VMEM((rows, rank), f32),
            pltpu.VMEM((rows, rank), f32),
            pltpu.VMEM((rows, rows), f32),
            pltpu.SemaphoreType.DMA((4,)),
        ],
        compiler_params=PARAMS,
        cost_estimate=cost(6 * rows * rows * rank, 16 * rows * rank),
        name="tile_pass",
    )(codes, count, ratings, user_noise, item_noise, *state)


def first_kernel(devices, feats_in, weights_in, users_in, own_mean, other_mean, *refs):
    sends, keeps, olds = refs[:CHUNKS], refs[CHUNKS : 2 * CHUNKS], refs[2 * CHUNKS : 3 * CHUNKS]
    mean, feats, weights, users, sems = refs[3 * CHUNKS :]
    copies = [
        pltpu.make_async_copy(source, target, sems.at[n])
        for n, (source, target) in enumerate(
            [(weights_in, weights), (feats_in, feats), (users_in, users)]
        )
    ]
    for copy in copies:
        copy.start()
    here = where_am_i(devices)[0]
    copies[0].wait()
    weights_b = weights[...].astype(bf16)
    copies[1].wait()
    mean[...] = dot(feats[...], weights_b)
    copies[2].wait()
    for grads, means, which in ((sends, other_mean, 1 - here), (keeps, own_mean, here)):
        mean_now = half_of(mean, which)
        means[...] = mean_now
        offset = (half_of(users, which) - mean_now).astype(bf16)
        for chunk, grad in enumerate(grads):
            depth = grad.shape[0]
            grad[...] = dot(feats[:, chunk * depth : (chunk + 1) * depth], offset, TN)
    for chunk, old in enumerate(olds):
        rows, width = old.shape
        _, first, second, *_ = where_am_i(devices, chunk)
        cols = pl.ds(pl.multiple_of(here * width, width), width)
        old[...] = weights[rows_at(chunk * 4 + first * 2 + second, rows), cols]


def first_pass(devices, feats, weights, users):
    rows, rank = users.shape
    feat = weights.shape[0]
    width = rank // CORES
    depth = feat // CHUNKS
    return pl.pallas_call(
        functools.partial(first_kernel, devices),
        out_shape=(shape(rows, width),) * 2
        + (shape(depth, width),) * (2 * CHUNKS)
        + (shape(depth // 4, width),) * CHUNKS,
        in_specs=[HBM] * 3,
        out_specs=(VMEM,) * (2 + 3 * CHUNKS),
        scratch_shapes=[
            pltpu.VMEM(users.shape, f32),
            pltpu.VMEM(feats.shape, bf16),
            pltpu.VMEM(weights.shape, f32),
            pltpu.VMEM(users.shape, f32),
            pltpu.SemaphoreType.DMA((3,)),
        ],
        compiler_params=PARAMS,
        cost_estimate=cost(4 * rows * feat * rank, 8 * feat * rank),
        name="first_pass",
    )(feats, weights, users)


def widen_kernel(narrow_in, wide, narrow, sem):
    copy = pltpu.make_async_copy(narrow_in, narrow, sem.at[0])
    copy.start()
    copy.wait()
    wide[...] = narrow[...].astype(f32)


def widen_pass(narrow):
    return pl.pallas_call(
        widen_kernel,
        out_shape=shape(*narrow.shape),
        in_specs=[HBM],
        out_specs=VMEM,
        scratch_shapes=[pltpu.VMEM(narrow.shape, bf16), pltpu.SemaphoreType.DMA((1,))],
        compiler_params=PARAMS,
        name="widen_pass",
    )(narrow)


def join_kernel(own, other, both, turned):
    rows = other.shape[0]
    both[:rows, :] = own[...]
    both[rows:, :] = other[...].astype(bf16)
    turned[:, :rows] = own[...].T
    turned[:, rows:] = other[...].T.astype(bf16)


def join_pass(own, other):
    rows, feat = own.shape
    return pl.pallas_call(
        join_kernel,
        out_shape=(shape(CORES * rows, feat, dtype=bf16), shape(feat, CORES * rows, dtype=bf16)),
        in_specs=[VMEM, VMEM],
        out_specs=(VMEM, VMEM),
        compiler_params=PARAMS,
        cost_estimate=cost(rows * feat, 12 * rows * feat),
        name="join_pass",
    )(own, other)


def halves_mean(feats, chunk, bit, part, got):
    half = part.shape[0]
    return dot(feats[:, rows_at(2 * chunk + bit, half)], part[...].astype(bf16)) + dot(
        feats[:, rows_at(2 * chunk + 1 - bit, half)], got[...].astype(bf16)
    )


def part_kernel(devices, feats, part, got, mean):
    mean[...] = halves_mean(feats, 0, where_am_i(devices)[1], part, got)


def part_pass(devices, feats, part, got):
    rows = feats.shape[0]
    half, width = part.shape
    return pl.pallas_call(
        functools.partial(part_kernel, devices),
        out_shape=shape(rows, width),
        in_specs=[VMEM] * 3,
        out_specs=VMEM,
        compiler_params=PARAMS,
        cost_estimate=cost(4 * rows * half * width, 4 * rows * half),
        name="part_pass",
    )(feats, part, got)


def find_offset(devices, feats, begun, part, got, own_cols, other_cols, own_mean, other_mean, offset):
    rows = own_cols.shape[0]
    mean = begun[...] + halves_mean(feats, 1, where_am_i(devices, 1)[1], part, got)
    own_mean[...] = mean[:rows]
    other_mean[...] = mean[rows:]
    offset[:rows, :] = (own_cols[...] - mean[:rows]).astype(bf16)
    offset[rows:, :] = (other_cols[...] - mean[rows:]).astype(bf16)


def prior_kernel(devices, feats, turned, begun, part, got, own_cols, other_cols, own_mean, other_mean, offset, send, keep):
    find_offset(devices, feats, begun, part, got, own_cols, other_cols, own_mean, other_mean, offset)
    bit = where_am_i(devices)[1]
    half = keep.shape[0]
    send[...] = dot(turned[rows_at(1 - bit, half), :], offset[...])
    keep[...] = dot(turned[rows_at(bit, half), :], offset[...])


def prior_pass(devices, feats, turned, begun, part, got, own_cols, other_cols):
    rows, width = own_cols.shape
    half = part.shape[0]
    return pl.pallas_call(
        functools.partial(prior_kernel, devices),
        out_shape=(shape(rows, width),) * 2
        + (shape(CORES * rows, width, dtype=bf16),)
        + (shape(half, width),) * 2,
        in_specs=[VMEM] * 7,
        out_specs=(VMEM,) * 5,
        compiler_params=PARAMS,
        cost_estimate=cost(16 * rows * half * width, 16 * rows * half),
        name="prior_pass",
    )(feats, turned, begun, part, got, own_cols, other_cols)


def rest_kernel(devices, turned, offset, stats, more_stats, send, keep):
    bit = where_am_i(devices, 1)[1]
    half = keep.shape[0]
    send[:half, :] = dot(turned[rows_at(2 + 1 - bit, half), :], offset[...])
    keep[...] = dot(turned[rows_at(2 + bit, half), :], offset[...])
    send[half:, :] = stats[...] + more_stats[...]


def rest_pass(devices, turned, offset, stats, more_stats):
    rows, width = offset.shape
    half = turned.shape[0] // (2 * CHUNKS)
    return pl.pallas_call(
        functools.partial(rest_kernel, devices),
        out_shape=(shape(half + RIDERS, width), shape(half, width)),
        in_specs=[VMEM] * 4,
        out_specs=(VMEM,) * 2,
        compiler_params=PARAMS,
        cost_estimate=cost(4 * rows * half * width, 4 * rows * half),
        name="rest_pass",
    )(turned, offset, stats, more_stats)


def final_kernel(places, devices, feats, turned, begun, part, got, first_part, first_got, own_cols, other_cols, stats, more_stats, own_mean, other_mean, send, keep, old, full, offset):
    find_offset(devices, feats, begun, part, got, own_cols, other_cols, own_mean, other_mean, offset)
    send[keep.shape[0] :, :] = stats[...] + more_stats[...]
    rows = part.shape[0]
    place = where_am_i(devices)
    for chunk, mine, theirs in ((0, first_part, first_got), (1, part, got)):
        bit = where_am_i(devices, chunk)[1]
        full[rows_at(2 * chunk + bit, rows), :] = mine[...]
        full[rows_at(2 * chunk + 1 - bit, rows), :] = theirs[...]
    old[...] = full[rows_at(place[-1], old.shape[0]), :]
    full[...] = dot(turned[...], offset[...])
    core, bit = place[0], place[1]
    blocks = len(places[0])
    block = full.shape[0] // blocks
    for ref, which in ((send, 1 - bit), (keep, bit)):
        for n in range(blocks // 2):
            source = jnp.int32(0)
            for c, order in enumerate(places):
                for b in range(2):
                    source = jnp.where((core == c) & (which == b), order[b * blocks // 2 + n], source)
            ref[n * block : (n + 1) * block, :] = full[rows_at(source, block), :]


def final_pass(places, devices, feats, turned, begun, part, got, first_part, first_got, own_cols, other_cols, stats, more_stats):
    rows, width = own_cols.shape
    feat = feats.shape[1]
    return pl.pallas_call(
        functools.partial(final_kernel, places, devices),
        out_shape=(shape(rows, width),) * 2
        + (shape(feat // 2 + RIDERS, width), shape(feat // 2, width), shape(feat // len(places[0]), width)),
        in_specs=[VMEM] * 11,
        out_specs=(VMEM,) * 5,
        scratch_shapes=[pltpu.VMEM((feat, width), f32), pltpu.VMEM((CORES * rows, width), bf16)],
        compiler_params=PARAMS,
        cost_estimate=cost(8 * rows * feat * width, 8 * rows * feat),
        name="final_pass",
    )(feats, turned, begun, part, got, first_part, first_got, own_cols, other_cols, stats, more_stats)


def step_kernel(halving, stage, chunk, riders, devices, held, got, *refs):
    send = refs[-2] if halving else refs[-1]
    rows = send.shape[0] - riders
    if halving:
        bit = where_am_i(devices, chunk)[1 + stage]
        for ref, which in ((send, 1 - bit), (refs[-1], bit)):
            at = rows_at(which, rows)
            ref[:rows, :] = held[at, :] + got[at, :]
    else:
        send[:rows, :] = held[:rows, :] + got[:rows, :]
    if riders:
        sent, more = refs[:2]
        send[rows:, :] = sent[sent.shape[0] - riders :, :] + more[more.shape[0] - riders :, :]


def step_pass(halving, stage, chunk, devices, held, got, rows, riders=(), later=()):
    width = held.shape[1]
    under = RIDERS if riders else 0
    outs = [shape(rows // 2 + under, width), shape(rows // 2, width)] if halving else [shape(rows + under, width)]
    return pl.pallas_call(
        functools.partial(step_kernel, halving, stage, chunk, under, devices),
        out_shape=tuple(outs),
        in_specs=[VMEM] * (2 + len(riders)) + [ANY] * len(later),
        out_specs=(VMEM,) * len(outs),
        compiler_params=PARAMS,
        cost_estimate=cost(rows * width, 12 * rows * width),
        name="step_pass",
    )(held, got, *riders, *later)


def update_kernel(rate, riding, held, got, old, *refs):
    rows = old.shape[0]
    new = refs[-2] if riding else refs[-1]
    total = held[:rows, :] + got[:rows, :]
    before = old[...]
    new[...] = before + rate * (prior_prec * total - weight_decay * before)
    if riding:
        refs[-1][...] = held_stats(refs[0]) + got[rows:, :]


def held_stats(sent):
    return sent[sent.shape[0] - RIDERS :, :]


def update_pass(rate, held, got, old, sent=None, later=()):
    riding = sent is not None
    out = shape(*old.shape)
    return pl.pallas_call(
        functools.partial(update_kernel, rate, riding),
        out_shape=(out, shape(RIDERS, old.shape[1])) if riding else out,
        in_specs=[VMEM] * (3 + riding) + [ANY] * len(later),
        out_specs=(VMEM,) * 2 if riding else VMEM,
        compiler_params=PARAMS,
        cost_estimate=cost(4 * old.size, 16 * old.size),
        name="update_pass",
    )(held, got, old, *([sent] if riding else []), *later)


def gather_kernel(stage, chunk, devices, part, got, *refs):
    both = refs[-1]
    rows = part.shape[0]
    bit = where_am_i(devices, chunk)[1 + stage]
    both[rows_at(bit, rows), :] = part[...]
    both[rows_at(1 - bit, rows), :] = got[...]


def gather_pass(stage, chunk, devices, part, got, later=()):
    rows, width = part.shape
    return pl.pallas_call(
        functools.partial(gather_kernel, stage, chunk, devices),
        out_shape=shape(2 * rows, width),
        in_specs=[VMEM, VMEM] + [ANY] * len(later),
        out_specs=VMEM,
        compiler_params=PARAMS,
        cost_estimate=cost(rows * width, 16 * rows * width),
        name="gather_pass",
    )(part, got, *later)


def split_kernel(devices, both, mine, other):
    place = where_am_i(devices)
    rows = mine.shape[0]
    for ref, which in ((mine, place[0]), (other, 1 - place[0])):
        at = pl.ds(pl.multiple_of(which * rows, 8), rows) if rows % 8 == 0 else pl.ds(which * rows, rows)
        ref[...] = both[at, :]


def split_pass(devices, both):
    rows, width = both.shape
    return pl.pallas_call(
        functools.partial(split_kernel, devices),
        out_shape=(shape(rows // CORES, width),) * 2,
        in_specs=[VMEM],
        out_specs=(VMEM,) * 2,
        compiler_params=PARAMS,
        name="split_pass",
    )(both)


def across_kernel(devices, mine, other, both):
    place = where_am_i(devices)
    width = mine.shape[1]
    both[:, pl.ds(pl.multiple_of(place[0] * width, width), width)] = mine[...]
    both[:, pl.ds(pl.multiple_of((1 - place[0]) * width, width), width)] = other[...]


def across_pass(devices, mine, other):
    rows, width = mine.shape
    return pl.pallas_call(
        functools.partial(across_kernel, devices),
        out_shape=shape(rows, CORES * width),
        in_specs=[VMEM, VMEM],
        out_specs=VMEM,
        compiler_params=PARAMS,
        name="across_pass",
    )(mine, other)


def last_kernel(devices, stats, base, grad, own_mean, other_mean, base_v, grad_v, users, items):
    place = where_am_i(devices)
    width = own_mean.shape[1]
    precision = precision_of(stats[...])
    precision = jnp.concatenate([precision] * CORES, 1)
    items[...] = base_v[...] + precision * grad_v[...]
    users[...] = base[...] + precision * grad[...]
    pull = step_size * prior_prec
    for mean, which in ((own_mean, place[0]), (other_mean, 1 - place[0])):
        at = pl.ds(pl.multiple_of(which * width, width), width)
        users[:, at] = users[:, at] + pull * mean[...]


def last_pass(devices, stats, base, *state):
    return pl.pallas_call(
        functools.partial(last_kernel, devices),
        out_shape=(shape(*base.shape),) * 2,
        in_specs=[VMEM] * 7,
        out_specs=(VMEM,) * 2,
        compiler_params=PARAMS,
        cost_estimate=cost(8 * base.size, 32 * base.size),
        name="last_pass",
    )(stats, base, *state)


def bit_order(devices, core, chunk=0):
    bits = devices.bit_length() - 1
    near = [1, 2] if core == chunk else [2, 1]
    far = list(range(3, bits))
    return near + (far if chunk == 0 else far[::-1])


def swap(array, devices):
    return lax.ppermute(array, "user", [(i, i ^ 1) for i in range(devices)])


def roll(array, devices):
    return lax.ppermute(array, "user", [(i, (i + 1) % devices) for i in range(devices)])


def exchange(array, devices, stage, chunk=0):
    orders = [bit_order(devices, core, chunk) for core in range(CORES)]
    pairs = [(i, i ^ (1 << orders[i & 1][stage])) for i in range(devices)]
    return lax.ppermute(array, "user", pairs)


def final_places(devices):
    bits = devices.bit_length() - 1
    return [
        [
            sum(
                ((place >> (bits - 2 - n)) & 1) << (bit - 1)
                for n, bit in enumerate(bit_order(devices, core))
            )
            for place in range(devices // 2)
        ]
        for core in range(CORES)
    ]


def local(
    ratings,
    tile_index,
    tile_count,
    side_features,
    user_factors,
    item_factors,
    prior_weights,
    user_noise,
    item_noise,
):
    devices = lax.axis_size("user")
    stages = devices.bit_length() - 2
    strata = ratings.shape[1]
    feat = prior_weights.shape[0]
    rate = rate_scale / (user_factors.shape[0] * devices)
    tables = (devices, tile_index, tile_count, ratings, user_noise, item_noise)

    both = range(CHUNKS)
    depth = feat // CHUNKS
    base_v = base_pass(item_factors, item_noise)
    own_mean, other_mean, *outs = first_pass(
        devices, side_features, prior_weights, user_factors
    )
    helds, olds = outs[CHUNKS : 2 * CHUNKS], outs[2 * CHUNKS :]
    gots = [swap(send, devices) for send in outs[:CHUNKS]]
    base, grad, err_b, user_b, stats = tile_pass(0, *tables, user_factors, item_factors)
    more = swap(stats, devices)
    sends = [None] * CHUNKS
    for c in both:
        riders = (stats, more) if c else ()
        sends[c], helds[c] = step_pass(True, 0, c, devices, helds[c], gots[c], depth, riders)
    feats, turned = join_pass(side_features, swap(widen_pass(side_features), devices))
    for stratum in range(strata - 1):
        base_v = roll(base_v, devices)
        for stage in range(stages - 1):
            for c in (1, 0):
                gots[c] = exchange(sends[c], devices, stage, c)
                riders = (sends[c], gots[c]) if c else ()
                rows = gots[c].shape[0] - RIDERS * c
                later = [] if c else [sends[1]] + ([base_v] if stage == BASE_BY else [])
                if stage < 1:
                    sends[c], helds[c] = step_pass(
                        True, stage + 1, c, devices, helds[c], gots[c], rows, riders, later
                    )
                else:
                    (sends[c],) = step_pass(False, 0, c, devices, helds[c], gots[c], rows, riders, later)
                    helds[c] = sends[c]
            if stage == PULL_BY:
                grad_v = roll(pull_pass(err_b, user_b, sends[:1]), devices)
        for c in (1, 0):
            gots[c] = exchange(sends[c], devices, stages - 1, c)
            if c:
                olds[c], stats = update_pass(rate, helds[c], gots[c], olds[c], sends[c])
            else:
                olds[c] = update_pass(rate, helds[c], gots[c], olds[c], None, olds[1:])
        parts = list(olds)
        for c in (1, 0):
            got = exchange(parts[c], devices, 1, c)
            parts[c] = gather_pass(1, c, devices, parts[c], got, [] if c else parts[1:])
        gots = [exchange(parts[c], devices, 0, c) for c in both]
        base, grad, err_b, user_b, stats, own_cols, other_cols, base_v = tile_pass(
            stratum + 1, *tables, base, grad, own_mean, other_mean, stats, base_v, grad_v, olds[0]
        )
        more = swap(stats, devices)
        other_cols = swap(other_cols, devices)
        begun = part_pass(devices, feats, parts[0], gots[0])
        if stratum + 2 < strata:
            own_mean, other_mean, offset, sends[0], helds[0] = prior_pass(
                devices, feats, turned, begun, parts[1], gots[1], own_cols, other_cols
            )
            sends[1], helds[1] = rest_pass(devices, turned, offset, stats, more)
        else:
            own_mean, other_mean, send, held, old = final_pass(
                final_places(devices),
                devices,
                feats,
                turned,
                begun,
                parts[1],
                gots[1],
                parts[0],
                gots[0],
                own_cols,
                other_cols,
                stats,
                more,
            )
        other_mean = swap(other_mean, devices)
    for stage in range(stages - 1):
        got = exchange(send, devices, stage)
        send, held = step_pass(True, stage + 1, 0, devices, held, got, got.shape[0] - RIDERS, (send, got))
    got = exchange(send, devices, stages - 1)
    part, stats = update_pass(rate, held, got, old, send)
    mine, other = split_pass(devices, part)
    got = swap(other, devices)
    grad_v = pull_pass(err_b, user_b, [part])
    users, items = last_pass(devices, stats, base, grad, own_mean, other_mean, base_v, grad_v)
    return (users, items, across_pass(devices, mine, got))


def solution(mesh):
    return jax.shard_map(
        local,
        mesh=mesh,
        in_specs=(
            P("user", None, None, None, None),
            P("user", None, None),
            P("user", None),
            P("user", None),
            P("user", None),
            P("user", None),
            P(),
            P(None, "user", None),
            P(None, "user", None),
        ),
        out_specs=(P("user", None), P("user", None), P("user", None)),
        check_vma=False,
    )
```

```python
import functools
import math

import jax
import jax.numpy as jnp
from jax import lax
from jax.experimental import pallas as pl
from jax.experimental.pallas import tpu as pltpu
from jax.sharding import PartitionSpec as P

step_size = 0.01
prior_prec = 8.0
item_prec = 1.0
weight_decay = 1.0
rate_scale = 0.04

CORES = 2
CHUNKS = 2
RIDERS = 8
NN = (((1,), (0,)), ((), ()))
NT = (((1,), (1,)), ((), ()))
TN = (((0,), (0,)), ((), ()))
VMEM = pl.BlockSpec(memory_space=pltpu.VMEM)
SMEM = pl.BlockSpec(memory_space=pltpu.SMEM)
HBM = pl.BlockSpec(memory_space=pltpu.HBM)
ANY = pl.BlockSpec(memory_space=pl.ANY)
PARAMS = pltpu.CompilerParams(vmem_limit_bytes=8 << 20)
f32 = jnp.float32
bf16 = jnp.bfloat16


def dot(a, b, dims=NN):
    return lax.dot_general(a, b, dims, preferred_element_type=f32)


def shape(*dims, dtype=f32):
    return jax.ShapeDtypeStruct(dims, dtype)


def cost(flops, size):
    return pl.CostEstimate(flops=flops, bytes_accessed=size, transcendentals=0)


def where_am_i(devices, chunk=0):
    own = lax.axis_index("user")
    core = own & 1
    zero, one = (bit_order(devices, c, chunk) for c in range(CORES))
    bits = [jnp.where(core == 0, own >> z, own >> o) & 1 for z, o in zip(zero, one, strict=True)]
    return [core, *bits, own >> 1]


def rows_at(which, rows):
    start = which * rows
    return pl.ds(pl.multiple_of(start, rows) if rows % 8 == 0 else start, rows)


def half_of(ref, core):
    width = ref.shape[1] // CORES
    return ref[:, pl.ds(pl.multiple_of(core * width, width), width)]


def precision_of(stats):
    return (1.0 + stats[1:2, :] / 2.0) / (1.0 + stats[0:1, :] / 2.0)


def tile_kernel(stratum, noise_scale, codes, count, ratings, user_noise, item_noise, *refs):
    users_in, items_in, base_u, grad_u, base_v, grad_v, stats = refs[:7]
    tiles, noise_u, noise_v, pred, err_b, sems = refs[7:13]
    rows = err_b.shape[0]
    tile = tiles.shape[-1]
    grid = rows // tile
    moves = [
        (ratings.at[0, stratum], tiles),
        (user_noise.at[stratum], noise_u),
        (item_noise.at[stratum], noise_v),
    ]
    users, items = users_in, items_in
    if stratum == 0:
        users, items = refs[13:]
        moves += [(users_in, users), (items_in, items)]
    copies = [
        pltpu.make_async_copy(source, target, sems.at[n]) for n, (source, target) in enumerate(moves)
    ]
    for copy in copies[::-1]:
        copy.start()
    for copy in copies[3:]:
        copy.wait()
    user_b = users[...].astype(bf16)
    item_b = items[...].astype(bf16)
    pred[...] = dot(user_b, item_b, NT)
    err_b[...] = jnp.zeros_like(err_b)
    live_slots = count[0, stratum]
    sse = jnp.zeros((tile, tile), f32)
    copies[0].wait()
    for slot in range(tiles.shape[0]):
        code = codes[0, stratum, slot]
        at_rows = rows_at(code // grid, tile)
        at_cols = rows_at(code % grid, tile)
        live = (slot < live_slots).astype(f32)
        err = (tiles[slot].astype(f32) - pred[at_rows, at_cols]) * live
        sse = sse + err * err
        err_b[at_rows, at_cols] = err.astype(bf16)
    err_all = err_b[...]
    total = jnp.sum(sse)
    counted = live_slots.astype(f32) * float(tile * tile)
    row = lax.broadcasted_iota(jnp.int32, stats.shape, 0)
    stats[...] = jnp.where(row == 0, total, jnp.where(row == 1, counted, 0.0))
    grad_u[...] = step_size * dot(err_all, item_b)
    grad_v[...] = step_size * dot(err_all, user_b, TN)
    copies[1].wait()
    base_u[...] = (1.0 - step_size * prior_prec) * users[...] + noise_scale * noise_u[...].astype(
        f32
    )
    copies[2].wait()
    base_v[...] = (1.0 - step_size * item_prec) * items[...] + noise_scale * noise_v[...].astype(f32)


def tile_pass(stratum, codes, count, ratings, user_noise, item_noise, users, items):
    slots, tile = ratings.shape[2:4]
    rows, rank = users.shape
    first = stratum == 0
    return pl.pallas_call(
        functools.partial(tile_kernel, stratum, math.sqrt(2.0 * step_size)),
        out_shape=(shape(rows, rank),) * 4 + (shape(RIDERS, rank // CORES),),
        in_specs=[SMEM] * 2 + [HBM] * 3 + [HBM if first else VMEM] * 2,
        out_specs=(VMEM,) * 5,
        scratch_shapes=[
            pltpu.VMEM((slots, tile, tile), bf16),
            pltpu.VMEM((rows, rank), bf16),
            pltpu.VMEM((rows, rank), bf16),
            pltpu.VMEM((rows, rows), f32),
            pltpu.VMEM((rows, rows), bf16),
            pltpu.SemaphoreType.DMA((5,)),
        ]
        + [pltpu.VMEM((rows, rank), f32)] * (2 if first else 0),
        compiler_params=PARAMS,
        cost_estimate=cost(6 * rows * rows * rank, 16 * rows * rank),
        name="tile_pass",
    )(codes, count, ratings, user_noise, item_noise, users, items)


def first_kernel(devices, feats_in, weights_in, users_in, own_mean, other_mean, *refs):
    sends, keeps, olds = refs[:CHUNKS], refs[CHUNKS : 2 * CHUNKS], refs[2 * CHUNKS : 3 * CHUNKS]
    mean, feats, weights, users, sems = refs[3 * CHUNKS :]
    copies = [
        pltpu.make_async_copy(source, target, sems.at[n])
        for n, (source, target) in enumerate(
            [(weights_in, weights), (feats_in, feats), (users_in, users)]
        )
    ]
    for copy in copies:
        copy.start()
    here = where_am_i(devices)[0]
    copies[0].wait()
    weights_b = weights[...].astype(bf16)
    copies[1].wait()
    mean[...] = dot(feats[...], weights_b)
    copies[2].wait()
    for grads, means, which in ((sends, other_mean, 1 - here), (keeps, own_mean, here)):
        mean_now = half_of(mean, which)
        means[...] = mean_now
        offset = (half_of(users, which) - mean_now).astype(bf16)
        for chunk, grad in enumerate(grads):
            depth = grad.shape[0]
            grad[...] = dot(feats[:, chunk * depth : (chunk + 1) * depth], offset, TN)
    for chunk, old in enumerate(olds):
        rows, width = old.shape
        _, first, second, *_ = where_am_i(devices, chunk)
        cols = pl.ds(pl.multiple_of(here * width, width), width)
        old[...] = weights[rows_at(chunk * 4 + first * 2 + second, rows), cols]


def first_pass(devices, feats, weights, users):
    rows, rank = users.shape
    feat = weights.shape[0]
    width = rank // CORES
    depth = feat // CHUNKS
    return pl.pallas_call(
        functools.partial(first_kernel, devices),
        out_shape=(shape(rows, width),) * 2
        + (shape(depth, width),) * (2 * CHUNKS)
        + (shape(depth // 4, width),) * CHUNKS,
        in_specs=[HBM] * 3,
        out_specs=(VMEM,) * (2 + 3 * CHUNKS),
        scratch_shapes=[
            pltpu.VMEM(users.shape, f32),
            pltpu.VMEM(feats.shape, bf16),
            pltpu.VMEM(weights.shape, f32),
            pltpu.VMEM(users.shape, f32),
            pltpu.SemaphoreType.DMA((3,)),
        ],
        compiler_params=PARAMS,
        cost_estimate=cost(4 * rows * feat * rank, 8 * feat * rank),
        name="first_pass",
    )(feats, weights, users)


def widen_kernel(narrow_in, wide, narrow, sem):
    copy = pltpu.make_async_copy(narrow_in, narrow, sem.at[0])
    copy.start()
    copy.wait()
    wide[...] = narrow[...].astype(f32)


def widen_pass(narrow):
    return pl.pallas_call(
        widen_kernel,
        out_shape=shape(*narrow.shape),
        in_specs=[HBM],
        out_specs=VMEM,
        scratch_shapes=[pltpu.VMEM(narrow.shape, bf16), pltpu.SemaphoreType.DMA((1,))],
        compiler_params=PARAMS,
        name="widen_pass",
    )(narrow)


def join_kernel(own, other, both, turned):
    rows = other.shape[0]
    both[:rows, :] = own[...]
    both[rows:, :] = other[...].astype(bf16)
    turned[:, :rows] = own[...].T
    turned[:, rows:] = other[...].T.astype(bf16)


def join_pass(own, other):
    rows, feat = own.shape
    return pl.pallas_call(
        join_kernel,
        out_shape=(shape(CORES * rows, feat, dtype=bf16), shape(feat, CORES * rows, dtype=bf16)),
        in_specs=[VMEM, VMEM],
        out_specs=(VMEM, VMEM),
        compiler_params=PARAMS,
        cost_estimate=cost(rows * feat, 12 * rows * feat),
        name="join_pass",
    )(own, other)


def halves_mean(feats, chunk, bit, part, got):
    half = part.shape[0]
    return dot(feats[:, rows_at(2 * chunk + bit, half)], part[...].astype(bf16)) + dot(
        feats[:, rows_at(2 * chunk + 1 - bit, half)], got[...].astype(bf16)
    )


def part_kernel(devices, feats, part, got, mean):
    mean[...] = halves_mean(feats, 0, where_am_i(devices)[1], part, got)


def part_pass(devices, feats, part, got):
    rows = feats.shape[0]
    half, width = part.shape
    return pl.pallas_call(
        functools.partial(part_kernel, devices),
        out_shape=shape(rows, width),
        in_specs=[VMEM] * 3,
        out_specs=VMEM,
        compiler_params=PARAMS,
        cost_estimate=cost(4 * rows * half * width, 4 * rows * half),
        name="part_pass",
    )(feats, part, got)


def find_offset(devices, feats, begun, part, got, own_cols, other_cols, own_mean, other_mean, offset):
    rows = own_cols.shape[0]
    mean = begun[...] + halves_mean(feats, 1, where_am_i(devices, 1)[1], part, got)
    own_mean[...] = mean[:rows]
    other_mean[...] = mean[rows:]
    offset[:rows, :] = (own_cols[...] - mean[:rows]).astype(bf16)
    offset[rows:, :] = (other_cols[...] - mean[rows:]).astype(bf16)


def prior_kernel(devices, feats, turned, begun, part, got, own_cols, other_cols, own_mean, other_mean, offset, send, keep):
    find_offset(devices, feats, begun, part, got, own_cols, other_cols, own_mean, other_mean, offset)
    bit = where_am_i(devices)[1]
    half = keep.shape[0]
    send[...] = dot(turned[rows_at(1 - bit, half), :], offset[...])
    keep[...] = dot(turned[rows_at(bit, half), :], offset[...])


def prior_pass(devices, feats, turned, begun, part, got, own_cols, other_cols):
    rows, width = own_cols.shape
    half = part.shape[0]
    return pl.pallas_call(
        functools.partial(prior_kernel, devices),
        out_shape=(shape(rows, width),) * 2
        + (shape(CORES * rows, width, dtype=bf16),)
        + (shape(half, width),) * 2,
        in_specs=[VMEM] * 7,
        out_specs=(VMEM,) * 5,
        compiler_params=PARAMS,
        cost_estimate=cost(16 * rows * half * width, 16 * rows * half),
        name="prior_pass",
    )(feats, turned, begun, part, got, own_cols, other_cols)


def rest_kernel(devices, turned, offset, stats, more_stats, send, keep):
    bit = where_am_i(devices, 1)[1]
    half = keep.shape[0]
    send[:half, :] = dot(turned[rows_at(2 + 1 - bit, half), :], offset[...])
    keep[...] = dot(turned[rows_at(2 + bit, half), :], offset[...])
    send[half:, :] = stats[...] + more_stats[...]


def rest_pass(devices, turned, offset, stats, more_stats):
    rows, width = offset.shape
    half = turned.shape[0] // (2 * CHUNKS)
    return pl.pallas_call(
        functools.partial(rest_kernel, devices),
        out_shape=(shape(half + RIDERS, width), shape(half, width)),
        in_specs=[VMEM] * 4,
        out_specs=(VMEM,) * 2,
        compiler_params=PARAMS,
        cost_estimate=cost(4 * rows * half * width, 4 * rows * half),
        name="rest_pass",
    )(turned, offset, stats, more_stats)


def final_kernel(places, devices, feats, turned, begun, part, got, first_part, first_got, own_cols, other_cols, stats, more_stats, own_mean, other_mean, *refs):
    sends, keeps, olds = refs[:CHUNKS], refs[CHUNKS : 2 * CHUNKS], refs[2 * CHUNKS : 3 * CHUNKS]
    full, offset = refs[3 * CHUNKS :]
    find_offset(devices, feats, begun, part, got, own_cols, other_cols, own_mean, other_mean, offset)
    sends[-1][keeps[-1].shape[0] :, :] = stats[...] + more_stats[...]
    rows = part.shape[0]
    for chunk, mine, theirs in ((0, first_part, first_got), (1, part, got)):
        bit = where_am_i(devices, chunk)[1]
        full[rows_at(2 * chunk + bit, rows), :] = mine[...]
        full[rows_at(2 * chunk + 1 - bit, rows), :] = theirs[...]
    core, *_, chip = where_am_i(devices)
    for chunk, old in enumerate(olds):
        old[...] = full[rows_at(CHUNKS * chip + chunk, old.shape[0]), :]
    full[...] = dot(turned[...], offset[...])
    for chunk, (send, keep) in enumerate(zip(sends, keeps, strict=True)):
        bit = where_am_i(devices, chunk)[1]
        zero, one = places[chunk]
        blocks = len(zero) // 2
        block = keep.shape[0] // blocks
        for ref, which in ((send, 1 - bit), (keep, bit)):
            for n in range(blocks):
                source = jnp.where(
                    core == 0,
                    jnp.where(which == 0, zero[n], zero[blocks + n]),
                    jnp.where(which == 0, one[n], one[blocks + n]),
                )
                ref[n * block : (n + 1) * block, :] = full[rows_at(source, block), :]


def final_pass(places, devices, feats, turned, begun, part, got, first_part, first_got, own_cols, other_cols, stats, more_stats):
    rows, width = own_cols.shape
    feat = feats.shape[1]
    quarter = feat // (2 * CHUNKS)
    return pl.pallas_call(
        functools.partial(final_kernel, places, devices),
        out_shape=(shape(rows, width),) * 2
        + (shape(quarter, width), shape(quarter + RIDERS, width))
        + (shape(quarter, width),) * CHUNKS
        + (shape(feat // devices, width),) * CHUNKS,
        in_specs=[VMEM] * 11,
        out_specs=(VMEM,) * (2 + 3 * CHUNKS),
        scratch_shapes=[pltpu.VMEM((feat, width), f32), pltpu.VMEM((CORES * rows, width), bf16)],
        compiler_params=PARAMS,
        cost_estimate=cost(8 * rows * feat * width, 8 * rows * feat),
        name="final_pass",
    )(feats, turned, begun, part, got, first_part, first_got, own_cols, other_cols, stats, more_stats)


def step_kernel(halving, stage, chunk, riders, devices, held, got, *refs):
    send = refs[-2] if halving else refs[-1]
    rows = send.shape[0] - riders
    if halving:
        bit = where_am_i(devices, chunk)[1 + stage]
        for ref, which in ((send, 1 - bit), (refs[-1], bit)):
            at = rows_at(which, rows)
            ref[:rows, :] = held[at, :] + got[at, :]
    else:
        send[:rows, :] = held[:rows, :] + got[:rows, :]
    if riders:
        sent, more = refs[:2]
        send[rows:, :] = sent[sent.shape[0] - riders :, :] + more[more.shape[0] - riders :, :]


def step_pass(halving, stage, chunk, devices, held, got, rows, riders=(), later=()):
    width = held.shape[1]
    under = RIDERS if riders else 0
    outs = [shape(rows // 2 + under, width), shape(rows // 2, width)] if halving else [shape(rows + under, width)]
    return pl.pallas_call(
        functools.partial(step_kernel, halving, stage, chunk, under, devices),
        out_shape=tuple(outs),
        in_specs=[VMEM] * (2 + len(riders)) + [ANY] * len(later),
        out_specs=(VMEM,) * len(outs),
        compiler_params=PARAMS,
        cost_estimate=cost(rows * width, 12 * rows * width),
        name="step_pass",
    )(held, got, *riders, *later)


def update_kernel(rate, riding, held, got, old, *refs):
    rows = old.shape[0]
    new = refs[-2] if riding else refs[-1]
    total = held[:rows, :] + got[:rows, :]
    before = old[...]
    new[...] = before + rate * (prior_prec * total - weight_decay * before)
    if riding:
        refs[-1][...] = held_stats(refs[0]) + got[rows:, :]


def held_stats(sent):
    return sent[sent.shape[0] - RIDERS :, :]


def update_pass(rate, held, got, old, sent=None, later=()):
    riding = sent is not None
    out = shape(*old.shape)
    return pl.pallas_call(
        functools.partial(update_kernel, rate, riding),
        out_shape=(out, shape(RIDERS, old.shape[1])) if riding else out,
        in_specs=[VMEM] * (3 + riding) + [ANY] * len(later),
        out_specs=(VMEM,) * 2 if riding else VMEM,
        compiler_params=PARAMS,
        cost_estimate=cost(4 * old.size, 16 * old.size),
        name="update_pass",
    )(held, got, old, *([sent] if riding else []), *later)


def gather_kernel(stage, chunk, devices, part, got, *refs):
    both = refs[-1]
    rows = part.shape[0]
    bit = where_am_i(devices, chunk)[1 + stage]
    both[rows_at(bit, rows), :] = part[...]
    both[rows_at(1 - bit, rows), :] = got[...]


def gather_pass(stage, chunk, devices, part, got, later=()):
    rows, width = part.shape
    return pl.pallas_call(
        functools.partial(gather_kernel, stage, chunk, devices),
        out_shape=shape(2 * rows, width),
        in_specs=[VMEM, VMEM] + [ANY] * len(later),
        out_specs=VMEM,
        compiler_params=PARAMS,
        cost_estimate=cost(rows * width, 16 * rows * width),
        name="gather_pass",
    )(part, got, *later)


def split_kernel(devices, first, second, mine, other):
    core = where_am_i(devices)[0]
    mine[...] = jnp.where(core == 0, first[...], second[...])
    other[...] = jnp.where(core == 0, second[...], first[...])


def split_pass(devices, first, second):
    return pl.pallas_call(
        functools.partial(split_kernel, devices),
        out_shape=(shape(*first.shape),) * 2,
        in_specs=[VMEM, VMEM],
        out_specs=(VMEM,) * 2,
        compiler_params=PARAMS,
        name="split_pass",
    )(first, second)


def across_kernel(devices, mine, other, both):
    core = where_am_i(devices)[0]
    width = mine.shape[1]
    both[:, rows_at(core, width)] = mine[...]
    both[:, rows_at(1 - core, width)] = other[...]


def across_pass(devices, mine, other):
    rows, width = mine.shape
    return pl.pallas_call(
        functools.partial(across_kernel, devices),
        out_shape=shape(rows, CORES * width),
        in_specs=[VMEM, VMEM],
        out_specs=VMEM,
        compiler_params=PARAMS,
        name="across_pass",
    )(mine, other)


def renew_kernel(devices, stats, base_u, grad_u, own_mean, other_mean, base_v, grad_v, users, items, *cols):
    core = where_am_i(devices)[0]
    width = own_mean.shape[1]
    precision = precision_of(stats[...])
    precision = jnp.concatenate([precision] * CORES, 1)
    items[...] = base_v[...] + precision * grad_v[...]
    new = base_u[...] + precision * grad_u[...]
    pull = step_size * prior_prec
    left = jnp.where(core == 0, own_mean[...], other_mean[...])
    right = jnp.where(core == 0, other_mean[...], own_mean[...])
    users[:, :width] = new[:, :width] + pull * left
    users[:, width:] = new[:, width:] + pull * right
    for ref, which in zip(cols, (core, 1 - core), strict=False):
        ref[...] = half_of(users, which)


def renew_pass(devices, last, stats, base_u, grad_u, own_mean, *state):
    outs = [shape(*base_u.shape)] * 2 + ([] if last else [shape(*own_mean.shape)] * 2)
    return pl.pallas_call(
        functools.partial(renew_kernel, devices),
        out_shape=tuple(outs),
        in_specs=[VMEM] * 7,
        out_specs=(VMEM,) * len(outs),
        compiler_params=PARAMS,
        cost_estimate=cost(8 * base_u.size, 32 * base_u.size),
        name="renew_pass",
    )(stats, base_u, grad_u, own_mean, *state)


def bit_order(devices, core, chunk=0):
    bits = devices.bit_length() - 1
    near = [1, 2] if core == chunk else [2, 1]
    far = list(range(3, bits))
    return near + (far if chunk == 0 else far[::-1])


def swap(array, devices):
    return lax.ppermute(array, "user", [(i, i ^ 1) for i in range(devices)])


def roll(array, devices):
    return lax.ppermute(array, "user", [(i, (i + 1) % devices) for i in range(devices)])


def exchange(array, devices, stage, chunk=0):
    orders = [bit_order(devices, core, chunk) for core in range(CORES)]
    pairs = [(i, i ^ (1 << orders[i & 1][stage])) for i in range(devices)]
    return lax.ppermute(array, "user", pairs)


def final_places(devices, chunk):
    bits = devices.bit_length() - 1
    return [
        [
            chunk
            | sum(
                ((place >> (bits - 2 - n)) & 1) << bit
                for n, bit in enumerate(bit_order(devices, core, chunk))
            )
            for place in range(devices // 2)
        ]
        for core in range(CORES)
    ]


def local(
    ratings,
    tile_index,
    tile_count,
    side_features,
    user_factors,
    item_factors,
    prior_weights,
    user_noise,
    item_noise,
):
    devices = lax.axis_size("user")
    stages = devices.bit_length() - 2
    strata = ratings.shape[1]
    feat = prior_weights.shape[0]
    rate = rate_scale / (user_factors.shape[0] * devices)
    tables = (tile_index, tile_count, ratings, user_noise, item_noise)
    both = range(CHUNKS)
    depth = feat // CHUNKS

    def stage_of(stage, sends, helds, halving):
        for c in (1, 0):
            got = exchange(sends[c], devices, stage, c)
            riders = (sends[c], got) if c else ()
            rows = got.shape[0] - RIDERS * c
            later = [sends[1 - c]]
            outs = step_pass(halving, stage + 1, c, devices, helds[c], got, rows, riders, later)
            sends[c], helds[c] = outs if halving else outs * 2

    def update_of(sends, helds, olds):
        news = list(olds)
        for c in (1, 0):
            got = exchange(sends[c], devices, stages - 1, c)
            if c:
                news[c], stats = update_pass(rate, helds[c], got, olds[c], sends[c], sends[:1])
            else:
                news[c] = update_pass(rate, helds[c], got, olds[c], None, news[1:])
        return news, stats

    own_mean, other_mean, *outs = first_pass(
        devices, side_features, prior_weights, user_factors
    )
    keeps, olds = outs[CHUNKS : 2 * CHUNKS], outs[2 * CHUNKS :]
    gots = [swap(send, devices) for send in outs[:CHUNKS]]
    *state, stats = tile_pass(0, *tables, user_factors, item_factors)
    more = swap(stats, devices)
    sends, helds = [None] * CHUNKS, [None] * CHUNKS
    for c in (1, 0):
        riders = (stats, more) if c else ()
        later = [] if c else [sends[1]]
        sends[c], helds[c] = step_pass(True, 0, c, devices, keeps[c], gots[c], depth, riders, later)
    feats, turned = join_pass(side_features, swap(widen_pass(side_features), devices))
    for stratum in range(strata - 1):
        for stage in range(stages - 1):
            stage_of(stage, sends, helds, stage < 1)
        olds, stats = update_of(sends, helds, olds)
        users, items, own_cols, other_cols = renew_pass(
            devices, False, stats, *state[:2], own_mean, other_mean, *state[2:]
        )
        items = roll(items, devices)
        other_cols = swap(other_cols, devices)
        parts = list(olds)
        for c in (1, 0):
            got = exchange(parts[c], devices, 1, c)
            parts[c] = gather_pass(1, c, devices, parts[c], got, [parts[1 - c]])
        gots = [exchange(parts[c], devices, 0, c) for c in both]
        *state, stats = tile_pass(stratum + 1, *tables, users, items)
        more = swap(stats, devices)
        begun = part_pass(devices, feats, parts[0], gots[0])
        if stratum + 2 < strata:
            own_mean, other_mean, offset, sends[0], helds[0] = prior_pass(
                devices, feats, turned, begun, parts[1], gots[1], own_cols, other_cols
            )
            sends[1], helds[1] = rest_pass(devices, turned, offset, stats, more)
        else:
            own_mean, other_mean, *outs = final_pass(
                [final_places(devices, c) for c in both],
                devices,
                feats,
                turned,
                begun,
                parts[1],
                gots[1],
                parts[0],
                gots[0],
                own_cols,
                other_cols,
                stats,
                more,
            )
            sends, helds, olds = outs[:CHUNKS], outs[CHUNKS : 2 * CHUNKS], outs[2 * CHUNKS :]
        other_mean = swap(other_mean, devices)
    for stage in range(stages - 1):
        stage_of(stage, sends, helds, True)
    news, stats = update_of(sends, helds, olds)
    mine, other = split_pass(devices, *news)
    got = swap(other, devices)
    users, items = renew_pass(devices, True, stats, *state[:2], own_mean, other_mean, *state[2:])
    return (users, items, across_pass(devices, mine, got))


def solution(mesh):
    return jax.shard_map(
        local,
        mesh=mesh,
        in_specs=(
            P("user", None, None, None, None),
            P("user", None, None),
            P("user", None),
            P("user", None),
            P("user", None),
            P("user", None),
            P(),
            P(None, "user", None),
            P(None, "user", None),
        ),
        out_specs=(P("user", None), P("user", None), P("user", None)),
        check_vma=False,
    )
```

```python
import functools
import math

import jax
import jax.numpy as jnp
from jax import lax
from jax.experimental import pallas as pl
from jax.experimental.pallas import tpu as pltpu
from jax.sharding import PartitionSpec as P

step_size = 0.01
prior_prec = 8.0
item_prec = 1.0
weight_decay = 1.0
rate_scale = 0.04

CORES = 2
RIDERS = 8
NN = (((1,), (0,)), ((), ()))
NT = (((1,), (1,)), ((), ()))
TN = (((0,), (0,)), ((), ()))
VMEM = pl.BlockSpec(memory_space=pltpu.VMEM)
SMEM = pl.BlockSpec(memory_space=pltpu.SMEM)
HBM = pl.BlockSpec(memory_space=pltpu.HBM)
ANY = pl.BlockSpec(memory_space=pl.ANY)
PARAMS = pltpu.CompilerParams(vmem_limit_bytes=8 << 20)
f32 = jnp.float32
bf16 = jnp.bfloat16


def dot(a, b, dims=NN):
    return lax.dot_general(a, b, dims, preferred_element_type=f32)


def shape(*dims, dtype=f32):
    return jax.ShapeDtypeStruct(dims, dtype)


def cost(flops, size):
    return pl.CostEstimate(flops=flops, bytes_accessed=size, transcendentals=0)


def where_am_i(devices):
    own = lax.axis_index("user")
    core = own & 1
    zero, one = (bit_order(devices, c) for c in range(CORES))
    bits = [jnp.where(core == 0, own >> z, own >> o) & 1 for z, o in zip(zero, one, strict=True)]
    return [core, *bits, own >> 1]


def rows_at(which, rows):
    start = which * rows
    return pl.ds(pl.multiple_of(start, rows) if rows % 8 == 0 else start, rows)


def half_of(ref, core):
    width = ref.shape[1] // CORES
    return ref[:, pl.ds(pl.multiple_of(core * width, width), width)]


def precision_of(stats):
    return (1.0 + stats[1:2, :] / 2.0) / (1.0 + stats[0:1, :] / 2.0)


def tile_kernel(stratum, noise_scale, codes, count, ratings, user_noise, item_noise, *refs):
    users_in, items_in, base_u, grad_u, base_v, grad_v, stats = refs[:7]
    tiles, noise_u, noise_v, pred, err_b, sems = refs[7:13]
    rows = err_b.shape[0]
    tile = tiles.shape[-1]
    grid = rows // tile
    moves = [
        (ratings.at[0, stratum], tiles),
        (user_noise.at[stratum], noise_u),
        (item_noise.at[stratum], noise_v),
    ]
    users, items = users_in, items_in
    if stratum == 0:
        users, items = refs[13:]
        moves += [(users_in, users), (items_in, items)]
    copies = [
        pltpu.make_async_copy(source, target, sems.at[n]) for n, (source, target) in enumerate(moves)
    ]
    for copy in copies[::-1]:
        copy.start()
    for copy in copies[3:]:
        copy.wait()
    user_b = users[...].astype(bf16)
    item_b = items[...].astype(bf16)
    pred[...] = dot(user_b, item_b, NT)
    err_b[...] = jnp.zeros_like(err_b)
    live_slots = count[0, stratum]
    sse = jnp.zeros((tile, tile), f32)
    copies[0].wait()
    for slot in range(tiles.shape[0]):
        code = codes[0, stratum, slot]
        at_rows = rows_at(code // grid, tile)
        at_cols = rows_at(code % grid, tile)
        live = (slot < live_slots).astype(f32)
        err = (tiles[slot].astype(f32) - pred[at_rows, at_cols]) * live
        sse = sse + err * err
        err_b[at_rows, at_cols] = err.astype(bf16)
    err_all = err_b[...]
    total = jnp.sum(sse)
    counted = live_slots.astype(f32) * float(tile * tile)
    row = lax.broadcasted_iota(jnp.int32, stats.shape, 0)
    stats[...] = jnp.where(row == 0, total, jnp.where(row == 1, counted, 0.0))
    grad_u[...] = step_size * dot(err_all, item_b)
    grad_v[...] = step_size * dot(err_all, user_b, TN)
    copies[1].wait()
    base_u[...] = (1.0 - step_size * prior_prec) * users[...] + noise_scale * noise_u[...].astype(
        f32
    )
    copies[2].wait()
    base_v[...] = (1.0 - step_size * item_prec) * items[...] + noise_scale * noise_v[...].astype(f32)


def tile_pass(stratum, codes, count, ratings, user_noise, item_noise, users, items):
    slots, tile = ratings.shape[2:4]
    rows, rank = users.shape
    first = stratum == 0
    return pl.pallas_call(
        functools.partial(tile_kernel, stratum, math.sqrt(2.0 * step_size)),
        out_shape=(shape(rows, rank),) * 4 + (shape(RIDERS, rank // CORES),),
        in_specs=[SMEM] * 2 + [HBM] * 3 + [HBM if first else VMEM] * 2,
        out_specs=(VMEM,) * 5,
        scratch_shapes=[
            pltpu.VMEM((slots, tile, tile), bf16),
            pltpu.VMEM((rows, rank), bf16),
            pltpu.VMEM((rows, rank), bf16),
            pltpu.VMEM((rows, rows), f32),
            pltpu.VMEM((rows, rows), bf16),
            pltpu.SemaphoreType.DMA((5,)),
        ]
        + [pltpu.VMEM((rows, rank), f32)] * (2 if first else 0),
        compiler_params=PARAMS,
        cost_estimate=cost(6 * rows * rows * rank, 16 * rows * rank),
        name="tile_pass",
    )(codes, count, ratings, user_noise, item_noise, users, items)


def first_kernel(devices, feats_in, weights_in, users_in, own_mean, other_mean, send, keep, old, mean, feats, weights, users, sems):
    copies = [
        pltpu.make_async_copy(source, target, sems.at[n])
        for n, (source, target) in enumerate(
            [(weights_in, weights), (feats_in, feats), (users_in, users)]
        )
    ]
    for copy in copies:
        copy.start()
    place = where_am_i(devices)
    here = place[0]
    copies[0].wait()
    weights_b = weights[...].astype(bf16)
    copies[1].wait()
    mean[...] = dot(feats[...], weights_b)
    copies[2].wait()
    for grad, means, which in ((send, other_mean, 1 - here), (keep, own_mean, here)):
        mean_now = half_of(mean, which)
        means[...] = mean_now
        offset = (half_of(users, which) - mean_now).astype(bf16)
        grad[...] = dot(feats[...], offset, TN)
    rows, width = old.shape
    start = place[1] * (weights.shape[0] // 2) + place[2] * rows
    cols = pl.ds(pl.multiple_of(here * width, width), width)
    old[...] = weights[pl.ds(pl.multiple_of(start, rows), rows), cols]


def first_pass(devices, feats, weights, users):
    rows, rank = users.shape
    feat = weights.shape[0]
    width = rank // CORES
    return pl.pallas_call(
        functools.partial(first_kernel, devices),
        out_shape=(shape(rows, width),) * 2 + (shape(feat, width),) * 2 + (shape(feat // 4, width),),
        in_specs=[HBM] * 3,
        out_specs=(VMEM,) * 5,
        scratch_shapes=[
            pltpu.VMEM(users.shape, f32),
            pltpu.VMEM(feats.shape, bf16),
            pltpu.VMEM(weights.shape, f32),
            pltpu.VMEM(users.shape, f32),
            pltpu.SemaphoreType.DMA((3,)),
        ],
        compiler_params=PARAMS,
        cost_estimate=cost(4 * rows * feat * rank, 8 * feat * rank),
        name="first_pass",
    )(feats, weights, users)


def widen_kernel(narrow_in, wide, narrow, sem):
    copy = pltpu.make_async_copy(narrow_in, narrow, sem.at[0])
    copy.start()
    copy.wait()
    wide[...] = narrow[...].astype(f32)


def widen_pass(narrow):
    return pl.pallas_call(
        widen_kernel,
        out_shape=shape(*narrow.shape),
        in_specs=[HBM],
        out_specs=VMEM,
        scratch_shapes=[pltpu.VMEM(narrow.shape, bf16), pltpu.SemaphoreType.DMA((1,))],
        compiler_params=PARAMS,
        name="widen_pass",
    )(narrow)


def join_kernel(own, other, both, turned):
    rows = other.shape[0]
    both[:rows, :] = own[...]
    both[rows:, :] = other[...].astype(bf16)
    turned[:, :rows] = own[...].T
    turned[:, rows:] = other[...].T.astype(bf16)


def join_pass(own, other):
    rows, feat = own.shape
    return pl.pallas_call(
        join_kernel,
        out_shape=(shape(CORES * rows, feat, dtype=bf16), shape(feat, CORES * rows, dtype=bf16)),
        in_specs=[VMEM, VMEM],
        out_specs=(VMEM, VMEM),
        compiler_params=PARAMS,
        cost_estimate=cost(rows * feat, 12 * rows * feat),
        name="join_pass",
    )(own, other)


def part_kernel(devices, feats, part, mean):
    half = part.shape[0]
    bit = where_am_i(devices)[1]
    here = pl.ds(pl.multiple_of(bit * half, half), half)
    mean[...] = dot(feats[:, here], part[...].astype(bf16))


def part_pass(devices, feats, part):
    rows = feats.shape[0]
    half, width = part.shape
    return pl.pallas_call(
        functools.partial(part_kernel, devices),
        out_shape=shape(rows, width),
        in_specs=[VMEM, VMEM],
        out_specs=VMEM,
        compiler_params=PARAMS,
        cost_estimate=cost(2 * rows * half * width, 4 * rows * half),
        name="part_pass",
    )(feats, part)


def prior_kernel(places, devices, feats, turned, begun, part, got, own_cols, other_cols, stats, more_stats, own_mean, other_mean, send, keep, *refs):
    rows = own_cols.shape[0]
    half = keep.shape[0]
    place = where_am_i(devices)
    core, bit = place[0], place[1]
    here = pl.ds(pl.multiple_of(bit * half, half), half)
    there = pl.ds(pl.multiple_of((1 - bit) * half, half), half)
    offset = refs[-1]
    mean = begun[...] + dot(feats[:, there], got[...].astype(bf16))
    own_mean[...] = mean[:rows]
    other_mean[...] = mean[rows:]
    offset[:rows, :] = (own_cols[...] - mean[:rows]).astype(bf16)
    offset[rows:, :] = (other_cols[...] - mean[rows:]).astype(bf16)
    send[half:, :] = stats[...] + more_stats[...]
    if places is None:
        send[:half, :] = dot(turned[there, :], offset[...])
        keep[...] = dot(turned[here, :], offset[...])
        return
    old, full = refs[:2]
    full[here, :] = part[...]
    full[there, :] = got[...]
    start = place[-1] * old.shape[0]
    if old.shape[0] % 8 == 0:
        start = pl.multiple_of(start, old.shape[0])
    old[...] = full[pl.ds(start, old.shape[0]), :]
    full[...] = dot(turned[...], offset[...])
    blocks = len(places[0])
    block = 2 * half // blocks
    for ref, which in ((send, 1 - bit), (keep, bit)):
        for n in range(blocks // 2):
            source = jnp.int32(0)
            for c, order in enumerate(places):
                for b in range(2):
                    source = jnp.where((core == c) & (which == b), order[b * blocks // 2 + n], source)
            source = source * block
            if block % 8 == 0:
                source = pl.multiple_of(source, block)
            ref[n * block : (n + 1) * block, :] = full[pl.ds(source, block), :]


def prior_pass(devices, feats, turned, begun, part, got, own_cols, other_cols, stats, more_stats, places=None):
    rows, width = own_cols.shape
    half = part.shape[0]
    outs = [shape(rows, width)] * 2 + [shape(half + stats.shape[0], width), shape(half, width)]
    scratch = [pltpu.VMEM((CORES * rows, width), bf16)]
    if places is not None:
        outs.append(shape(2 * half // len(places[0]), width))
        scratch.insert(0, pltpu.VMEM((2 * half, width), f32))
    return pl.pallas_call(
        functools.partial(prior_kernel, places, devices),
        out_shape=tuple(outs),
        in_specs=[VMEM] * 9,
        out_specs=(VMEM,) * len(outs),
        scratch_shapes=scratch,
        compiler_params=PARAMS,
        cost_estimate=cost(16 * rows * half * width, 16 * rows * half),
        name="prior_pass",
    )(feats, turned, begun, part, got, own_cols, other_cols, stats, more_stats)


def step_kernel(halving, slot, devices, held, got, sent, more, *refs):
    send = refs[-2] if halving else refs[-1]
    riders = sent.shape[0] - RIDERS, more.shape[0] - RIDERS
    rider = sent[riders[0] :, :] + more[riders[1] :, :]
    rows = send.shape[0] - RIDERS
    if halving:
        bit = where_am_i(devices)[slot]
        for ref, which in ((send, 1 - bit), (refs[-1], bit)):
            at = pl.ds(pl.multiple_of(which * rows, 8), rows) if rows % 8 == 0 else pl.ds(which * rows, rows)
            ref[:rows, :] = held[at, :] + got[at, :]
    else:
        send[:rows, :] = held[:rows, :] + got[:rows, :]
    send[rows:, :] = rider


def step_pass(halving, stage, devices, held, got, sent, more, rows, later=()):
    width = held.shape[1]
    outs = [shape(rows // 2 + RIDERS, width), shape(rows // 2, width)] if halving else [shape(rows + RIDERS, width)]
    return pl.pallas_call(
        functools.partial(step_kernel, halving, 1 + stage, devices),
        out_shape=tuple(outs),
        in_specs=[VMEM] * 4 + [ANY] * len(later),
        out_specs=(VMEM,) * len(outs),
        compiler_params=PARAMS,
        cost_estimate=cost(rows * width, 12 * rows * width),
        name="step_pass",
    )(held, got, sent, more, *later)


def update_kernel(rate, held, got, sent, old, *refs):
    new, stats = refs[-2:]
    rows = old.shape[0]
    total = held[:rows, :] + got[:rows, :]
    before = old[...]
    new[...] = before + rate * (prior_prec * total - weight_decay * before)
    stats[...] = sent[sent.shape[0] - RIDERS :, :] + got[rows:, :]


def update_pass(rate, held, got, sent, old, later=()):
    return pl.pallas_call(
        functools.partial(update_kernel, rate),
        out_shape=(shape(*old.shape), shape(RIDERS, old.shape[1])),
        in_specs=[VMEM] * 4 + [ANY] * len(later),
        out_specs=(VMEM,) * 2,
        compiler_params=PARAMS,
        cost_estimate=cost(4 * old.size, 16 * old.size),
        name="update_pass",
    )(held, got, sent, old, *later)


def gather_kernel(slot, devices, part, got, both):
    rows = part.shape[0]
    bit = where_am_i(devices)[slot]
    both[pl.ds(pl.multiple_of(bit * rows, rows), rows), :] = part[...]
    both[pl.ds(pl.multiple_of((1 - bit) * rows, rows), rows), :] = got[...]


def gather_pass(stage, devices, part, got):
    rows, width = part.shape
    return pl.pallas_call(
        functools.partial(gather_kernel, 1 + stage, devices),
        out_shape=shape(2 * rows, width),
        in_specs=[VMEM, VMEM],
        out_specs=VMEM,
        compiler_params=PARAMS,
        cost_estimate=cost(rows * width, 16 * rows * width),
        name="gather_pass",
    )(part, got)


def split_kernel(devices, both, mine, other):
    place = where_am_i(devices)
    rows = mine.shape[0]
    for ref, which in ((mine, place[0]), (other, 1 - place[0])):
        at = pl.ds(pl.multiple_of(which * rows, 8), rows) if rows % 8 == 0 else pl.ds(which * rows, rows)
        ref[...] = both[at, :]


def split_pass(devices, both):
    rows, width = both.shape
    return pl.pallas_call(
        functools.partial(split_kernel, devices),
        out_shape=(shape(rows // CORES, width),) * 2,
        in_specs=[VMEM],
        out_specs=(VMEM,) * 2,
        compiler_params=PARAMS,
        name="split_pass",
    )(both)


def across_kernel(devices, mine, other, both):
    place = where_am_i(devices)
    width = mine.shape[1]
    both[:, pl.ds(pl.multiple_of(place[0] * width, width), width)] = mine[...]
    both[:, pl.ds(pl.multiple_of((1 - place[0]) * width, width), width)] = other[...]


def across_pass(devices, mine, other):
    rows, width = mine.shape
    return pl.pallas_call(
        functools.partial(across_kernel, devices),
        out_shape=shape(rows, CORES * width),
        in_specs=[VMEM, VMEM],
        out_specs=VMEM,
        compiler_params=PARAMS,
        name="across_pass",
    )(mine, other)


def renew_kernel(devices, stats, base_u, grad_u, own_mean, other_mean, base_v, grad_v, users, items, *cols):
    core = where_am_i(devices)[0]
    width = own_mean.shape[1]
    precision = precision_of(stats[...])
    precision = jnp.concatenate([precision] * CORES, 1)
    items[...] = base_v[...] + precision * grad_v[...]
    new = base_u[...] + precision * grad_u[...]
    pull = step_size * prior_prec
    left = jnp.where(core == 0, own_mean[...], other_mean[...])
    right = jnp.where(core == 0, other_mean[...], own_mean[...])
    users[:, :width] = new[:, :width] + pull * left
    users[:, width:] = new[:, width:] + pull * right
    for ref, which in zip(cols, (core, 1 - core), strict=False):
        ref[...] = half_of(users, which)


def renew_pass(devices, last, stats, base_u, grad_u, own_mean, *state):
    outs = [shape(*base_u.shape)] * 2 + ([] if last else [shape(*own_mean.shape)] * 2)
    return pl.pallas_call(
        functools.partial(renew_kernel, devices),
        out_shape=tuple(outs),
        in_specs=[VMEM] * 7,
        out_specs=(VMEM,) * len(outs),
        compiler_params=PARAMS,
        cost_estimate=cost(8 * base_u.size, 32 * base_u.size),
        name="renew_pass",
    )(stats, base_u, grad_u, own_mean, *state)


def bit_order(devices, core):
    bits = devices.bit_length() - 1
    far = list(range(3, bits))
    return [1, 2] + far if core == 0 else [2, 1] + far[::-1]


def swap(array, devices):
    return lax.ppermute(array, "user", [(i, i ^ 1) for i in range(devices)])


def roll(array, devices):
    return lax.ppermute(array, "user", [(i, (i + 1) % devices) for i in range(devices)])


def exchange(array, devices, stage):
    orders = [bit_order(devices, core) for core in range(CORES)]
    pairs = [(i, i ^ (1 << orders[i & 1][stage])) for i in range(devices)]
    return lax.ppermute(array, "user", pairs)


def final_places(devices):
    bits = devices.bit_length() - 1
    return [
        [
            sum(
                ((place >> (bits - 2 - n)) & 1) << (bit - 1)
                for n, bit in enumerate(bit_order(devices, core))
            )
            for place in range(devices // 2)
        ]
        for core in range(CORES)
    ]


def local(
    ratings,
    tile_index,
    tile_count,
    side_features,
    user_factors,
    item_factors,
    prior_weights,
    user_noise,
    item_noise,
):
    devices = lax.axis_size("user")
    stages = devices.bit_length() - 2
    strata = ratings.shape[1]
    feat = prior_weights.shape[0]
    rate = rate_scale / (user_factors.shape[0] * devices)
    tables = (tile_index, tile_count, ratings, user_noise, item_noise)

    own_mean, other_mean, send, held, old = first_pass(
        devices, side_features, prior_weights, user_factors
    )
    got = swap(send, devices)
    *state, stats = tile_pass(0, *tables, user_factors, item_factors)
    more = swap(stats, devices)
    send, held = step_pass(True, 0, devices, held, got, stats, more, feat)
    feats, turned = join_pass(side_features, swap(widen_pass(side_features), devices))
    for stratum in range(strata):
        last = stratum + 1 == strata
        for stage in range(stages - 1):
            got = exchange(send, devices, stage)
            rows = got.shape[0] - RIDERS
            if last or stage < 1:
                send, held = step_pass(True, stage + 1, devices, held, got, send, got, rows)
            else:
                (send,) = step_pass(False, 0, devices, held, got, send, got, rows)
                held = send
        got = exchange(send, devices, stages - 1)
        part, stats = update_pass(rate, held, got, send, old)
        users, items, *cols = renew_pass(
            devices, last, stats, *state[:2], own_mean, other_mean, *state[2:]
        )
        if last:
            break
        old = part
        items = roll(items, devices)
        own_cols, other_cols = cols[0], swap(cols[1], devices)
        part = gather_pass(1, devices, part, exchange(part, devices, 1))
        got = exchange(part, devices, 0)
        *state, stats = tile_pass(stratum + 1, *tables, users, items)
        more = swap(stats, devices)
        begun = part_pass(devices, feats, part)
        own_mean, other_mean, send, held, *olds = prior_pass(
            devices,
            feats,
            turned,
            begun,
            part,
            got,
            own_cols,
            other_cols,
            stats,
            more,
            final_places(devices) if stratum + 2 == strata else None,
        )
        if olds:
            (old,) = olds
        other_mean = swap(other_mean, devices)
    mine, other = split_pass(devices, part)
    return (users, items, across_pass(devices, mine, swap(other, devices)))


def solution(mesh):
    return jax.shard_map(
        local,
        mesh=mesh,
        in_specs=(
            P("user", None, None, None, None),
            P("user", None, None),
            P("user", None),
            P("user", None),
            P("user", None),
            P("user", None),
            P(),
            P(None, "user", None),
            P(None, "user", None),
        ),
        out_specs=(P("user", None), P("user", None), P("user", None)),
        check_vma=False,
    )
```

```python
import functools
import math

import jax
import jax.numpy as jnp
from jax import lax
from jax.experimental import pallas as pl
from jax.experimental.pallas import tpu as pltpu
from jax.sharding import PartitionSpec as P

step_size = 0.01
prior_prec = 8.0
item_prec = 1.0
weight_decay = 1.0
rate_scale = 0.04

CORES = 2
RIDERS = 8
ITEM_PARTS = 2
NN = (((1,), (0,)), ((), ()))
NT = (((1,), (1,)), ((), ()))
TN = (((0,), (0,)), ((), ()))
VMEM = pl.BlockSpec(memory_space=pltpu.VMEM)
SMEM = pl.BlockSpec(memory_space=pltpu.SMEM)
ANY = pl.BlockSpec(memory_space=pl.ANY)
PARAMS = pltpu.CompilerParams(vmem_limit_bytes=8 << 20)
f32 = jnp.float32
bf16 = jnp.bfloat16


def dot(a, b, dims=NN):
    return lax.dot_general(a, b, dims, preferred_element_type=f32)


def shape(*dims, dtype=f32):
    return jax.ShapeDtypeStruct(dims, dtype)


def cost(flops, size):
    return pl.CostEstimate(flops=flops, bytes_accessed=size, transcendentals=0)


def where_am_i(devices):
    own = lax.axis_index("user")
    core = own & 1
    zero, one = (bit_order(devices, c) for c in range(CORES))
    bits = [jnp.where(core == 0, own >> z, own >> o) & 1 for z, o in zip(zero, one, strict=True)]
    return [core, *bits, own >> 1]


def rows_at(which, rows):
    start = which * rows
    return pl.ds(pl.multiple_of(start, rows) if rows % 8 == 0 else start, rows)


def half_of(ref, core):
    width = ref.shape[1] // CORES
    return ref[:, pl.ds(pl.multiple_of(core * width, width), width)]


def precision_of(stats):
    return (1.0 + stats[1:2, :] / 2.0) / (1.0 + stats[0:1, :] / 2.0)


def error_kernel(stratum, codes, count, ratings, users, *refs):
    items, (err_b, stats, pred) = refs[:-3], refs[-3:]
    tile = ratings.shape[-1]
    grid = users.shape[0] // tile
    user_b = users[...].astype(bf16)
    start = 0
    for part in items:
        pred[:, start : start + part.shape[0]] = dot(user_b, part[...].astype(bf16), NT)
        start += part.shape[0]
    err_b[...] = jnp.zeros_like(err_b)
    live_slots = count[0, stratum]
    sse = jnp.zeros((tile, tile), f32)
    for slot in range(ratings.shape[2]):
        code = codes[0, stratum, slot]
        at_rows = rows_at(code // grid, tile)
        at_cols = rows_at(code % grid, tile)
        live = (slot < live_slots).astype(f32)
        err = (ratings[0, stratum, slot].astype(f32) - pred[at_rows, at_cols]) * live
        sse = sse + err * err
        err_b[at_rows, at_cols] = err.astype(bf16)
    total = jnp.sum(sse)
    counted = live_slots.astype(f32) * float(tile * tile)
    row = lax.broadcasted_iota(jnp.int32, stats.shape, 0)
    stats[...] = jnp.where(row == 0, total, jnp.where(row == 1, counted, 0.0))


def error_pass(stratum, codes, count, ratings, users, *items):
    rows, rank = users.shape
    return pl.pallas_call(
        functools.partial(error_kernel, stratum),
        out_shape=(shape(rows, rows, dtype=bf16), shape(RIDERS, rank // CORES)),
        in_specs=[SMEM] * 2 + [VMEM] * (2 + len(items)),
        out_specs=(VMEM,) * 2,
        scratch_shapes=[pltpu.VMEM((rows, rows), f32)],
        compiler_params=PARAMS,
        cost_estimate=cost(24 * rows * rows * rank, 64 * rows * rank),
        name="error_pass",
    )(codes, count, ratings, users, *items)


def grad_kernel(stratum, noise_scale, err_b, user_noise, item_noise, users, *refs):
    items, (base_u, grad_u, base_v, grad_v) = refs[:-4], refs[-4:]
    item_b = jnp.concatenate([part[...].astype(bf16) for part in items], 0)
    grad_u[...] = step_size * dot(err_b[...], item_b)
    grad_v[...] = step_size * dot(err_b[...], users[...].astype(bf16), TN)
    noise = noise_scale * user_noise[stratum].astype(f32)
    base_u[...] = (1.0 - step_size * prior_prec) * users[...] + noise
    start = 0
    for part in items:
        at = slice(start, start + part.shape[0])
        noise = noise_scale * item_noise[stratum, at].astype(f32)
        base_v[at, :] = (1.0 - step_size * item_prec) * part[...] + noise
        start += part.shape[0]


def grad_pass(stratum, err_b, user_noise, item_noise, users, *items):
    rows, rank = users.shape
    return pl.pallas_call(
        functools.partial(grad_kernel, stratum, math.sqrt(2.0 * step_size)),
        out_shape=(shape(rows, rank),) * 4,
        in_specs=[VMEM] * (4 + len(items)),
        out_specs=(VMEM,) * 4,
        compiler_params=PARAMS,
        cost_estimate=cost(4 * rows * rows * rank, 28 * rows * rank),
        name="grad_pass",
    )(err_b, user_noise, item_noise, users, *items)


def first_kernel(devices, feats, weights, users, later, own_mean, other_mean, send, keep, old, mean):
    place = where_am_i(devices)
    here = place[0]
    mean[...] = dot(feats[...], weights[...].astype(bf16))
    for grad, means, which in ((send, other_mean, 1 - here), (keep, own_mean, here)):
        mean_now = half_of(mean, which)
        means[...] = mean_now
        offset = (half_of(users, which) - mean_now).astype(bf16)
        grad[...] = dot(feats[...], offset, TN)
    rows, width = old.shape
    old[...] = weights[rows_at(2 * place[1] + place[2], rows), rows_at(here, width)]


def first_pass(devices, feats, weights, users, later):
    rows, rank = users.shape
    feat = weights.shape[0]
    width = rank // CORES
    return pl.pallas_call(
        functools.partial(first_kernel, devices),
        out_shape=(shape(rows, width),) * 2 + (shape(feat, width),) * 2 + (shape(feat // 4, width),),
        in_specs=[VMEM] * 3 + [ANY],
        out_specs=(VMEM,) * 5,
        scratch_shapes=[pltpu.VMEM(users.shape, f32)],
        compiler_params=PARAMS,
        cost_estimate=cost(4 * rows * feat * rank, 8 * feat * rank),
        name="first_pass",
    )(feats, weights, users, later)


def widen_kernel(narrow, wide):
    wide[...] = narrow[...].astype(f32)


def widen_pass(narrow):
    return pl.pallas_call(
        widen_kernel,
        out_shape=shape(*narrow.shape),
        in_specs=[VMEM],
        out_specs=VMEM,
        compiler_params=PARAMS,
        name="widen_pass",
    )(narrow)


def join_kernel(own, other, both, turned):
    rows = other.shape[0]
    both[:rows, :] = own[...]
    both[rows:, :] = other[...].astype(bf16)
    turned[:, :rows] = own[...].T
    turned[:, rows:] = other[...].T.astype(bf16)


def join_pass(own, other):
    rows, feat = own.shape
    return pl.pallas_call(
        join_kernel,
        out_shape=(shape(CORES * rows, feat, dtype=bf16), shape(feat, CORES * rows, dtype=bf16)),
        in_specs=[VMEM, VMEM],
        out_specs=(VMEM, VMEM),
        compiler_params=PARAMS,
        cost_estimate=cost(rows * feat, 12 * rows * feat),
        name="join_pass",
    )(own, other)


def part_kernel(devices, feats, part, mean):
    half = part.shape[0]
    bit = where_am_i(devices)[1]
    here = pl.ds(pl.multiple_of(bit * half, half), half)
    mean[...] = dot(feats[:, here], part[...].astype(bf16))


def part_pass(devices, feats, part):
    rows = feats.shape[0]
    half, width = part.shape
    return pl.pallas_call(
        functools.partial(part_kernel, devices),
        out_shape=shape(rows, width),
        in_specs=[VMEM, VMEM],
        out_specs=VMEM,
        compiler_params=PARAMS,
        cost_estimate=cost(2 * rows * half * width, 4 * rows * half),
        name="part_pass",
    )(feats, part)


def prior_kernel(places, devices, feats, turned, begun, part, got, own_cols, other_cols, stats, more_stats, own_mean, other_mean, send, keep, *refs):
    rows = own_cols.shape[0]
    half = keep.shape[0]
    place = where_am_i(devices)
    core, bit = place[0], place[1]
    here = pl.ds(pl.multiple_of(bit * half, half), half)
    there = pl.ds(pl.multiple_of((1 - bit) * half, half), half)
    offset = refs[-1]
    mean = begun[...] + dot(feats[:, there], got[...].astype(bf16))
    own_mean[...] = mean[:rows]
    other_mean[...] = mean[rows:]
    offset[:rows, :] = (own_cols[...] - mean[:rows]).astype(bf16)
    offset[rows:, :] = (other_cols[...] - mean[rows:]).astype(bf16)
    send[half:, :] = stats[...] + more_stats[...]
    if places is None:
        send[:half, :] = dot(turned[there, :], offset[...])
        keep[...] = dot(turned[here, :], offset[...])
        return
    old, full = refs[:2]
    full[here, :] = part[...]
    full[there, :] = got[...]
    start = place[-1] * old.shape[0]
    if old.shape[0] % 8 == 0:
        start = pl.multiple_of(start, old.shape[0])
    old[...] = full[pl.ds(start, old.shape[0]), :]
    full[...] = dot(turned[...], offset[...])
    blocks = len(places[0])
    block = 2 * half // blocks
    for ref, which in ((send, 1 - bit), (keep, bit)):
        for n in range(blocks // 2):
            source = jnp.int32(0)
            for c, order in enumerate(places):
                for b in range(2):
                    source = jnp.where((core == c) & (which == b), order[b * blocks // 2 + n], source)
            source = source * block
            if block % 8 == 0:
                source = pl.multiple_of(source, block)
            ref[n * block : (n + 1) * block, :] = full[pl.ds(source, block), :]


def prior_pass(devices, feats, turned, begun, part, got, own_cols, other_cols, stats, more_stats, places=None):
    rows, width = own_cols.shape
    half = part.shape[0]
    outs = [shape(rows, width)] * 2 + [shape(half + stats.shape[0], width), shape(half, width)]
    scratch = [pltpu.VMEM((CORES * rows, width), bf16)]
    if places is not None:
        outs.append(shape(2 * half // len(places[0]), width))
        scratch.insert(0, pltpu.VMEM((2 * half, width), f32))
    return pl.pallas_call(
        functools.partial(prior_kernel, places, devices),
        out_shape=tuple(outs),
        in_specs=[VMEM] * 9,
        out_specs=(VMEM,) * len(outs),
        scratch_shapes=scratch,
        compiler_params=PARAMS,
        cost_estimate=cost(16 * rows * half * width, 16 * rows * half),
        name="prior_pass",
    )(feats, turned, begun, part, got, own_cols, other_cols, stats, more_stats)


def step_kernel(halving, slot, devices, held, got, sent, more, *refs):
    send = refs[-2] if halving else refs[-1]
    riders = sent.shape[0] - RIDERS, more.shape[0] - RIDERS
    rider = sent[riders[0] :, :] + more[riders[1] :, :]
    rows = send.shape[0] - RIDERS
    if halving:
        bit = where_am_i(devices)[slot]
        for ref, which in ((send, 1 - bit), (refs[-1], bit)):
            at = pl.ds(pl.multiple_of(which * rows, 8), rows) if rows % 8 == 0 else pl.ds(which * rows, rows)
            ref[:rows, :] = held[at, :] + got[at, :]
    else:
        send[:rows, :] = held[:rows, :] + got[:rows, :]
    send[rows:, :] = rider


def step_pass(halving, stage, devices, held, got, sent, more, rows, later=()):
    width = held.shape[1]
    outs = [shape(rows // 2 + RIDERS, width), shape(rows // 2, width)] if halving else [shape(rows + RIDERS, width)]
    return pl.pallas_call(
        functools.partial(step_kernel, halving, 1 + stage, devices),
        out_shape=tuple(outs),
        in_specs=[VMEM] * 4 + [ANY] * len(later),
        out_specs=(VMEM,) * len(outs),
        compiler_params=PARAMS,
        cost_estimate=cost(rows * width, 12 * rows * width),
        name="step_pass",
    )(held, got, sent, more, *later)


def update_kernel(rate, held, got, sent, old, *refs):
    new, stats = refs[-2:]
    rows = old.shape[0]
    total = held[:rows, :] + got[:rows, :]
    before = old[...]
    new[...] = before + rate * (prior_prec * total - weight_decay * before)
    stats[...] = sent[sent.shape[0] - RIDERS :, :] + got[rows:, :]


def update_pass(rate, held, got, sent, old, later=()):
    return pl.pallas_call(
        functools.partial(update_kernel, rate),
        out_shape=(shape(*old.shape), shape(RIDERS, old.shape[1])),
        in_specs=[VMEM] * 4 + [ANY] * len(later),
        out_specs=(VMEM,) * 2,
        compiler_params=PARAMS,
        cost_estimate=cost(4 * old.size, 16 * old.size),
        name="update_pass",
    )(held, got, sent, old, *later)


def gather_kernel(slot, devices, part, got, both):
    rows = part.shape[0]
    bit = where_am_i(devices)[slot]
    both[pl.ds(pl.multiple_of(bit * rows, rows), rows), :] = part[...]
    both[pl.ds(pl.multiple_of((1 - bit) * rows, rows), rows), :] = got[...]


def gather_pass(stage, devices, part, got):
    rows, width = part.shape
    return pl.pallas_call(
        functools.partial(gather_kernel, 1 + stage, devices),
        out_shape=shape(2 * rows, width),
        in_specs=[VMEM, VMEM],
        out_specs=VMEM,
        compiler_params=PARAMS,
        cost_estimate=cost(rows * width, 16 * rows * width),
        name="gather_pass",
    )(part, got)


def split_kernel(devices, both, mine, other):
    place = where_am_i(devices)
    rows = mine.shape[0]
    for ref, which in ((mine, place[0]), (other, 1 - place[0])):
        at = pl.ds(pl.multiple_of(which * rows, 8), rows) if rows % 8 == 0 else pl.ds(which * rows, rows)
        ref[...] = both[at, :]


def split_pass(devices, both):
    rows, width = both.shape
    return pl.pallas_call(
        functools.partial(split_kernel, devices),
        out_shape=(shape(rows // CORES, width),) * 2,
        in_specs=[VMEM],
        out_specs=(VMEM,) * 2,
        compiler_params=PARAMS,
        name="split_pass",
    )(both)


def across_kernel(devices, mine, other, both):
    place = where_am_i(devices)
    width = mine.shape[1]
    both[:, pl.ds(pl.multiple_of(place[0] * width, width), width)] = mine[...]
    both[:, pl.ds(pl.multiple_of((1 - place[0]) * width, width), width)] = other[...]


def across_pass(devices, mine, other):
    rows, width = mine.shape
    return pl.pallas_call(
        functools.partial(across_kernel, devices),
        out_shape=shape(rows, CORES * width),
        in_specs=[VMEM, VMEM],
        out_specs=VMEM,
        compiler_params=PARAMS,
        name="across_pass",
    )(mine, other)


def renew_kernel(devices, stats, base_u, grad_u, own_mean, other_mean, base_v, grad_v, users, *outs):
    core = where_am_i(devices)[0]
    width = own_mean.shape[1]
    precision = precision_of(stats[...])
    precision = jnp.concatenate([precision] * CORES, 1)
    parts = 1 if len(outs) == 1 else ITEM_PARTS
    rows = base_v.shape[0] // parts
    for n, items in enumerate(outs[:parts]):
        at = slice(n * rows, (n + 1) * rows)
        items[...] = base_v[at, :] + precision * grad_v[at, :]
    new = base_u[...] + precision * grad_u[...]
    pull = step_size * prior_prec
    left = jnp.where(core == 0, own_mean[...], other_mean[...])
    right = jnp.where(core == 0, other_mean[...], own_mean[...])
    users[:, :width] = new[:, :width] + pull * left
    users[:, width:] = new[:, width:] + pull * right
    for ref, which in zip(outs[parts:], (core, 1 - core), strict=False):
        ref[...] = half_of(users, which)


def renew_pass(devices, last, stats, base_u, grad_u, own_mean, *state):
    rows, rank = base_u.shape
    outs = [shape(rows, rank)]
    if last:
        outs.append(shape(rows, rank))
    else:
        outs += [shape(rows // ITEM_PARTS, rank)] * ITEM_PARTS + [shape(*own_mean.shape)] * 2
    return pl.pallas_call(
        functools.partial(renew_kernel, devices),
        out_shape=tuple(outs),
        in_specs=[VMEM] * 7,
        out_specs=(VMEM,) * len(outs),
        compiler_params=PARAMS,
        cost_estimate=cost(8 * base_u.size, 32 * base_u.size),
        name="renew_pass",
    )(stats, base_u, grad_u, own_mean, *state)


def bit_order(devices, core):
    bits = devices.bit_length() - 1
    far = list(range(3, bits))
    return [1, 2] + far if core == 0 else [2, 1] + far[::-1]


def swap(array, devices):
    return lax.ppermute(array, "user", [(i, i ^ 1) for i in range(devices)])


def roll(array, devices):
    return lax.ppermute(array, "user", [(i, (i + 1) % devices) for i in range(devices)])


def exchange(array, devices, stage):
    orders = [bit_order(devices, core) for core in range(CORES)]
    pairs = [(i, i ^ (1 << orders[i & 1][stage])) for i in range(devices)]
    return lax.ppermute(array, "user", pairs)


def final_places(devices):
    bits = devices.bit_length() - 1
    return [
        [
            sum(
                ((place >> (bits - 2 - n)) & 1) << (bit - 1)
                for n, bit in enumerate(bit_order(devices, core))
            )
            for place in range(devices // 2)
        ]
        for core in range(CORES)
    ]


def local(
    ratings,
    tile_index,
    tile_count,
    side_features,
    user_factors,
    item_factors,
    prior_weights,
    user_noise,
    item_noise,
):
    devices = lax.axis_size("user")
    stages = devices.bit_length() - 2
    strata = ratings.shape[1]
    feat = prior_weights.shape[0]
    rate = rate_scale / (user_factors.shape[0] * devices)
    def errors_of(stratum, users, *items):
        err_b, stats = error_pass(stratum, tile_index, tile_count, ratings, users, *items)
        return err_b, stats, swap(stats, devices)

    wide = widen_pass(side_features)
    own_mean, other_mean, send, held, old = first_pass(
        devices, side_features, prior_weights, user_factors, wide
    )
    got = swap(send, devices)
    users, items = user_factors, [item_factors]
    err_b, stats, more = errors_of(0, users, *items)
    send, held = step_pass(True, 0, devices, held, got, stats, more, feat)
    feats, turned = join_pass(side_features, swap(wide, devices))
    for stratum in range(strata):
        last = stratum + 1 == strata
        state = grad_pass(stratum, err_b, user_noise, item_noise, users, *items)
        for stage in range(stages - 1):
            got = exchange(send, devices, stage)
            rows = got.shape[0] - RIDERS
            later = state[:1] if stage == 0 else ()
            if last or stage < 1:
                send, held = step_pass(True, stage + 1, devices, held, got, send, got, rows, later)
            else:
                (send,) = step_pass(False, 0, devices, held, got, send, got, rows)
                held = send
        got = exchange(send, devices, stages - 1)
        part, stats = update_pass(rate, held, got, send, old)
        users, *items = renew_pass(
            devices, last, stats, *state[:2], own_mean, other_mean, *state[2:]
        )
        if last:
            break
        old = part
        *items, own_cols, other_cols = items
        items = [roll(part, devices) for part in items]
        other_cols = swap(other_cols, devices)
        part = gather_pass(1, devices, part, exchange(part, devices, 1))
        got = exchange(part, devices, 0)
        err_b, stats, more = errors_of(stratum + 1, users, *items)
        begun = part_pass(devices, feats, part)
        own_mean, other_mean, send, held, *olds = prior_pass(
            devices,
            feats,
            turned,
            begun,
            part,
            got,
            own_cols,
            other_cols,
            stats,
            more,
            final_places(devices) if stratum + 2 == strata else None,
        )
        if olds:
            (old,) = olds
        other_mean = swap(other_mean, devices)
    mine, other = split_pass(devices, part)
    return (users, *items, across_pass(devices, mine, swap(other, devices)))


def solution(mesh):
    return jax.shard_map(
        local,
        mesh=mesh,
        in_specs=(
            P("user", None, None, None, None),
            P("user", None, None),
            P("user", None),
            P("user", None),
            P("user", None),
            P("user", None),
            P(),
            P(None, "user", None),
            P(None, "user", None),
        ),
        out_specs=(P("user", None), P("user", None), P("user", None)),
        check_vma=False,
    )
```

```python
import functools
import math

import jax
import jax.numpy as jnp
from jax import lax
from jax.experimental import pallas as pl
from jax.experimental.pallas import tpu as pltpu
from jax.sharding import PartitionSpec as P

step_size = 0.01
prior_prec = 8.0
item_prec = 1.0
weight_decay = 1.0
rate_scale = 0.04

CORES = 2
RIDERS = 8
ITEM_PARTS = 1
NN = (((1,), (0,)), ((), ()))
NT = (((1,), (1,)), ((), ()))
TN = (((0,), (0,)), ((), ()))
VMEM = pl.BlockSpec(memory_space=pltpu.VMEM)
SMEM = pl.BlockSpec(memory_space=pltpu.SMEM)
ANY = pl.BlockSpec(memory_space=pl.ANY)
PARAMS = pltpu.CompilerParams(vmem_limit_bytes=8 << 20)
f32 = jnp.float32
bf16 = jnp.bfloat16


def dot(a, b, dims=NN):
    return lax.dot_general(a, b, dims, preferred_element_type=f32)


def shape(*dims, dtype=f32):
    return jax.ShapeDtypeStruct(dims, dtype)


def cost(flops, size):
    return pl.CostEstimate(flops=flops, bytes_accessed=size, transcendentals=0)


def where_am_i(devices):
    own = lax.axis_index("user")
    core = own & 1
    zero, one = (bit_order(devices, c) for c in range(CORES))
    bits = [jnp.where(core == 0, own >> z, own >> o) & 1 for z, o in zip(zero, one, strict=True)]
    return [core, *bits, own >> 1]


def rows_at(which, rows):
    start = which * rows
    return pl.ds(pl.multiple_of(start, rows) if rows % 8 == 0 else start, rows)


def half_of(ref, core):
    width = ref.shape[1] // CORES
    return ref[:, pl.ds(pl.multiple_of(core * width, width), width)]


def precision_of(stats):
    return (1.0 + stats[1:2, :] / 2.0) / (1.0 + stats[0:1, :] / 2.0)


def error_kernel(stratum, codes, count, ratings, users, *refs):
    items, (err_b, stats, pred) = refs[1:-3], refs[-3:]
    tile = ratings.shape[-1]
    grid = users.shape[0] // tile
    user_b = users[...].astype(bf16)
    start = 0
    for part in items:
        pred[:, start : start + part.shape[0]] = dot(user_b, part[...].astype(bf16), NT)
        start += part.shape[0]
    err_b[...] = jnp.zeros_like(err_b)
    live_slots = count[0, stratum]
    sse = jnp.zeros((tile, tile), f32)
    for slot in range(ratings.shape[2]):
        code = codes[0, stratum, slot]
        at_rows = rows_at(code // grid, tile)
        at_cols = rows_at(code % grid, tile)
        live = (slot < live_slots).astype(f32)
        err = (ratings[0, stratum, slot].astype(f32) - pred[at_rows, at_cols]) * live
        sse = sse + err * err
        err_b[at_rows, at_cols] = err.astype(bf16)
    total = jnp.sum(sse)
    counted = live_slots.astype(f32) * float(tile * tile)
    row = lax.broadcasted_iota(jnp.int32, stats.shape, 0)
    stats[...] = jnp.where(row == 0, total, jnp.where(row == 1, counted, 0.0))


def error_pass(stratum, codes, count, ratings, users, later, *items):
    rows, rank = users.shape
    return pl.pallas_call(
        functools.partial(error_kernel, stratum),
        out_shape=(shape(rows, rows, dtype=bf16), shape(RIDERS, rank // CORES)),
        in_specs=[SMEM] * 2 + [VMEM] * 2 + [ANY] + [VMEM] * len(items),
        out_specs=(VMEM,) * 2,
        scratch_shapes=[pltpu.VMEM((rows, rows), f32)],
        compiler_params=PARAMS,
        cost_estimate=cost(24 * rows * rows * rank, 64 * rows * rank),
        name="error_pass",
    )(codes, count, ratings, users, later, *items)


def grad_kernel(stratum, noise_scale, err_b, user_noise, item_noise, users, *refs):
    items, (base_u, grad_u, base_v, grad_v) = refs[:-4], refs[-4:]
    item_b = jnp.concatenate([part[...].astype(bf16) for part in items], 0)
    grad_u[...] = step_size * dot(err_b[...], item_b)
    grad_v[...] = step_size * dot(err_b[...], users[...].astype(bf16), TN)
    noise = noise_scale * user_noise[stratum].astype(f32)
    base_u[...] = (1.0 - step_size * prior_prec) * users[...] + noise
    start = 0
    for part in items:
        at = slice(start, start + part.shape[0])
        noise = noise_scale * item_noise[stratum, at].astype(f32)
        base_v[at, :] = (1.0 - step_size * item_prec) * part[...] + noise
        start += part.shape[0]


def grad_pass(stratum, err_b, user_noise, item_noise, users, *items):
    rows, rank = users.shape
    return pl.pallas_call(
        functools.partial(grad_kernel, stratum, math.sqrt(2.0 * step_size)),
        out_shape=(shape(rows, rank),) * 4,
        in_specs=[VMEM] * (4 + len(items)),
        out_specs=(VMEM,) * 4,
        compiler_params=PARAMS,
        cost_estimate=cost(4 * rows * rows * rank, 28 * rows * rank),
        name="grad_pass",
    )(err_b, user_noise, item_noise, users, *items)


def turn_kernel(feats, turned):
    turned[...] = feats[...].T


def turn_pass(feats):
    rows, feat = feats.shape
    return pl.pallas_call(
        turn_kernel,
        out_shape=shape(feat, rows, dtype=bf16),
        in_specs=[VMEM],
        out_specs=VMEM,
        compiler_params=PARAMS,
        cost_estimate=cost(rows * feat, 4 * rows * feat),
        name="turn_pass",
    )(feats)


def first_kernel(devices, feats, turned, weights, users, own_mean, other_mean, send, keep, old, mean):
    place = where_am_i(devices)
    here = place[0]
    mean[...] = dot(feats[...], weights[...].astype(bf16))
    for grad, means, which in ((send, other_mean, 1 - here), (keep, own_mean, here)):
        mean_now = half_of(mean, which)
        means[...] = mean_now
        offset = (half_of(users, which) - mean_now).astype(bf16)
        grad[...] = dot(turned[...], offset)
    rows, width = old.shape
    old[...] = weights[rows_at(2 * place[1] + place[2], rows), rows_at(here, width)]


def first_pass(devices, feats, turned, weights, users):
    rows, rank = users.shape
    feat = weights.shape[0]
    width = rank // CORES
    return pl.pallas_call(
        functools.partial(first_kernel, devices),
        out_shape=(shape(rows, width),) * 2 + (shape(feat, width),) * 2 + (shape(feat // 4, width),),
        in_specs=[VMEM] * 4,
        out_specs=(VMEM,) * 5,
        scratch_shapes=[pltpu.VMEM(users.shape, f32)],
        compiler_params=PARAMS,
        cost_estimate=cost(4 * rows * feat * rank, 8 * feat * rank),
        name="first_pass",
    )(feats, turned, weights, users)


def widen_kernel(narrow, later, wide):
    wide[...] = narrow[...].astype(f32)


def widen_pass(narrow, later):
    return pl.pallas_call(
        widen_kernel,
        out_shape=shape(*narrow.shape),
        in_specs=[VMEM, ANY],
        out_specs=VMEM,
        compiler_params=PARAMS,
        name="widen_pass",
    )(narrow, later)


def join_kernel(own, own_turned, other, both, turned):
    rows = other.shape[0]
    both[:rows, :] = own[...]
    both[rows:, :] = other[...].astype(bf16)
    turned[:, :rows] = own_turned[...]
    turned[:, rows:] = other[...].T.astype(bf16)


def join_pass(own, own_turned, other):
    rows, feat = own.shape
    return pl.pallas_call(
        join_kernel,
        out_shape=(shape(CORES * rows, feat, dtype=bf16), shape(feat, CORES * rows, dtype=bf16)),
        in_specs=[VMEM] * 3,
        out_specs=(VMEM, VMEM),
        compiler_params=PARAMS,
        cost_estimate=cost(rows * feat, 12 * rows * feat),
        name="join_pass",
    )(own, own_turned, other)


def part_kernel(devices, feats, part, mean):
    half = part.shape[0]
    bit = where_am_i(devices)[1]
    here = pl.ds(pl.multiple_of(bit * half, half), half)
    mean[...] = dot(feats[:, here], part[...].astype(bf16))


def part_pass(devices, feats, part):
    rows = feats.shape[0]
    half, width = part.shape
    return pl.pallas_call(
        functools.partial(part_kernel, devices),
        out_shape=shape(rows, width),
        in_specs=[VMEM, VMEM],
        out_specs=VMEM,
        compiler_params=PARAMS,
        cost_estimate=cost(2 * rows * half * width, 4 * rows * half),
        name="part_pass",
    )(feats, part)


def prior_kernel(places, devices, feats, turned, begun, part, got, own_cols, other_cols, own_mean, other_mean, send, keep, *refs):
    rows = own_cols.shape[0]
    half = keep.shape[0]
    place = where_am_i(devices)
    core, bit = place[0], place[1]
    here = pl.ds(pl.multiple_of(bit * half, half), half)
    there = pl.ds(pl.multiple_of((1 - bit) * half, half), half)
    offset = refs[-1]
    mean = begun[...] + dot(feats[:, there], got[...].astype(bf16))
    own_mean[...] = mean[:rows]
    other_mean[...] = mean[rows:]
    offset[:rows, :] = (own_cols[...] - mean[:rows]).astype(bf16)
    offset[rows:, :] = (other_cols[...] - mean[rows:]).astype(bf16)
    if places is None:
        send[...] = dot(turned[there, :], offset[...])
        keep[...] = dot(turned[here, :], offset[...])
        return
    old, full = refs[:2]
    full[here, :] = part[...]
    full[there, :] = got[...]
    start = place[-1] * old.shape[0]
    if old.shape[0] % 8 == 0:
        start = pl.multiple_of(start, old.shape[0])
    old[...] = full[pl.ds(start, old.shape[0]), :]
    full[...] = dot(turned[...], offset[...])
    blocks = len(places[0])
    block = 2 * half // blocks
    for ref, which in ((send, 1 - bit), (keep, bit)):
        for n in range(blocks // 2):
            source = jnp.int32(0)
            for c, order in enumerate(places):
                for b in range(2):
                    source = jnp.where((core == c) & (which == b), order[b * blocks // 2 + n], source)
            source = source * block
            if block % 8 == 0:
                source = pl.multiple_of(source, block)
            ref[n * block : (n + 1) * block, :] = full[pl.ds(source, block), :]


def prior_pass(devices, feats, turned, begun, part, got, own_cols, other_cols, places=None):
    rows, width = own_cols.shape
    half = part.shape[0]
    outs = [shape(rows, width)] * 2 + [shape(half, width)] * 2
    scratch = [pltpu.VMEM((CORES * rows, width), bf16)]
    if places is not None:
        outs.append(shape(2 * half // len(places[0]), width))
        scratch.insert(0, pltpu.VMEM((2 * half, width), f32))
    return pl.pallas_call(
        functools.partial(prior_kernel, places, devices),
        out_shape=tuple(outs),
        in_specs=[VMEM] * 7,
        out_specs=(VMEM,) * len(outs),
        scratch_shapes=scratch,
        compiler_params=PARAMS,
        cost_estimate=cost(16 * rows * half * width, 16 * rows * half),
        name="prior_pass",
    )(feats, turned, begun, part, got, own_cols, other_cols)


def step_kernel(halving, stage, under, devices, held, got, *refs):
    send = refs[-2] if halving else refs[-1]
    rows = send.shape[0] - under
    if halving:
        bit = where_am_i(devices)[1 + stage]
        for ref, which in ((send, 1 - bit), (refs[-1], bit)):
            at = rows_at(which, rows)
            ref[:rows, :] = held[at, :] + got[at, :]
    else:
        send[:rows, :] = held[:rows, :] + got[:rows, :]
    if under:
        sent, more = refs[:2]
        send[rows:, :] = sent[sent.shape[0] - under :, :] + more[more.shape[0] - under :, :]


def step_pass(halving, stage, devices, held, got, rows, riders=(), later=()):
    width = held.shape[1]
    under = RIDERS if riders else 0
    outs = [shape(rows // 2 + under, width), shape(rows // 2, width)] if halving else [shape(rows + under, width)]
    return pl.pallas_call(
        functools.partial(step_kernel, halving, stage, under, devices),
        out_shape=tuple(outs),
        in_specs=[VMEM] * (2 + len(riders)) + [ANY] * len(later),
        out_specs=(VMEM,) * len(outs),
        compiler_params=PARAMS,
        cost_estimate=cost(rows * width, 12 * rows * width),
        name="step_pass",
    )(held, got, *riders, *later)


def update_kernel(rate, held, got, sent, old, *refs):
    new, stats = refs[-2:]
    rows = old.shape[0]
    total = held[:rows, :] + got[:rows, :]
    before = old[...]
    new[...] = before + rate * (prior_prec * total - weight_decay * before)
    stats[...] = sent[sent.shape[0] - RIDERS :, :] + got[rows:, :]


def update_pass(rate, held, got, sent, old, later=()):
    return pl.pallas_call(
        functools.partial(update_kernel, rate),
        out_shape=(shape(*old.shape), shape(RIDERS, old.shape[1])),
        in_specs=[VMEM] * 4 + [ANY] * len(later),
        out_specs=(VMEM,) * 2,
        compiler_params=PARAMS,
        cost_estimate=cost(4 * old.size, 16 * old.size),
        name="update_pass",
    )(held, got, sent, old, *later)


def gather_kernel(slot, devices, part, got, *refs):
    both = refs[-1]
    rows = part.shape[0]
    bit = where_am_i(devices)[slot]
    both[pl.ds(pl.multiple_of(bit * rows, rows), rows), :] = part[...]
    both[pl.ds(pl.multiple_of((1 - bit) * rows, rows), rows), :] = got[...]


def gather_pass(stage, devices, part, got, later=()):
    rows, width = part.shape
    return pl.pallas_call(
        functools.partial(gather_kernel, 1 + stage, devices),
        out_shape=shape(2 * rows, width),
        in_specs=[VMEM, VMEM] + [ANY] * len(later),
        out_specs=VMEM,
        compiler_params=PARAMS,
        cost_estimate=cost(rows * width, 16 * rows * width),
        name="gather_pass",
    )(part, got, *later)


def split_kernel(devices, both, mine, other):
    place = where_am_i(devices)
    rows = mine.shape[0]
    for ref, which in ((mine, place[0]), (other, 1 - place[0])):
        at = pl.ds(pl.multiple_of(which * rows, 8), rows) if rows % 8 == 0 else pl.ds(which * rows, rows)
        ref[...] = both[at, :]


def split_pass(devices, both):
    rows, width = both.shape
    return pl.pallas_call(
        functools.partial(split_kernel, devices),
        out_shape=(shape(rows // CORES, width),) * 2,
        in_specs=[VMEM],
        out_specs=(VMEM,) * 2,
        compiler_params=PARAMS,
        name="split_pass",
    )(both)


def across_kernel(devices, mine, other, both):
    place = where_am_i(devices)
    width = mine.shape[1]
    both[:, pl.ds(pl.multiple_of(place[0] * width, width), width)] = mine[...]
    both[:, pl.ds(pl.multiple_of((1 - place[0]) * width, width), width)] = other[...]


def across_pass(devices, mine, other):
    rows, width = mine.shape
    return pl.pallas_call(
        functools.partial(across_kernel, devices),
        out_shape=shape(rows, CORES * width),
        in_specs=[VMEM, VMEM],
        out_specs=VMEM,
        compiler_params=PARAMS,
        name="across_pass",
    )(mine, other)


def renew_kernel(devices, stats, more, base_u, grad_u, own_mean, other_mean, base_v, grad_v, users, *outs):
    core = where_am_i(devices)[0]
    width = own_mean.shape[1]
    precision = precision_of(stats[...] + more[...])
    precision = jnp.concatenate([precision] * CORES, 1)
    parts = 1 if len(outs) == 1 else ITEM_PARTS
    rows = base_v.shape[0] // parts
    for n, items in enumerate(outs[:parts]):
        at = slice(n * rows, (n + 1) * rows)
        items[...] = base_v[at, :] + precision * grad_v[at, :]
    new = base_u[...] + precision * grad_u[...]
    pull = step_size * prior_prec
    left = jnp.where(core == 0, own_mean[...], other_mean[...])
    right = jnp.where(core == 0, other_mean[...], own_mean[...])
    users[:, :width] = new[:, :width] + pull * left
    users[:, width:] = new[:, width:] + pull * right
    for ref, which in zip(outs[parts:], (core, 1 - core), strict=False):
        ref[...] = half_of(users, which)


def renew_pass(devices, last, stats, more, base_u, grad_u, own_mean, *state):
    rows, rank = base_u.shape
    outs = [shape(rows, rank)]
    if last:
        outs.append(shape(rows, rank))
    else:
        outs += [shape(rows // ITEM_PARTS, rank)] * ITEM_PARTS + [shape(*own_mean.shape)] * 2
    return pl.pallas_call(
        functools.partial(renew_kernel, devices),
        out_shape=tuple(outs),
        in_specs=[VMEM] * 8,
        out_specs=(VMEM,) * len(outs),
        compiler_params=PARAMS,
        cost_estimate=cost(8 * base_u.size, 32 * base_u.size),
        name="renew_pass",
    )(stats, more, base_u, grad_u, own_mean, *state)


def bit_order(devices, core):
    bits = devices.bit_length() - 1
    far = list(range(3, bits))
    return [1, 2] + far if core == 0 else [2, 1] + far[::-1]


def swap(array, devices):
    return lax.ppermute(array, "user", [(i, i ^ 1) for i in range(devices)])


def roll(array, devices):
    return lax.ppermute(array, "user", [(i, (i + 1) % devices) for i in range(devices)])


def exchange(array, devices, stage):
    orders = [bit_order(devices, core) for core in range(CORES)]
    pairs = [(i, i ^ (1 << orders[i & 1][stage])) for i in range(devices)]
    return lax.ppermute(array, "user", pairs)


def final_places(devices):
    bits = devices.bit_length() - 1
    return [
        [
            sum(
                ((place >> (bits - 2 - n)) & 1) << (bit - 1)
                for n, bit in enumerate(bit_order(devices, core))
            )
            for place in range(devices // 2)
        ]
        for core in range(CORES)
    ]


def local(
    ratings,
    tile_index,
    tile_count,
    side_features,
    user_factors,
    item_factors,
    prior_weights,
    user_noise,
    item_noise,
):
    devices = lax.axis_size("user")
    stages = devices.bit_length() - 2
    strata = ratings.shape[1]
    feat = prior_weights.shape[0]
    rate = rate_scale / (user_factors.shape[0] * devices)
    own_turned = turn_pass(side_features)
    own_mean, other_mean, send, held, old = first_pass(
        devices, side_features, own_turned, prior_weights, user_factors
    )
    send, held = step_pass(True, 0, devices, held, swap(send, devices), feat)
    users, items = user_factors, [item_factors]
    for stratum in range(strata):
        last = stratum + 1 == strata
        got = exchange(send, devices, 0)
        later = send if stratum else own_turned
        err_b, stats = error_pass(stratum, tile_index, tile_count, ratings, users, later, *items)
        state = grad_pass(stratum, err_b, user_noise, item_noise, users, *items)
        riders = (stats, exchange(stats, devices, 0))
        send, held = step_pass(True, 1, devices, held, got, got.shape[0], riders)
        if stratum == 0:
            wide = swap(widen_pass(side_features, state[0]), devices)
            feats, turned = join_pass(side_features, own_turned, wide)
        for stage in range(1, stages - 1):
            got = exchange(send, devices, stage)
            rows = got.shape[0] - RIDERS
            later = state[:1] if stage == 1 else ()
            if last:
                send, held = step_pass(True, stage + 1, devices, held, got, rows, (send, got), later)
            else:
                (send,) = step_pass(False, 0, devices, held, got, rows, (send, got), later)
                held = send
        got = exchange(send, devices, stages - 1)
        part, stats = update_pass(rate, held, got, send, old)
        users, *items = renew_pass(
            devices, last, stats, swap(stats, devices), *state[:2], own_mean, other_mean, *state[2:]
        )
        if last:
            break
        old = part
        *items, own_cols, other_cols = items
        items = [roll(rows, devices) for rows in items]
        other_cols = swap(other_cols, devices)
        part = gather_pass(1, devices, part, exchange(part, devices, 1), [users])
        got = exchange(part, devices, 0)
        begun = part_pass(devices, feats, part)
        own_mean, other_mean, send, held, *olds = prior_pass(
            devices,
            feats,
            turned,
            begun,
            part,
            got,
            own_cols,
            other_cols,
            final_places(devices) if stratum + 2 == strata else None,
        )
        if olds:
            (old,) = olds
        other_mean = swap(other_mean, devices)
    mine, other = split_pass(devices, part)
    return (users, *items, across_pass(devices, mine, swap(other, devices)))


def solution(mesh):
    return jax.shard_map(
        local,
        mesh=mesh,
        in_specs=(
            P("user", None, None, None, None),
            P("user", None, None),
            P("user", None),
            P("user", None),
            P("user", None),
            P("user", None),
            P(),
            P(None, "user", None),
            P(None, "user", None),
        ),
        out_specs=(P("user", None), P("user", None), P("user", None)),
        check_vma=False,
    )
```

```python
import functools
import math

import jax
import jax.numpy as jnp
from jax import lax
from jax.experimental import pallas as pl
from jax.experimental.pallas import tpu as pltpu
from jax.sharding import PartitionSpec as P

step_size = 0.01
prior_prec = 8.0
item_prec = 1.0
weight_decay = 1.0
rate_scale = 0.04

CORES = 2
RIDERS = 8
ITEM_PARTS = 1
NN = (((1,), (0,)), ((), ()))
NT = (((1,), (1,)), ((), ()))
TN = (((0,), (0,)), ((), ()))
VMEM = pl.BlockSpec(memory_space=pltpu.VMEM)
SMEM = pl.BlockSpec(memory_space=pltpu.SMEM)
ANY = pl.BlockSpec(memory_space=pl.ANY)
PARAMS = pltpu.CompilerParams(vmem_limit_bytes=8 << 20)
f32 = jnp.float32
bf16 = jnp.bfloat16


def dot(a, b, dims=NN):
    return lax.dot_general(a, b, dims, preferred_element_type=f32)


def shape(*dims, dtype=f32):
    return jax.ShapeDtypeStruct(dims, dtype)


def cost(flops, size):
    return pl.CostEstimate(flops=flops, bytes_accessed=size, transcendentals=0)


def where_am_i(devices):
    own = lax.axis_index("user")
    core = own & 1
    zero, one = (bit_order(devices, c) for c in range(CORES))
    bits = [jnp.where(core == 0, own >> z, own >> o) & 1 for z, o in zip(zero, one, strict=True)]
    return [core, *bits, own >> 1]


def rows_at(which, rows):
    start = which * rows
    return pl.ds(pl.multiple_of(start, rows) if rows % 8 == 0 else start, rows)


def half_of(ref, core):
    width = ref.shape[1] // CORES
    return ref[:, pl.ds(pl.multiple_of(core * width, width), width)]


def precision_of(stats):
    return (1.0 + stats[1:2, :] / 2.0) / (1.0 + stats[0:1, :] / 2.0)


def error_kernel(stratum, codes, count, ratings, users, *refs):
    items, (err_b, stats, pred) = refs[:-3], refs[-3:]
    tile = ratings.shape[-1]
    grid = users.shape[0] // tile
    user_b = users[...].astype(bf16)
    start = 0
    for part in items:
        pred[:, start : start + part.shape[0]] = dot(user_b, part[...].astype(bf16), NT)
        start += part.shape[0]
    err_b[...] = jnp.zeros_like(err_b)
    live_slots = count[0, stratum]
    sse = jnp.zeros((tile, tile), f32)
    for slot in range(ratings.shape[2]):
        code = codes[0, stratum, slot]
        at_rows = rows_at(code // grid, tile)
        at_cols = rows_at(code % grid, tile)
        live = (slot < live_slots).astype(f32)
        err = (ratings[0, stratum, slot].astype(f32) - pred[at_rows, at_cols]) * live
        sse = sse + err * err
        err_b[at_rows, at_cols] = err.astype(bf16)
    total = jnp.sum(sse)
    counted = live_slots.astype(f32) * float(tile * tile)
    row = lax.broadcasted_iota(jnp.int32, stats.shape, 0)
    stats[...] = jnp.where(row == 0, total, jnp.where(row == 1, counted, 0.0))


def error_pass(stratum, codes, count, ratings, users, *items):
    rows, rank = users.shape
    return pl.pallas_call(
        functools.partial(error_kernel, stratum),
        out_shape=(shape(rows, rows, dtype=bf16), shape(RIDERS, rank // CORES)),
        in_specs=[SMEM] * 2 + [VMEM] * (2 + len(items)),
        out_specs=(VMEM,) * 2,
        scratch_shapes=[pltpu.VMEM((rows, rows), f32)],
        compiler_params=PARAMS,
        cost_estimate=cost(24 * rows * rows * rank, 64 * rows * rank),
        name="error_pass",
    )(codes, count, ratings, users, *items)


def grad_kernel(stratum, noise_scale, err_b, user_noise, item_noise, users, *refs):
    items, (base_u, grad_u, base_v, grad_v) = refs[:-4], refs[-4:]
    item_b = jnp.concatenate([part[...].astype(bf16) for part in items], 0)
    grad_u[...] = step_size * dot(err_b[...], item_b)
    grad_v[...] = step_size * dot(err_b[...], users[...].astype(bf16), TN)
    noise = noise_scale * user_noise[stratum].astype(f32)
    base_u[...] = (1.0 - step_size * prior_prec) * users[...] + noise
    start = 0
    for part in items:
        at = slice(start, start + part.shape[0])
        noise = noise_scale * item_noise[stratum, at].astype(f32)
        base_v[at, :] = (1.0 - step_size * item_prec) * part[...] + noise
        start += part.shape[0]


def grad_pass(stratum, err_b, user_noise, item_noise, users, *items):
    rows, rank = users.shape
    return pl.pallas_call(
        functools.partial(grad_kernel, stratum, math.sqrt(2.0 * step_size)),
        out_shape=(shape(rows, rank),) * 4,
        in_specs=[VMEM] * (4 + len(items)),
        out_specs=(VMEM,) * 4,
        compiler_params=PARAMS,
        cost_estimate=cost(4 * rows * rows * rank, 28 * rows * rank),
        name="grad_pass",
    )(err_b, user_noise, item_noise, users, *items)


def turn_kernel(feats, turned):
    turned[...] = feats[...].T


def turn_pass(feats):
    rows, feat = feats.shape
    return pl.pallas_call(
        turn_kernel,
        out_shape=shape(feat, rows, dtype=bf16),
        in_specs=[VMEM],
        out_specs=VMEM,
        compiler_params=PARAMS,
        cost_estimate=cost(rows * feat, 4 * rows * feat),
        name="turn_pass",
    )(feats)


def first_kernel(devices, feats, turned, weights, users, own_mean, other_mean, send, keep, old, mean):
    place = where_am_i(devices)
    here = place[0]
    mean[...] = dot(feats[...], weights[...].astype(bf16))
    for grad, means, which in ((send, other_mean, 1 - here), (keep, own_mean, here)):
        mean_now = half_of(mean, which)
        means[...] = mean_now
        offset = (half_of(users, which) - mean_now).astype(bf16)
        grad[...] = dot(turned[...], offset)
    rows, width = old.shape
    old[...] = weights[rows_at(2 * place[1] + place[2], rows), rows_at(here, width)]


def first_pass(devices, feats, turned, weights, users):
    rows, rank = users.shape
    feat = weights.shape[0]
    width = rank // CORES
    return pl.pallas_call(
        functools.partial(first_kernel, devices),
        out_shape=(shape(rows, width),) * 2 + (shape(feat, width),) * 2 + (shape(feat // 4, width),),
        in_specs=[VMEM] * 4,
        out_specs=(VMEM,) * 5,
        scratch_shapes=[pltpu.VMEM(users.shape, f32)],
        compiler_params=PARAMS,
        cost_estimate=cost(4 * rows * feat * rank, 8 * feat * rank),
        name="first_pass",
    )(feats, turned, weights, users)


def widen_kernel(narrow, later, wide):
    wide[...] = narrow[...].astype(f32)


def widen_pass(narrow, later):
    return pl.pallas_call(
        widen_kernel,
        out_shape=shape(*narrow.shape),
        in_specs=[VMEM, ANY],
        out_specs=VMEM,
        compiler_params=PARAMS,
        name="widen_pass",
    )(narrow, later)


def join_kernel(own, own_turned, other, both, turned):
    rows = other.shape[0]
    both[:rows, :] = own[...]
    both[rows:, :] = other[...].astype(bf16)
    turned[:, :rows] = own_turned[...]
    turned[:, rows:] = other[...].T.astype(bf16)


def join_pass(own, own_turned, other):
    rows, feat = own.shape
    return pl.pallas_call(
        join_kernel,
        out_shape=(shape(CORES * rows, feat, dtype=bf16), shape(feat, CORES * rows, dtype=bf16)),
        in_specs=[VMEM] * 3,
        out_specs=(VMEM, VMEM),
        compiler_params=PARAMS,
        cost_estimate=cost(rows * feat, 12 * rows * feat),
        name="join_pass",
    )(own, own_turned, other)


def part_kernel(devices, feats, part, mean):
    half = part.shape[0]
    bit = where_am_i(devices)[1]
    here = pl.ds(pl.multiple_of(bit * half, half), half)
    mean[...] = dot(feats[:, here], part[...].astype(bf16))


def part_pass(devices, feats, part):
    rows = feats.shape[0]
    half, width = part.shape
    return pl.pallas_call(
        functools.partial(part_kernel, devices),
        out_shape=shape(rows, width),
        in_specs=[VMEM, VMEM],
        out_specs=VMEM,
        compiler_params=PARAMS,
        cost_estimate=cost(2 * rows * half * width, 4 * rows * half),
        name="part_pass",
    )(feats, part)


def prior_kernel(places, devices, feats, turned, begun, part, got, own_cols, other_cols, stats, more_stats, own_mean, other_mean, send, keep, *refs):
    rows = own_cols.shape[0]
    half = keep.shape[0]
    place = where_am_i(devices)
    core, bit = place[0], place[1]
    here = pl.ds(pl.multiple_of(bit * half, half), half)
    there = pl.ds(pl.multiple_of((1 - bit) * half, half), half)
    offset = refs[-1]
    mean = begun[...] + dot(feats[:, there], got[...].astype(bf16))
    own_mean[...] = mean[:rows]
    other_mean[...] = mean[rows:]
    offset[:rows, :] = (own_cols[...] - mean[:rows]).astype(bf16)
    offset[rows:, :] = (other_cols[...] - mean[rows:]).astype(bf16)
    send[half:, :] = stats[...] + more_stats[...]
    if places is None:
        send[:half, :] = dot(turned[there, :], offset[...])
        keep[...] = dot(turned[here, :], offset[...])
        return
    old, full = refs[:2]
    full[here, :] = part[...]
    full[there, :] = got[...]
    start = place[-1] * old.shape[0]
    if old.shape[0] % 8 == 0:
        start = pl.multiple_of(start, old.shape[0])
    old[...] = full[pl.ds(start, old.shape[0]), :]
    full[...] = dot(turned[...], offset[...])
    blocks = len(places[0])
    block = 2 * half // blocks
    for ref, which in ((send, 1 - bit), (keep, bit)):
        for n in range(blocks // 2):
            source = jnp.int32(0)
            for c, order in enumerate(places):
                for b in range(2):
                    source = jnp.where((core == c) & (which == b), order[b * blocks // 2 + n], source)
            source = source * block
            if block % 8 == 0:
                source = pl.multiple_of(source, block)
            ref[n * block : (n + 1) * block, :] = full[pl.ds(source, block), :]


def prior_pass(devices, feats, turned, begun, part, got, own_cols, other_cols, stats, more_stats, places=None):
    rows, width = own_cols.shape
    half = part.shape[0]
    outs = [shape(rows, width)] * 2 + [shape(half + RIDERS, width), shape(half, width)]
    scratch = [pltpu.VMEM((CORES * rows, width), bf16)]
    if places is not None:
        outs.append(shape(2 * half // len(places[0]), width))
        scratch.insert(0, pltpu.VMEM((2 * half, width), f32))
    return pl.pallas_call(
        functools.partial(prior_kernel, places, devices),
        out_shape=tuple(outs),
        in_specs=[VMEM] * 9,
        out_specs=(VMEM,) * len(outs),
        scratch_shapes=scratch,
        compiler_params=PARAMS,
        cost_estimate=cost(16 * rows * half * width, 16 * rows * half),
        name="prior_pass",
    )(feats, turned, begun, part, got, own_cols, other_cols, stats, more_stats)


def step_kernel(halving, stage, under, apart, devices, held, got, *refs):
    outs = refs[-(1 + halving + apart) :]
    send = outs[0]
    rows = send.shape[0] - (0 if apart else under)
    if halving:
        bit = where_am_i(devices)[1 + stage]
        for ref, which in ((send, 1 - bit), (outs[1], bit)):
            at = rows_at(which, rows)
            ref[:rows, :] = held[at, :] + got[at, :]
    else:
        send[:rows, :] = held[:rows, :] + got[:rows, :]
    if under:
        sent, more = refs[:2]
        rider = sent[sent.shape[0] - under :, :] + more[more.shape[0] - under :, :]
        if apart:
            outs[-1][...] = rider
        else:
            send[rows:, :] = rider


def step_pass(halving, stage, devices, held, got, rows, riders=(), later=(), apart=False):
    width = held.shape[1]
    under = RIDERS if riders else 0
    below = 0 if apart else under
    outs = [shape(rows // 2 + below, width), shape(rows // 2, width)] if halving else [shape(rows + below, width)]
    if apart:
        outs.append(shape(RIDERS, width))
    return pl.pallas_call(
        functools.partial(step_kernel, halving, stage, under, apart, devices),
        out_shape=tuple(outs),
        in_specs=[VMEM] * (2 + len(riders)) + [ANY] * len(later),
        out_specs=(VMEM,) * len(outs),
        compiler_params=PARAMS,
        cost_estimate=cost(rows * width, 12 * rows * width),
        name="step_pass",
    )(held, got, *riders, *later)


def update_kernel(rate, held, got, old, new):
    rows = old.shape[0]
    total = held[:rows, :] + got[...]
    before = old[...]
    new[...] = before + rate * (prior_prec * total - weight_decay * before)


def update_pass(rate, held, got, old):
    return pl.pallas_call(
        functools.partial(update_kernel, rate),
        out_shape=shape(*old.shape),
        in_specs=[VMEM] * 3,
        out_specs=VMEM,
        compiler_params=PARAMS,
        cost_estimate=cost(4 * old.size, 16 * old.size),
        name="update_pass",
    )(held, got, old)


def gather_kernel(slot, devices, part, got, *refs):
    both = refs[-1]
    rows = part.shape[0]
    bit = where_am_i(devices)[slot]
    both[pl.ds(pl.multiple_of(bit * rows, rows), rows), :] = part[...]
    both[pl.ds(pl.multiple_of((1 - bit) * rows, rows), rows), :] = got[...]


def gather_pass(stage, devices, part, got, later=()):
    rows, width = part.shape
    return pl.pallas_call(
        functools.partial(gather_kernel, 1 + stage, devices),
        out_shape=shape(2 * rows, width),
        in_specs=[VMEM, VMEM] + [ANY] * len(later),
        out_specs=VMEM,
        compiler_params=PARAMS,
        cost_estimate=cost(rows * width, 16 * rows * width),
        name="gather_pass",
    )(part, got, *later)


def split_kernel(devices, both, mine, other):
    place = where_am_i(devices)
    rows = mine.shape[0]
    for ref, which in ((mine, place[0]), (other, 1 - place[0])):
        at = pl.ds(pl.multiple_of(which * rows, 8), rows) if rows % 8 == 0 else pl.ds(which * rows, rows)
        ref[...] = both[at, :]


def split_pass(devices, both):
    rows, width = both.shape
    return pl.pallas_call(
        functools.partial(split_kernel, devices),
        out_shape=(shape(rows // CORES, width),) * 2,
        in_specs=[VMEM],
        out_specs=(VMEM,) * 2,
        compiler_params=PARAMS,
        name="split_pass",
    )(both)


def across_kernel(devices, mine, other, both):
    place = where_am_i(devices)
    width = mine.shape[1]
    both[:, pl.ds(pl.multiple_of(place[0] * width, width), width)] = mine[...]
    both[:, pl.ds(pl.multiple_of((1 - place[0]) * width, width), width)] = other[...]


def across_pass(devices, mine, other):
    rows, width = mine.shape
    return pl.pallas_call(
        functools.partial(across_kernel, devices),
        out_shape=shape(rows, CORES * width),
        in_specs=[VMEM, VMEM],
        out_specs=VMEM,
        compiler_params=PARAMS,
        name="across_pass",
    )(mine, other)


def renew_kernel(devices, stats, base_u, grad_u, own_mean, other_mean, base_v, grad_v, users, *outs):
    core = where_am_i(devices)[0]
    width = own_mean.shape[1]
    precision = precision_of(stats[...])
    precision = jnp.concatenate([precision] * CORES, 1)
    parts = 1 if len(outs) == 1 else ITEM_PARTS
    rows = base_v.shape[0] // parts
    for n, items in enumerate(outs[:parts]):
        at = slice(n * rows, (n + 1) * rows)
        items[...] = base_v[at, :] + precision * grad_v[at, :]
    new = base_u[...] + precision * grad_u[...]
    pull = step_size * prior_prec
    left = jnp.where(core == 0, own_mean[...], other_mean[...])
    right = jnp.where(core == 0, other_mean[...], own_mean[...])
    users[:, :width] = new[:, :width] + pull * left
    users[:, width:] = new[:, width:] + pull * right
    for ref, which in zip(outs[parts:], (core, 1 - core), strict=False):
        ref[...] = half_of(users, which)


def renew_pass(devices, last, stats, base_u, grad_u, own_mean, *state):
    rows, rank = base_u.shape
    outs = [shape(rows, rank)]
    if last:
        outs.append(shape(rows, rank))
    else:
        outs += [shape(rows // ITEM_PARTS, rank)] * ITEM_PARTS + [shape(*own_mean.shape)] * 2
    return pl.pallas_call(
        functools.partial(renew_kernel, devices),
        out_shape=tuple(outs),
        in_specs=[VMEM] * 7,
        out_specs=(VMEM,) * len(outs),
        compiler_params=PARAMS,
        cost_estimate=cost(8 * base_u.size, 32 * base_u.size),
        name="renew_pass",
    )(stats, base_u, grad_u, own_mean, *state)


def bit_order(devices, core):
    bits = devices.bit_length() - 1
    far = list(range(3, bits))
    return [1, 2] + far if core == 0 else [2, 1] + far[::-1]


def swap(array, devices):
    return lax.ppermute(array, "user", [(i, i ^ 1) for i in range(devices)])


def roll(array, devices):
    return lax.ppermute(array, "user", [(i, (i + 1) % devices) for i in range(devices)])


def exchange(array, devices, stage):
    orders = [bit_order(devices, core) for core in range(CORES)]
    pairs = [(i, i ^ (1 << orders[i & 1][stage])) for i in range(devices)]
    return lax.ppermute(array, "user", pairs)


def final_places(devices):
    bits = devices.bit_length() - 1
    return [
        [
            sum(
                ((place >> (bits - 2 - n)) & 1) << (bit - 1)
                for n, bit in enumerate(bit_order(devices, core))
            )
            for place in range(devices // 2)
        ]
        for core in range(CORES)
    ]


def local(
    ratings,
    tile_index,
    tile_count,
    side_features,
    user_factors,
    item_factors,
    prior_weights,
    user_noise,
    item_noise,
):
    devices = lax.axis_size("user")
    stages = devices.bit_length() - 2
    strata = ratings.shape[1]
    feat = prior_weights.shape[0]
    rate = rate_scale / (user_factors.shape[0] * devices)
    def errors_of(stratum, users, *items):
        err_b, stats = error_pass(stratum, tile_index, tile_count, ratings, users, *items)
        stats = stats + swap(stats, devices)
        return err_b, (stats, exchange(stats, devices, stages - 1))

    users, items = user_factors, [item_factors]
    err_b, riders = errors_of(0, users, *items)
    own_turned = turn_pass(side_features)
    own_mean, other_mean, send, held, old = first_pass(
        devices, side_features, own_turned, prior_weights, user_factors
    )
    send, held = step_pass(True, 0, devices, held, swap(send, devices), feat, (), riders[:1])
    for stratum in range(strata):
        last = stratum + 1 == strata
        state = grad_pass(stratum, err_b, user_noise, item_noise, users, *items)
        got = exchange(send, devices, 0)
        if stratum:
            riders = send, got
        else:
            stats = riders[0] + riders[1]
            riders = stats, exchange(stats, devices, 0)
        send, held = step_pass(True, 1, devices, held, got, feat // 2, riders, state[:1])
        if stratum == 0:
            wide = swap(widen_pass(side_features, send), devices)
            feats, turned = join_pass(side_features, own_turned, wide)
        for stage in range(1, stages - 1):
            got = exchange(send, devices, stage)
            rows = got.shape[0] - RIDERS
            apart = stage == stages - 2
            outs = step_pass(last, stage + 1, devices, held, got, rows, (send, got), (), apart)
            send, held = outs[0], outs[1 if last else 0]
        stats = outs[-1]
        got = exchange(send, devices, stages - 1)
        users, *items = renew_pass(devices, last, stats, *state[:2], own_mean, other_mean, *state[2:])
        part = update_pass(rate, held, got, old)
        if last:
            break
        old = part
        *items, own_cols, other_cols = items
        items = [roll(rows, devices) for rows in items]
        other_cols = swap(other_cols, devices)
        part = gather_pass(1, devices, part, exchange(part, devices, 1))
        got = exchange(part, devices, 0)
        err_b, riders = errors_of(stratum + 1, users, *items)
        begun = part_pass(devices, feats, part)
        own_mean, other_mean, send, held, *olds = prior_pass(
            devices,
            feats,
            turned,
            begun,
            part,
            got,
            own_cols,
            other_cols,
            *riders,
            final_places(devices) if stratum + 2 == strata else None,
        )
        if olds:
            (old,) = olds
        other_mean = swap(other_mean, devices)
    mine, other = split_pass(devices, part)
    return (users, *items, across_pass(devices, mine, swap(other, devices)))


def solution(mesh):
    return jax.shard_map(
        local,
        mesh=mesh,
        in_specs=(
            P("user", None, None, None, None),
            P("user", None, None),
            P("user", None),
            P("user", None),
            P("user", None),
            P("user", None),
            P(),
            P(None, "user", None),
            P(None, "user", None),
        ),
        out_specs=(P("user", None), P("user", None), P("user", None)),
        check_vma=False,
    )
```

```python
import functools
import math

import jax
import jax.numpy as jnp
from jax import lax
from jax.experimental import pallas as pl
from jax.experimental.pallas import tpu as pltpu
from jax.sharding import PartitionSpec as P

step_size = 0.01
prior_prec = 8.0
item_prec = 1.0
weight_decay = 1.0
rate_scale = 0.04

CORES = 2
RIDERS = 8
ITEM_PARTS = 1
NN = (((1,), (0,)), ((), ()))
NT = (((1,), (1,)), ((), ()))
TN = (((0,), (0,)), ((), ()))
VMEM = pl.BlockSpec(memory_space=pltpu.VMEM)
SMEM = pl.BlockSpec(memory_space=pltpu.SMEM)
ANY = pl.BlockSpec(memory_space=pl.ANY)
PARAMS = pltpu.CompilerParams(vmem_limit_bytes=8 << 20)
f32 = jnp.float32
bf16 = jnp.bfloat16


def dot(a, b, dims=NN):
    return lax.dot_general(a, b, dims, preferred_element_type=f32)


def shape(*dims, dtype=f32):
    return jax.ShapeDtypeStruct(dims, dtype)


def cost(flops, size):
    return pl.CostEstimate(flops=flops, bytes_accessed=size, transcendentals=0)


def where_am_i(devices):
    own = lax.axis_index("user")
    core = own & 1
    zero, one = (bit_order(devices, c) for c in range(CORES))
    bits = [jnp.where(core == 0, own >> z, own >> o) & 1 for z, o in zip(zero, one, strict=True)]
    return [core, *bits, own >> 1]


def rows_at(which, rows):
    start = which * rows
    return pl.ds(pl.multiple_of(start, rows) if rows % 8 == 0 else start, rows)


def half_of(ref, core):
    width = ref.shape[1] // CORES
    return ref[:, pl.ds(pl.multiple_of(core * width, width), width)]


def precision_of(stats):
    return (1.0 + stats[1:2, :] / 2.0) / (1.0 + stats[0:1, :] / 2.0)


def error_kernel(stratum, codes, count, ratings, users, *refs):
    items, (err_b, stats, pred) = refs[1:-3], refs[-3:]
    tile = ratings.shape[-1]
    grid = users.shape[0] // tile
    user_b = users[...].astype(bf16)
    start = 0
    for part in items:
        pred[:, start : start + part.shape[0]] = dot(user_b, part[...].astype(bf16), NT)
        start += part.shape[0]
    err_b[...] = jnp.zeros_like(err_b)
    live_slots = count[0, stratum]
    sse = jnp.zeros((tile, tile), f32)
    for slot in range(ratings.shape[2]):
        code = codes[0, stratum, slot]
        at_rows = rows_at(code // grid, tile)
        at_cols = rows_at(code % grid, tile)
        live = (slot < live_slots).astype(f32)
        err = (ratings[0, stratum, slot].astype(f32) - pred[at_rows, at_cols]) * live
        sse = sse + err * err
        err_b[at_rows, at_cols] = err.astype(bf16)
    total = jnp.sum(sse)
    counted = live_slots.astype(f32) * float(tile * tile)
    row = lax.broadcasted_iota(jnp.int32, stats.shape, 0)
    stats[...] = jnp.where(row == 0, total, jnp.where(row == 1, counted, 0.0))


def error_pass(stratum, codes, count, ratings, users, later, *items):
    rows, rank = users.shape
    return pl.pallas_call(
        functools.partial(error_kernel, stratum),
        out_shape=(shape(rows, rows, dtype=bf16), shape(RIDERS, rank // CORES)),
        in_specs=[SMEM] * 2 + [VMEM] * 2 + [ANY] + [VMEM] * len(items),
        out_specs=(VMEM,) * 2,
        scratch_shapes=[pltpu.VMEM((rows, rows), f32)],
        compiler_params=PARAMS,
        cost_estimate=cost(24 * rows * rows * rank, 64 * rows * rank),
        name="error_pass",
    )(codes, count, ratings, users, later, *items)


def grad_kernel(stratum, noise_scale, err_b, user_noise, item_noise, users, *refs):
    items, (base_u, grad_u, base_v, grad_v) = refs[:-4], refs[-4:]
    item_b = jnp.concatenate([part[...].astype(bf16) for part in items], 0)
    grad_u[...] = step_size * dot(err_b[...], item_b)
    grad_v[...] = step_size * dot(err_b[...], users[...].astype(bf16), TN)
    noise = noise_scale * user_noise[stratum].astype(f32)
    base_u[...] = (1.0 - step_size * prior_prec) * users[...] + noise
    start = 0
    for part in items:
        at = slice(start, start + part.shape[0])
        noise = noise_scale * item_noise[stratum, at].astype(f32)
        base_v[at, :] = (1.0 - step_size * item_prec) * part[...] + noise
        start += part.shape[0]


def grad_pass(stratum, err_b, user_noise, item_noise, users, *items):
    rows, rank = users.shape
    return pl.pallas_call(
        functools.partial(grad_kernel, stratum, math.sqrt(2.0 * step_size)),
        out_shape=(shape(rows, rank),) * 4,
        in_specs=[VMEM] * (4 + len(items)),
        out_specs=(VMEM,) * 4,
        compiler_params=PARAMS,
        cost_estimate=cost(4 * rows * rows * rank, 28 * rows * rank),
        name="grad_pass",
    )(err_b, user_noise, item_noise, users, *items)


def turn_kernel(feats, turned):
    turned[...] = feats[...].T


def turn_pass(feats):
    rows, feat = feats.shape
    return pl.pallas_call(
        turn_kernel,
        out_shape=shape(feat, rows, dtype=bf16),
        in_specs=[VMEM],
        out_specs=VMEM,
        compiler_params=PARAMS,
        cost_estimate=cost(rows * feat, 4 * rows * feat),
        name="turn_pass",
    )(feats)


def first_kernel(devices, feats, turned, weights, users, own_mean, other_mean, send, keep, old, mean):
    place = where_am_i(devices)
    here = place[0]
    mean[...] = dot(feats[...], weights[...].astype(bf16))
    for grad, means, which in ((send, other_mean, 1 - here), (keep, own_mean, here)):
        mean_now = half_of(mean, which)
        means[...] = mean_now
        offset = (half_of(users, which) - mean_now).astype(bf16)
        grad[...] = dot(turned[...], offset)
    rows, width = old.shape
    old[...] = weights[rows_at(2 * place[1] + place[2], rows), rows_at(here, width)]


def first_pass(devices, feats, turned, weights, users):
    rows, rank = users.shape
    feat = weights.shape[0]
    width = rank // CORES
    return pl.pallas_call(
        functools.partial(first_kernel, devices),
        out_shape=(shape(rows, width),) * 2 + (shape(feat, width),) * 2 + (shape(feat // 4, width),),
        in_specs=[VMEM] * 4,
        out_specs=(VMEM,) * 5,
        scratch_shapes=[pltpu.VMEM(users.shape, f32)],
        compiler_params=PARAMS,
        cost_estimate=cost(4 * rows * feat * rank, 8 * feat * rank),
        name="first_pass",
    )(feats, turned, weights, users)


def widen_kernel(narrow, later, wide):
    wide[...] = narrow[...].astype(f32)


def widen_pass(narrow, later):
    return pl.pallas_call(
        widen_kernel,
        out_shape=shape(*narrow.shape),
        in_specs=[VMEM, ANY],
        out_specs=VMEM,
        compiler_params=PARAMS,
        name="widen_pass",
    )(narrow, later)


def join_kernel(own, own_turned, other, both, turned):
    rows = other.shape[0]
    both[:rows, :] = own[...]
    both[rows:, :] = other[...].astype(bf16)
    turned[:, :rows] = own_turned[...]
    turned[:, rows:] = other[...].T.astype(bf16)


def join_pass(own, own_turned, other):
    rows, feat = own.shape
    return pl.pallas_call(
        join_kernel,
        out_shape=(shape(CORES * rows, feat, dtype=bf16), shape(feat, CORES * rows, dtype=bf16)),
        in_specs=[VMEM] * 3,
        out_specs=(VMEM, VMEM),
        compiler_params=PARAMS,
        cost_estimate=cost(rows * feat, 12 * rows * feat),
        name="join_pass",
    )(own, own_turned, other)


def part_kernel(devices, feats, part, mean):
    half = part.shape[0]
    bit = where_am_i(devices)[1]
    here = pl.ds(pl.multiple_of(bit * half, half), half)
    mean[...] = dot(feats[:, here], part[...].astype(bf16))


def part_pass(devices, feats, part):
    rows = feats.shape[0]
    half, width = part.shape
    return pl.pallas_call(
        functools.partial(part_kernel, devices),
        out_shape=shape(rows, width),
        in_specs=[VMEM, VMEM],
        out_specs=VMEM,
        compiler_params=PARAMS,
        cost_estimate=cost(2 * rows * half * width, 4 * rows * half),
        name="part_pass",
    )(feats, part)


def prior_kernel(places, devices, feats, turned, begun, part, got, own_cols, other_cols, later, own_mean, other_mean, send, keep, *refs):
    rows = own_cols.shape[0]
    half = keep.shape[0]
    place = where_am_i(devices)
    core, bit = place[0], place[1]
    here = pl.ds(pl.multiple_of(bit * half, half), half)
    there = pl.ds(pl.multiple_of((1 - bit) * half, half), half)
    offset = refs[-1]
    mean = begun[...] + dot(feats[:, there], got[...].astype(bf16))
    own_mean[...] = mean[:rows]
    other_mean[...] = mean[rows:]
    offset[:rows, :] = (own_cols[...] - mean[:rows]).astype(bf16)
    offset[rows:, :] = (other_cols[...] - mean[rows:]).astype(bf16)
    if places is None:
        send[...] = dot(turned[there, :], offset[...])
        keep[...] = dot(turned[here, :], offset[...])
        return
    old, full = refs[:2]
    full[here, :] = part[...]
    full[there, :] = got[...]
    start = place[-1] * old.shape[0]
    if old.shape[0] % 8 == 0:
        start = pl.multiple_of(start, old.shape[0])
    old[...] = full[pl.ds(start, old.shape[0]), :]
    full[...] = dot(turned[...], offset[...])
    blocks = len(places[0])
    block = 2 * half // blocks
    for ref, which in ((send, 1 - bit), (keep, bit)):
        for n in range(blocks // 2):
            source = jnp.int32(0)
            for c, order in enumerate(places):
                for b in range(2):
                    source = jnp.where((core == c) & (which == b), order[b * blocks // 2 + n], source)
            source = source * block
            if block % 8 == 0:
                source = pl.multiple_of(source, block)
            ref[n * block : (n + 1) * block, :] = full[pl.ds(source, block), :]


def prior_pass(devices, feats, turned, begun, part, got, own_cols, other_cols, later, places=None):
    rows, width = own_cols.shape
    half = part.shape[0]
    outs = [shape(rows, width)] * 2 + [shape(half, width)] * 2
    scratch = [pltpu.VMEM((CORES * rows, width), bf16)]
    if places is not None:
        outs.append(shape(2 * half // len(places[0]), width))
        scratch.insert(0, pltpu.VMEM((2 * half, width), f32))
    return pl.pallas_call(
        functools.partial(prior_kernel, places, devices),
        out_shape=tuple(outs),
        in_specs=[VMEM] * 7 + [ANY],
        out_specs=(VMEM,) * len(outs),
        scratch_shapes=scratch,
        compiler_params=PARAMS,
        cost_estimate=cost(16 * rows * half * width, 16 * rows * half),
        name="prior_pass",
    )(feats, turned, begun, part, got, own_cols, other_cols, later)


def step_kernel(halving, stage, under, devices, held, got, *refs):
    send = refs[-2] if halving else refs[-1]
    rows = send.shape[0] - under
    if halving:
        bit = where_am_i(devices)[1 + stage]
        for ref, which in ((send, 1 - bit), (refs[-1], bit)):
            at = rows_at(which, rows)
            ref[:rows, :] = held[at, :] + got[at, :]
    else:
        send[:rows, :] = held[:rows, :] + got[:rows, :]
    if under:
        sent, more = refs[:2]
        send[rows:, :] = sent[sent.shape[0] - under :, :] + more[more.shape[0] - under :, :]


def step_pass(halving, stage, devices, held, got, rows, riders=(), later=()):
    width = held.shape[1]
    under = RIDERS if riders else 0
    outs = [shape(rows // 2 + under, width), shape(rows // 2, width)] if halving else [shape(rows + under, width)]
    return pl.pallas_call(
        functools.partial(step_kernel, halving, stage, under, devices),
        out_shape=tuple(outs),
        in_specs=[VMEM] * (2 + len(riders)) + [ANY] * len(later),
        out_specs=(VMEM,) * len(outs),
        compiler_params=PARAMS,
        cost_estimate=cost(rows * width, 12 * rows * width),
        name="step_pass",
    )(held, got, *riders, *later)


def update_kernel(rate, held, got, sent, old, *refs):
    new, stats = refs[-2:]
    rows = old.shape[0]
    total = held[:rows, :] + got[:rows, :]
    before = old[...]
    new[...] = before + rate * (prior_prec * total - weight_decay * before)
    stats[...] = sent[sent.shape[0] - RIDERS :, :] + got[rows:, :]


def update_pass(rate, held, got, sent, old, later=()):
    return pl.pallas_call(
        functools.partial(update_kernel, rate),
        out_shape=(shape(*old.shape), shape(RIDERS, old.shape[1])),
        in_specs=[VMEM] * 4 + [ANY] * len(later),
        out_specs=(VMEM,) * 2,
        compiler_params=PARAMS,
        cost_estimate=cost(4 * old.size, 16 * old.size),
        name="update_pass",
    )(held, got, sent, old, *later)


def gather_kernel(slot, devices, part, got, *refs):
    both = refs[-1]
    rows = part.shape[0]
    bit = where_am_i(devices)[slot]
    both[pl.ds(pl.multiple_of(bit * rows, rows), rows), :] = part[...]
    both[pl.ds(pl.multiple_of((1 - bit) * rows, rows), rows), :] = got[...]


def gather_pass(stage, devices, part, got, later=()):
    rows, width = part.shape
    return pl.pallas_call(
        functools.partial(gather_kernel, 1 + stage, devices),
        out_shape=shape(2 * rows, width),
        in_specs=[VMEM, VMEM] + [ANY] * len(later),
        out_specs=VMEM,
        compiler_params=PARAMS,
        cost_estimate=cost(rows * width, 16 * rows * width),
        name="gather_pass",
    )(part, got, *later)


def split_kernel(devices, both, mine, other):
    place = where_am_i(devices)
    rows = mine.shape[0]
    for ref, which in ((mine, place[0]), (other, 1 - place[0])):
        at = pl.ds(pl.multiple_of(which * rows, 8), rows) if rows % 8 == 0 else pl.ds(which * rows, rows)
        ref[...] = both[at, :]


def split_pass(devices, both):
    rows, width = both.shape
    return pl.pallas_call(
        functools.partial(split_kernel, devices),
        out_shape=(shape(rows // CORES, width),) * 2,
        in_specs=[VMEM],
        out_specs=(VMEM,) * 2,
        compiler_params=PARAMS,
        name="split_pass",
    )(both)


def across_kernel(devices, mine, other, both):
    place = where_am_i(devices)
    width = mine.shape[1]
    both[:, pl.ds(pl.multiple_of(place[0] * width, width), width)] = mine[...]
    both[:, pl.ds(pl.multiple_of((1 - place[0]) * width, width), width)] = other[...]


def across_pass(devices, mine, other):
    rows, width = mine.shape
    return pl.pallas_call(
        functools.partial(across_kernel, devices),
        out_shape=shape(rows, CORES * width),
        in_specs=[VMEM, VMEM],
        out_specs=VMEM,
        compiler_params=PARAMS,
        name="across_pass",
    )(mine, other)


def renew_kernel(devices, stats, more, base_u, grad_u, own_mean, other_mean, base_v, grad_v, users, *outs):
    core = where_am_i(devices)[0]
    width = own_mean.shape[1]
    precision = precision_of(stats[...] + more[...])
    precision = jnp.concatenate([precision] * CORES, 1)
    parts = 1 if len(outs) == 1 else ITEM_PARTS
    rows = base_v.shape[0] // parts
    for n, items in enumerate(outs[:parts]):
        at = slice(n * rows, (n + 1) * rows)
        items[...] = base_v[at, :] + precision * grad_v[at, :]
    new = base_u[...] + precision * grad_u[...]
    pull = step_size * prior_prec
    left = jnp.where(core == 0, own_mean[...], other_mean[...])
    right = jnp.where(core == 0, other_mean[...], own_mean[...])
    users[:, :width] = new[:, :width] + pull * left
    users[:, width:] = new[:, width:] + pull * right
    for ref, which in zip(outs[parts:], (core, 1 - core), strict=False):
        ref[...] = half_of(users, which)


def renew_pass(devices, last, stats, more, base_u, grad_u, own_mean, *state):
    rows, rank = base_u.shape
    outs = [shape(rows, rank)]
    if last:
        outs.append(shape(rows, rank))
    else:
        outs += [shape(rows // ITEM_PARTS, rank)] * ITEM_PARTS + [shape(*own_mean.shape)] * 2
    return pl.pallas_call(
        functools.partial(renew_kernel, devices),
        out_shape=tuple(outs),
        in_specs=[VMEM] * 8,
        out_specs=(VMEM,) * len(outs),
        compiler_params=PARAMS,
        cost_estimate=cost(8 * base_u.size, 32 * base_u.size),
        name="renew_pass",
    )(stats, more, base_u, grad_u, own_mean, *state)


def bit_order(devices, core):
    bits = devices.bit_length() - 1
    far = list(range(3, bits))
    return [1, 2] + far if core == 0 else [2, 1] + far[::-1]


def swap(array, devices):
    return lax.ppermute(array, "user", [(i, i ^ 1) for i in range(devices)])


def roll(array, devices):
    return lax.ppermute(array, "user", [(i, (i + 1) % devices) for i in range(devices)])


def exchange(array, devices, stage):
    orders = [bit_order(devices, core) for core in range(CORES)]
    pairs = [(i, i ^ (1 << orders[i & 1][stage])) for i in range(devices)]
    return lax.ppermute(array, "user", pairs)


def final_places(devices):
    bits = devices.bit_length() - 1
    return [
        [
            sum(
                ((place >> (bits - 2 - n)) & 1) << (bit - 1)
                for n, bit in enumerate(bit_order(devices, core))
            )
            for place in range(devices // 2)
        ]
        for core in range(CORES)
    ]


def local(
    ratings,
    tile_index,
    tile_count,
    side_features,
    user_factors,
    item_factors,
    prior_weights,
    user_noise,
    item_noise,
):
    devices = lax.axis_size("user")
    stages = devices.bit_length() - 2
    strata = ratings.shape[1]
    feat = prior_weights.shape[0]
    rate = rate_scale / (user_factors.shape[0] * devices)
    own_turned = turn_pass(side_features)
    own_mean, other_mean, send, held, old = first_pass(
        devices, side_features, own_turned, prior_weights, user_factors
    )
    send, held = step_pass(True, 0, devices, held, swap(send, devices), feat)
    users, items = user_factors, [item_factors]
    for stratum in range(strata):
        last = stratum + 1 == strata
        got = exchange(send, devices, 0)
        later = send if stratum else own_turned
        err_b, stats = error_pass(stratum, tile_index, tile_count, ratings, users, later, *items)
        state = grad_pass(stratum, err_b, user_noise, item_noise, users, *items)
        riders = (stats, exchange(stats, devices, 0))
        send, held = step_pass(True, 1, devices, held, got, got.shape[0], riders)
        for stage in range(1, stages - 1):
            got = exchange(send, devices, stage)
            rows = got.shape[0] - RIDERS
            later = state[:1] if stage == 1 else ()
            if last:
                send, held = step_pass(True, stage + 1, devices, held, got, rows, (send, got), later)
            else:
                (send,) = step_pass(False, 0, devices, held, got, rows, (send, got), later)
                held = send
            if stratum == 0 and stage == 1:
                wide = swap(widen_pass(side_features, send), devices)
                feats, turned = join_pass(side_features, own_turned, wide)
        got = exchange(send, devices, stages - 1)
        part, stats = update_pass(rate, held, got, send, old)
        users, *items = renew_pass(
            devices, last, stats, swap(stats, devices), *state[:2], own_mean, other_mean, *state[2:]
        )
        if last:
            break
        old = part
        *items, own_cols, other_cols = items
        items = [roll(rows, devices) for rows in items]
        other_cols = swap(other_cols, devices)
        part = gather_pass(1, devices, part, exchange(part, devices, 1), [users])
        got = exchange(part, devices, 0)
        begun = part_pass(devices, feats, part)
        own_mean, other_mean, send, held, *olds = prior_pass(
            devices,
            feats,
            turned,
            begun,
            part,
            got,
            own_cols,
            other_cols,
            items[0],
            final_places(devices) if stratum + 2 == strata else None,
        )
        if olds:
            (old,) = olds
        other_mean = swap(other_mean, devices)
    mine, other = split_pass(devices, part)
    return (users, *items, across_pass(devices, mine, swap(other, devices)))


def solution(mesh):
    return jax.shard_map(
        local,
        mesh=mesh,
        in_specs=(
            P("user", None, None, None, None),
            P("user", None, None),
            P("user", None),
            P("user", None),
            P("user", None),
            P("user", None),
            P(),
            P(None, "user", None),
            P(None, "user", None),
        ),
        out_specs=(P("user", None), P("user", None), P("user", None)),
        check_vma=False,
    )
```

```python
import functools
import math

import jax
import jax.numpy as jnp
from jax import lax
from jax.experimental import pallas as pl
from jax.experimental.pallas import tpu as pltpu
from jax.sharding import PartitionSpec as P

step_size = 0.01
prior_prec = 8.0
item_prec = 1.0
weight_decay = 1.0
rate_scale = 0.04

CORES = 2
RIDERS = 8
ITEM_PARTS = 1
FEAT_PARTS = 3
NN = (((1,), (0,)), ((), ()))
NT = (((1,), (1,)), ((), ()))
TN = (((0,), (0,)), ((), ()))
VMEM = pl.BlockSpec(memory_space=pltpu.VMEM)
SMEM = pl.BlockSpec(memory_space=pltpu.SMEM)
ANY = pl.BlockSpec(memory_space=pl.ANY)
PARAMS = pltpu.CompilerParams(vmem_limit_bytes=8 << 20)
f32 = jnp.float32
bf16 = jnp.bfloat16


def dot(a, b, dims=NN):
    return lax.dot_general(a, b, dims, preferred_element_type=f32)


def shape(*dims, dtype=f32):
    return jax.ShapeDtypeStruct(dims, dtype)


def cost(flops, size):
    return pl.CostEstimate(flops=flops, bytes_accessed=size, transcendentals=0)


def where_am_i(devices):
    own = lax.axis_index("user")
    core = own & 1
    zero, one = (bit_order(devices, c) for c in range(CORES))
    bits = [jnp.where(core == 0, own >> z, own >> o) & 1 for z, o in zip(zero, one, strict=True)]
    return [core, *bits, own >> 1]


def rows_at(which, rows):
    start = which * rows
    return pl.ds(pl.multiple_of(start, rows) if rows % 8 == 0 else start, rows)


def half_of(ref, core):
    width = ref.shape[1] // CORES
    return ref[:, pl.ds(pl.multiple_of(core * width, width), width)]


def precision_of(stats):
    return (1.0 + stats[1:2, :] / 2.0) / (1.0 + stats[0:1, :] / 2.0)


def error_kernel(stratum, codes, count, ratings, users, *refs):
    items, (err_b, stats, pred) = refs[1:-3], refs[-3:]
    tile = ratings.shape[-1]
    grid = users.shape[0] // tile
    user_b = users[...].astype(bf16)
    start = 0
    for part in items:
        pred[:, start : start + part.shape[0]] = dot(user_b, part[...].astype(bf16), NT)
        start += part.shape[0]
    err_b[...] = jnp.zeros_like(err_b)
    live_slots = count[0, stratum]
    sse = jnp.zeros((tile, tile), f32)
    for slot in range(ratings.shape[2]):
        code = codes[0, stratum, slot]
        at_rows = rows_at(code // grid, tile)
        at_cols = rows_at(code % grid, tile)
        live = (slot < live_slots).astype(f32)
        err = (ratings[0, stratum, slot].astype(f32) - pred[at_rows, at_cols]) * live
        sse = sse + err * err
        err_b[at_rows, at_cols] = err.astype(bf16)
    total = jnp.sum(sse)
    counted = live_slots.astype(f32) * float(tile * tile)
    row = lax.broadcasted_iota(jnp.int32, stats.shape, 0)
    stats[...] = jnp.where(row == 0, total, jnp.where(row == 1, counted, 0.0))


def error_pass(stratum, codes, count, ratings, users, later, *items):
    rows, rank = users.shape
    return pl.pallas_call(
        functools.partial(error_kernel, stratum),
        out_shape=(shape(rows, rows, dtype=bf16), shape(RIDERS, rank // CORES)),
        in_specs=[SMEM] * 2 + [VMEM] * 2 + [ANY] + [VMEM] * len(items),
        out_specs=(VMEM,) * 2,
        scratch_shapes=[pltpu.VMEM((rows, rows), f32)],
        compiler_params=PARAMS,
        cost_estimate=cost(24 * rows * rows * rank, 64 * rows * rank),
        name="error_pass",
    )(codes, count, ratings, users, later, *items)


def grad_kernel(stratum, noise_scale, err_b, user_noise, item_noise, users, *refs):
    items, (base_u, grad_u, base_v, grad_v) = refs[:-4], refs[-4:]
    item_b = jnp.concatenate([part[...].astype(bf16) for part in items], 0)
    grad_u[...] = step_size * dot(err_b[...], item_b)
    grad_v[...] = step_size * dot(err_b[...], users[...].astype(bf16), TN)
    noise = noise_scale * user_noise[stratum].astype(f32)
    base_u[...] = (1.0 - step_size * prior_prec) * users[...] + noise
    start = 0
    for part in items:
        at = slice(start, start + part.shape[0])
        noise = noise_scale * item_noise[stratum, at].astype(f32)
        base_v[at, :] = (1.0 - step_size * item_prec) * part[...] + noise
        start += part.shape[0]


def grad_pass(stratum, err_b, user_noise, item_noise, users, *items):
    rows, rank = users.shape
    return pl.pallas_call(
        functools.partial(grad_kernel, stratum, math.sqrt(2.0 * step_size)),
        out_shape=(shape(rows, rank),) * 4,
        in_specs=[VMEM] * (4 + len(items)),
        out_specs=(VMEM,) * 4,
        compiler_params=PARAMS,
        cost_estimate=cost(4 * rows * rows * rank, 28 * rows * rank),
        name="grad_pass",
    )(err_b, user_noise, item_noise, users, *items)


def turn_kernel(feats, turned):
    turned[...] = feats[...].T


def turn_pass(feats):
    rows, feat = feats.shape
    return pl.pallas_call(
        turn_kernel,
        out_shape=shape(feat, rows, dtype=bf16),
        in_specs=[VMEM],
        out_specs=VMEM,
        compiler_params=PARAMS,
        cost_estimate=cost(rows * feat, 4 * rows * feat),
        name="turn_pass",
    )(feats)


def first_kernel(devices, feats, turned, weights, users, own_mean, other_mean, send, keep, old, mean):
    place = where_am_i(devices)
    here = place[0]
    mean[...] = dot(feats[...], weights[...].astype(bf16))
    for grad, means, which in ((send, other_mean, 1 - here), (keep, own_mean, here)):
        mean_now = half_of(mean, which)
        means[...] = mean_now
        offset = (half_of(users, which) - mean_now).astype(bf16)
        grad[...] = dot(turned[...], offset)
    rows, width = old.shape
    old[...] = weights[rows_at(2 * place[1] + place[2], rows), rows_at(here, width)]


def first_pass(devices, feats, turned, weights, users):
    rows, rank = users.shape
    feat = weights.shape[0]
    width = rank // CORES
    return pl.pallas_call(
        functools.partial(first_kernel, devices),
        out_shape=(shape(rows, width),) * 2 + (shape(feat, width),) * 2 + (shape(feat // 4, width),),
        in_specs=[VMEM] * 4,
        out_specs=(VMEM,) * 5,
        scratch_shapes=[pltpu.VMEM(users.shape, f32)],
        compiler_params=PARAMS,
        cost_estimate=cost(4 * rows * feat * rank, 8 * feat * rank),
        name="first_pass",
    )(feats, turned, weights, users)


def widen_kernel(narrow, later, *wide):
    rows = wide[0].shape[0]
    for n, ref in enumerate(wide):
        ref[...] = narrow[n * rows : (n + 1) * rows, :].astype(f32)


def widen_pass(narrow, later):
    rows, feat = narrow.shape
    return pl.pallas_call(
        widen_kernel,
        out_shape=(shape(rows // FEAT_PARTS, feat),) * FEAT_PARTS,
        in_specs=[VMEM, ANY],
        out_specs=(VMEM,) * FEAT_PARTS,
        compiler_params=PARAMS,
        name="widen_pass",
    )(narrow, later)


def join_kernel(own, own_turned, *refs):
    others, (both, turned) = refs[:-2], refs[-2:]
    rows = own.shape[0]
    both[:rows, :] = own[...]
    turned[:, :rows] = own_turned[...]
    for other in others:
        at = slice(rows, rows + other.shape[0])
        both[at, :] = other[...].astype(bf16)
        turned[:, at] = other[...].T.astype(bf16)
        rows += other.shape[0]


def join_pass(own, own_turned, *others):
    rows, feat = own.shape
    return pl.pallas_call(
        join_kernel,
        out_shape=(shape(CORES * rows, feat, dtype=bf16), shape(feat, CORES * rows, dtype=bf16)),
        in_specs=[VMEM] * (2 + len(others)),
        out_specs=(VMEM, VMEM),
        compiler_params=PARAMS,
        cost_estimate=cost(rows * feat, 12 * rows * feat),
        name="join_pass",
    )(own, own_turned, *others)


def part_kernel(devices, feats, part, mean):
    half = part.shape[0]
    bit = where_am_i(devices)[1]
    here = pl.ds(pl.multiple_of(bit * half, half), half)
    mean[...] = dot(feats[:, here], part[...].astype(bf16))


def part_pass(devices, feats, part):
    rows = feats.shape[0]
    half, width = part.shape
    return pl.pallas_call(
        functools.partial(part_kernel, devices),
        out_shape=shape(rows, width),
        in_specs=[VMEM, VMEM],
        out_specs=VMEM,
        compiler_params=PARAMS,
        cost_estimate=cost(2 * rows * half * width, 4 * rows * half),
        name="part_pass",
    )(feats, part)


def prior_kernel(places, devices, feats, turned, begun, part, got, own_cols, other_cols, later, own_mean, other_mean, send, keep, *refs):
    rows = own_cols.shape[0]
    half = keep.shape[0]
    place = where_am_i(devices)
    core, bit = place[0], place[1]
    here = pl.ds(pl.multiple_of(bit * half, half), half)
    there = pl.ds(pl.multiple_of((1 - bit) * half, half), half)
    offset = refs[-1]
    mean = begun[...] + dot(feats[:, there], got[...].astype(bf16))
    own_mean[...] = mean[:rows]
    other_mean[...] = mean[rows:]
    offset[:rows, :] = (own_cols[...] - mean[:rows]).astype(bf16)
    offset[rows:, :] = (other_cols[...] - mean[rows:]).astype(bf16)
    if places is None:
        send[...] = dot(turned[there, :], offset[...])
        keep[...] = dot(turned[here, :], offset[...])
        return
    old, full = refs[:2]
    full[here, :] = part[...]
    full[there, :] = got[...]
    start = place[-1] * old.shape[0]
    if old.shape[0] % 8 == 0:
        start = pl.multiple_of(start, old.shape[0])
    old[...] = full[pl.ds(start, old.shape[0]), :]
    full[...] = dot(turned[...], offset[...])
    blocks = len(places[0])
    block = 2 * half // blocks
    for ref, which in ((send, 1 - bit), (keep, bit)):
        for n in range(blocks // 2):
            source = jnp.int32(0)
            for c, order in enumerate(places):
                for b in range(2):
                    source = jnp.where((core == c) & (which == b), order[b * blocks // 2 + n], source)
            source = source * block
            if block % 8 == 0:
                source = pl.multiple_of(source, block)
            ref[n * block : (n + 1) * block, :] = full[pl.ds(source, block), :]


def prior_pass(devices, feats, turned, begun, part, got, own_cols, other_cols, later, places=None):
    rows, width = own_cols.shape
    half = part.shape[0]
    outs = [shape(rows, width)] * 2 + [shape(half, width)] * 2
    scratch = [pltpu.VMEM((CORES * rows, width), bf16)]
    if places is not None:
        outs.append(shape(2 * half // len(places[0]), width))
        scratch.insert(0, pltpu.VMEM((2 * half, width), f32))
    return pl.pallas_call(
        functools.partial(prior_kernel, places, devices),
        out_shape=tuple(outs),
        in_specs=[VMEM] * 7 + [ANY],
        out_specs=(VMEM,) * len(outs),
        scratch_shapes=scratch,
        compiler_params=PARAMS,
        cost_estimate=cost(16 * rows * half * width, 16 * rows * half),
        name="prior_pass",
    )(feats, turned, begun, part, got, own_cols, other_cols, later)


def step_kernel(halving, stage, under, devices, held, got, *refs):
    send = refs[-2] if halving else refs[-1]
    rows = send.shape[0] - under
    if halving:
        bit = where_am_i(devices)[1 + stage]
        for ref, which in ((send, 1 - bit), (refs[-1], bit)):
            at = rows_at(which, rows)
            ref[:rows, :] = held[at, :] + got[at, :]
    else:
        send[:rows, :] = held[:rows, :] + got[:rows, :]
    if under:
        sent, more = refs[:2]
        send[rows:, :] = sent[sent.shape[0] - under :, :] + more[more.shape[0] - under :, :]


def step_pass(halving, stage, devices, held, got, rows, riders=(), later=()):
    width = held.shape[1]
    under = RIDERS if riders else 0
    outs = [shape(rows // 2 + under, width), shape(rows // 2, width)] if halving else [shape(rows + under, width)]
    return pl.pallas_call(
        functools.partial(step_kernel, halving, stage, under, devices),
        out_shape=tuple(outs),
        in_specs=[VMEM] * (2 + len(riders)) + [ANY] * len(later),
        out_specs=(VMEM,) * len(outs),
        compiler_params=PARAMS,
        cost_estimate=cost(rows * width, 12 * rows * width),
        name="step_pass",
    )(held, got, *riders, *later)


def update_kernel(rate, held, got, sent, old, *refs):
    new, stats = refs[-2:]
    rows = old.shape[0]
    total = held[:rows, :] + got[:rows, :]
    before = old[...]
    new[...] = before + rate * (prior_prec * total - weight_decay * before)
    stats[...] = sent[sent.shape[0] - RIDERS :, :] + got[rows:, :]


def update_pass(rate, held, got, sent, old, later=()):
    return pl.pallas_call(
        functools.partial(update_kernel, rate),
        out_shape=(shape(*old.shape), shape(RIDERS, old.shape[1])),
        in_specs=[VMEM] * 4 + [ANY] * len(later),
        out_specs=(VMEM,) * 2,
        compiler_params=PARAMS,
        cost_estimate=cost(4 * old.size, 16 * old.size),
        name="update_pass",
    )(held, got, sent, old, *later)


def gather_kernel(slot, devices, part, got, *refs):
    both = refs[-1]
    rows = part.shape[0]
    bit = where_am_i(devices)[slot]
    both[pl.ds(pl.multiple_of(bit * rows, rows), rows), :] = part[...]
    both[pl.ds(pl.multiple_of((1 - bit) * rows, rows), rows), :] = got[...]


def gather_pass(stage, devices, part, got, later=()):
    rows, width = part.shape
    return pl.pallas_call(
        functools.partial(gather_kernel, 1 + stage, devices),
        out_shape=shape(2 * rows, width),
        in_specs=[VMEM, VMEM] + [ANY] * len(later),
        out_specs=VMEM,
        compiler_params=PARAMS,
        cost_estimate=cost(rows * width, 16 * rows * width),
        name="gather_pass",
    )(part, got, *later)


def split_kernel(devices, both, stats, mine, other):
    rows = mine.shape[0]
    core = where_am_i(devices)[0]
    mine[...] = both[rows_at(core, rows), :]
    other[:rows, :] = both[rows_at(1 - core, rows), :]
    other[rows:, :] = stats[...]


def split_pass(devices, both, stats):
    rows, width = both.shape
    rows = rows // CORES
    return pl.pallas_call(
        functools.partial(split_kernel, devices),
        out_shape=(shape(rows, width), shape(rows + RIDERS, width)),
        in_specs=[VMEM] * 2,
        out_specs=(VMEM,) * 2,
        compiler_params=PARAMS,
        name="split_pass",
    )(both, stats)


def renew(core, stats, base_u, grad_u, own_mean, other_mean, base_v, grad_v, users, *items):
    width = own_mean.shape[1]
    precision = precision_of(stats)
    precision = jnp.concatenate([precision] * CORES, 1)
    rows = base_v.shape[0] // len(items)
    for n, ref in enumerate(items):
        at = slice(n * rows, (n + 1) * rows)
        ref[...] = base_v[at, :] + precision * grad_v[at, :]
    new = base_u[...] + precision * grad_u[...]
    pull = step_size * prior_prec
    left = jnp.where(core == 0, own_mean[...], other_mean[...])
    right = jnp.where(core == 0, other_mean[...], own_mean[...])
    users[:, :width] = new[:, :width] + pull * left
    users[:, width:] = new[:, width:] + pull * right


def renew_kernel(devices, stats, more, *refs):
    core = where_am_i(devices)[0]
    renew(core, stats[...] + more[...], *refs[:-2])
    users = refs[6]
    for ref, which in zip(refs[-2:], (core, 1 - core), strict=True):
        ref[...] = half_of(users, which)


def renew_pass(devices, stats, more, base_u, grad_u, own_mean, *state):
    rows, rank = base_u.shape
    outs = [shape(rows, rank)] + [shape(rows // ITEM_PARTS, rank)] * ITEM_PARTS + [shape(*own_mean.shape)] * 2
    return pl.pallas_call(
        functools.partial(renew_kernel, devices),
        out_shape=tuple(outs),
        in_specs=[VMEM] * 8,
        out_specs=(VMEM,) * len(outs),
        compiler_params=PARAMS,
        cost_estimate=cost(8 * base_u.size, 32 * base_u.size),
        name="renew_pass",
    )(stats, more, base_u, grad_u, own_mean, *state)


def last_kernel(devices, stats, mine, got, *refs):
    core = where_am_i(devices)[0]
    weights = refs[-1]
    rows, width = mine.shape
    weights[:, rows_at(core, width)] = mine[...]
    weights[:, rows_at(1 - core, width)] = got[:rows, :]
    renew(core, stats[...] + got[rows:, :], *refs[:-1])


def last_pass(devices, stats, mine, got, base_u, *state):
    rows, width = mine.shape
    return pl.pallas_call(
        functools.partial(last_kernel, devices),
        out_shape=(shape(*base_u.shape),) * 2 + (shape(rows, CORES * width),),
        in_specs=[VMEM] * 9,
        out_specs=(VMEM,) * 3,
        compiler_params=PARAMS,
        cost_estimate=cost(8 * base_u.size, 32 * base_u.size),
        name="last_pass",
    )(stats, mine, got, base_u, *state)


def bit_order(devices, core):
    bits = devices.bit_length() - 1
    far = list(range(3, bits))
    return [1, 2] + far if core == 0 else [2, 1] + far[::-1]


def swap(array, devices):
    return lax.ppermute(array, "user", [(i, i ^ 1) for i in range(devices)])


def roll(array, devices):
    return lax.ppermute(array, "user", [(i, (i + 1) % devices) for i in range(devices)])


def exchange(array, devices, stage):
    orders = [bit_order(devices, core) for core in range(CORES)]
    pairs = [(i, i ^ (1 << orders[i & 1][stage])) for i in range(devices)]
    return lax.ppermute(array, "user", pairs)


def final_places(devices):
    bits = devices.bit_length() - 1
    return [
        [
            sum(
                ((place >> (bits - 2 - n)) & 1) << (bit - 1)
                for n, bit in enumerate(bit_order(devices, core))
            )
            for place in range(devices // 2)
        ]
        for core in range(CORES)
    ]


def local(
    ratings,
    tile_index,
    tile_count,
    side_features,
    user_factors,
    item_factors,
    prior_weights,
    user_noise,
    item_noise,
):
    devices = lax.axis_size("user")
    stages = devices.bit_length() - 2
    strata = ratings.shape[1]
    feat = prior_weights.shape[0]
    rate = rate_scale / (user_factors.shape[0] * devices)
    own_turned = turn_pass(side_features)
    own_mean, other_mean, send, held, old = first_pass(
        devices, side_features, own_turned, prior_weights, user_factors
    )
    send, held = step_pass(True, 0, devices, held, swap(send, devices), feat)
    users, items = user_factors, [item_factors]
    for stratum in range(strata):
        last = stratum + 1 == strata
        got = exchange(send, devices, 0)
        later = send if stratum else own_turned
        err_b, stats = error_pass(stratum, tile_index, tile_count, ratings, users, later, *items)
        state = grad_pass(stratum, err_b, user_noise, item_noise, users, *items)
        riders = (stats, exchange(stats, devices, 0))
        send, held = step_pass(True, 1, devices, held, got, got.shape[0], riders)
        for stage in range(1, stages - 1):
            got = exchange(send, devices, stage)
            rows = got.shape[0] - RIDERS
            later = state[:1] if stage == 1 else ()
            if last:
                send, held = step_pass(True, stage + 1, devices, held, got, rows, (send, got), later)
            else:
                (send,) = step_pass(False, 0, devices, held, got, rows, (send, got), later)
                held = send
            if stratum == 0 and stage == 1:
                wide = [swap(part, devices) for part in widen_pass(side_features, send)]
                feats, turned = join_pass(side_features, own_turned, *wide)
        got = exchange(send, devices, stages - 1)
        part, stats = update_pass(rate, held, got, send, old)
        if last:
            break
        users, *items = renew_pass(
            devices, stats, swap(stats, devices), *state[:2], own_mean, other_mean, *state[2:]
        )
        old = part
        *items, own_cols, other_cols = items
        items = [roll(rows, devices) for rows in items]
        other_cols = swap(other_cols, devices)
        part = gather_pass(1, devices, part, exchange(part, devices, 1), [users])
        got = exchange(part, devices, 0)
        begun = part_pass(devices, feats, part)
        own_mean, other_mean, send, held, *olds = prior_pass(
            devices,
            feats,
            turned,
            begun,
            part,
            got,
            own_cols,
            other_cols,
            items[0],
            final_places(devices) if stratum + 2 == strata else None,
        )
        if olds:
            (old,) = olds
        other_mean = swap(other_mean, devices)
    mine, other = split_pass(devices, part, stats)
    return last_pass(
        devices, stats, mine, swap(other, devices), *state[:2], own_mean, other_mean, *state[2:]
    )


def solution(mesh):
    return jax.shard_map(
        local,
        mesh=mesh,
        in_specs=(
            P("user", None, None, None, None),
            P("user", None, None),
            P("user", None),
            P("user", None),
            P("user", None),
            P("user", None),
            P(),
            P(None, "user", None),
            P(None, "user", None),
        ),
        out_specs=(P("user", None), P("user", None), P("user", None)),
        check_vma=False,
    )
```

```python
import functools
import math

import jax
import jax.numpy as jnp
from jax import lax
from jax.experimental import pallas as pl
from jax.experimental.pallas import tpu as pltpu
from jax.sharding import PartitionSpec as P

step_size = 0.01
prior_prec = 8.0
item_prec = 1.0
weight_decay = 1.0
rate_scale = 0.04

CORES = 2
RIDERS = 8
ITEM_PARTS = 1
FEAT_PARTS = 3
NN = (((1,), (0,)), ((), ()))
NT = (((1,), (1,)), ((), ()))
TN = (((0,), (0,)), ((), ()))
VMEM = pl.BlockSpec(memory_space=pltpu.VMEM)
SMEM = pl.BlockSpec(memory_space=pltpu.SMEM)
ANY = pl.BlockSpec(memory_space=pl.ANY)
PARAMS = pltpu.CompilerParams(vmem_limit_bytes=8 << 20)
f32 = jnp.float32
bf16 = jnp.bfloat16


def dot(a, b, dims=NN):
    return lax.dot_general(a, b, dims, preferred_element_type=f32)


def shape(*dims, dtype=f32):
    return jax.ShapeDtypeStruct(dims, dtype)


def cost(flops, size):
    return pl.CostEstimate(flops=flops, bytes_accessed=size, transcendentals=0)


def where_am_i(devices):
    own = lax.axis_index("user")
    core = own & 1
    zero, one = (bit_order(devices, c) for c in range(CORES))
    bits = [jnp.where(core == 0, own >> z, own >> o) & 1 for z, o in zip(zero, one, strict=True)]
    return [core, *bits, own >> 1]


def rows_at(which, rows):
    start = which * rows
    return pl.ds(pl.multiple_of(start, rows) if rows % 8 == 0 else start, rows)


def half_of(ref, core):
    width = ref.shape[1] // CORES
    return ref[:, pl.ds(pl.multiple_of(core * width, width), width)]


def precision_of(stats):
    return (1.0 + stats[1:2, :] / 2.0) / (1.0 + stats[0:1, :] / 2.0)


def error_kernel(stratum, codes, count, ratings, users, *refs):
    items, (err_b, stats, pred) = refs[1:-3], refs[-3:]
    tile = ratings.shape[-1]
    grid = users.shape[0] // tile
    user_b = users[...].astype(bf16)
    start = 0
    for part in items:
        pred[:, start : start + part.shape[0]] = dot(user_b, part[...].astype(bf16), NT)
        start += part.shape[0]
    err_b[...] = jnp.zeros_like(err_b)
    live_slots = count[0, stratum]
    sse = jnp.zeros((tile, tile), f32)
    for slot in range(ratings.shape[2]):
        code = codes[0, stratum, slot]
        at_rows = rows_at(code // grid, tile)
        at_cols = rows_at(code % grid, tile)
        live = (slot < live_slots).astype(f32)
        err = (ratings[0, stratum, slot].astype(f32) - pred[at_rows, at_cols]) * live
        sse = sse + err * err
        err_b[at_rows, at_cols] = err.astype(bf16)
    total = jnp.sum(sse)
    counted = live_slots.astype(f32) * float(tile * tile)
    row = lax.broadcasted_iota(jnp.int32, stats.shape, 0)
    stats[...] = jnp.where(row == 0, total, jnp.where(row == 1, counted, 0.0))


def error_pass(stratum, codes, count, ratings, users, later, *items):
    rows, rank = users.shape
    return pl.pallas_call(
        functools.partial(error_kernel, stratum),
        out_shape=(shape(rows, rows, dtype=bf16), shape(RIDERS, rank // CORES)),
        in_specs=[SMEM] * 2 + [VMEM] * 2 + [ANY] + [VMEM] * len(items),
        out_specs=(VMEM,) * 2,
        scratch_shapes=[pltpu.VMEM((rows, rows), f32)],
        compiler_params=PARAMS,
        cost_estimate=cost(24 * rows * rows * rank, 64 * rows * rank),
        name="error_pass",
    )(codes, count, ratings, users, later, *items)


def grad_kernel(stratum, noise_scale, err_b, user_noise, item_noise, users, *refs):
    items, (base_u, grad_u, base_v, grad_v) = refs[:-4], refs[-4:]
    item_b = jnp.concatenate([part[...].astype(bf16) for part in items], 0)
    grad_u[...] = step_size * dot(err_b[...], item_b)
    grad_v[...] = step_size * dot(err_b[...], users[...].astype(bf16), TN)
    noise = noise_scale * user_noise[stratum].astype(f32)
    base_u[...] = (1.0 - step_size * prior_prec) * users[...] + noise
    start = 0
    for part in items:
        at = slice(start, start + part.shape[0])
        noise = noise_scale * item_noise[stratum, at].astype(f32)
        base_v[at, :] = (1.0 - step_size * item_prec) * part[...] + noise
        start += part.shape[0]


def grad_pass(stratum, err_b, user_noise, item_noise, users, *items):
    rows, rank = users.shape
    return pl.pallas_call(
        functools.partial(grad_kernel, stratum, math.sqrt(2.0 * step_size)),
        out_shape=(shape(rows, rank),) * 4,
        in_specs=[VMEM] * (4 + len(items)),
        out_specs=(VMEM,) * 4,
        compiler_params=PARAMS,
        cost_estimate=cost(4 * rows * rows * rank, 28 * rows * rank),
        name="grad_pass",
    )(err_b, user_noise, item_noise, users, *items)


def turn_kernel(feats, turned):
    turned[...] = feats[...].T


def turn_pass(feats):
    rows, feat = feats.shape
    return pl.pallas_call(
        turn_kernel,
        out_shape=shape(feat, rows, dtype=bf16),
        in_specs=[VMEM],
        out_specs=VMEM,
        compiler_params=PARAMS,
        cost_estimate=cost(rows * feat, 4 * rows * feat),
        name="turn_pass",
    )(feats)


def first_kernel(devices, feats, turned, weights, users, own_mean, other_mean, send, offset, old, mean):
    place = where_am_i(devices)
    here = place[0]
    mean[...] = dot(feats[...], weights[...].astype(bf16))
    other_mean[...] = half_of(mean, 1 - here)
    send[...] = dot(turned[...], (half_of(users, 1 - here) - other_mean[...]).astype(bf16))
    own_mean[...] = half_of(mean, here)
    offset[...] = (half_of(users, here) - own_mean[...]).astype(bf16)
    rows, width = old.shape
    old[...] = weights[rows_at(2 * place[1] + place[2], rows), rows_at(here, width)]


def first_pass(devices, feats, turned, weights, users):
    rows, rank = users.shape
    feat = weights.shape[0]
    width = rank // CORES
    return pl.pallas_call(
        functools.partial(first_kernel, devices),
        out_shape=(shape(rows, width),) * 2
        + (shape(feat, width), shape(rows, width, dtype=bf16), shape(feat // 4, width)),
        in_specs=[VMEM] * 4,
        out_specs=(VMEM,) * 5,
        scratch_shapes=[pltpu.VMEM(users.shape, f32)],
        compiler_params=PARAMS,
        cost_estimate=cost(3 * rows * feat * rank, 8 * feat * rank),
        name="first_pass",
    )(feats, turned, weights, users)


def keep_kernel(turned, offset, grad):
    grad[...] = dot(turned[...], offset[...])


def keep_pass(turned, offset):
    feat, rows = turned.shape
    width = offset.shape[1]
    return pl.pallas_call(
        keep_kernel,
        out_shape=shape(feat, width),
        in_specs=[VMEM] * 2,
        out_specs=VMEM,
        compiler_params=PARAMS,
        cost_estimate=cost(2 * rows * feat * width, 4 * feat * width),
        name="keep_pass",
    )(turned, offset)


def widen_kernel(narrow, later, *wide):
    rows = wide[0].shape[0]
    for n, ref in enumerate(wide):
        ref[...] = narrow[n * rows : (n + 1) * rows, :].astype(f32)


def widen_pass(narrow, later):
    rows, feat = narrow.shape
    return pl.pallas_call(
        widen_kernel,
        out_shape=(shape(rows // FEAT_PARTS, feat),) * FEAT_PARTS,
        in_specs=[VMEM, ANY],
        out_specs=(VMEM,) * FEAT_PARTS,
        compiler_params=PARAMS,
        name="widen_pass",
    )(narrow, later)


def join_kernel(own, own_turned, *refs):
    others, (both, turned) = refs[:-2], refs[-2:]
    rows = own.shape[0]
    both[:rows, :] = own[...]
    turned[:, :rows] = own_turned[...]
    for other in others:
        at = slice(rows, rows + other.shape[0])
        both[at, :] = other[...].astype(bf16)
        turned[:, at] = other[...].T.astype(bf16)
        rows += other.shape[0]


def join_pass(own, own_turned, *others):
    rows, feat = own.shape
    return pl.pallas_call(
        join_kernel,
        out_shape=(shape(CORES * rows, feat, dtype=bf16), shape(feat, CORES * rows, dtype=bf16)),
        in_specs=[VMEM] * (2 + len(others)),
        out_specs=(VMEM, VMEM),
        compiler_params=PARAMS,
        cost_estimate=cost(rows * feat, 12 * rows * feat),
        name="join_pass",
    )(own, own_turned, *others)


def part_kernel(devices, feats, part, mean):
    half = part.shape[0]
    bit = where_am_i(devices)[1]
    here = pl.ds(pl.multiple_of(bit * half, half), half)
    mean[...] = dot(feats[:, here], part[...].astype(bf16))


def part_pass(devices, feats, part):
    rows = feats.shape[0]
    half, width = part.shape
    return pl.pallas_call(
        functools.partial(part_kernel, devices),
        out_shape=shape(rows, width),
        in_specs=[VMEM, VMEM],
        out_specs=VMEM,
        compiler_params=PARAMS,
        cost_estimate=cost(2 * rows * half * width, 4 * rows * half),
        name="part_pass",
    )(feats, part)


def prior_kernel(places, devices, feats, turned, begun, part, got, own_cols, other_cols, later, own_mean, other_mean, send, keep, *refs):
    rows = own_cols.shape[0]
    half = keep.shape[0]
    place = where_am_i(devices)
    core, bit = place[0], place[1]
    here = pl.ds(pl.multiple_of(bit * half, half), half)
    there = pl.ds(pl.multiple_of((1 - bit) * half, half), half)
    offset = refs[-1]
    mean = begun[...] + dot(feats[:, there], got[...].astype(bf16))
    own_mean[...] = mean[:rows]
    other_mean[...] = mean[rows:]
    offset[:rows, :] = (own_cols[...] - mean[:rows]).astype(bf16)
    offset[rows:, :] = (other_cols[...] - mean[rows:]).astype(bf16)
    if places is None:
        send[...] = dot(turned[there, :], offset[...])
        keep[...] = dot(turned[here, :], offset[...])
        return
    old, full = refs[:2]
    full[here, :] = part[...]
    full[there, :] = got[...]
    start = place[-1] * old.shape[0]
    if old.shape[0] % 8 == 0:
        start = pl.multiple_of(start, old.shape[0])
    old[...] = full[pl.ds(start, old.shape[0]), :]
    full[...] = dot(turned[...], offset[...])
    blocks = len(places[0])
    block = 2 * half // blocks
    for ref, which in ((send, 1 - bit), (keep, bit)):
        for n in range(blocks // 2):
            source = jnp.int32(0)
            for c, order in enumerate(places):
                for b in range(2):
                    source = jnp.where((core == c) & (which == b), order[b * blocks // 2 + n], source)
            source = source * block
            if block % 8 == 0:
                source = pl.multiple_of(source, block)
            ref[n * block : (n + 1) * block, :] = full[pl.ds(source, block), :]


def prior_pass(devices, feats, turned, begun, part, got, own_cols, other_cols, later, places=None):
    rows, width = own_cols.shape
    half = part.shape[0]
    outs = [shape(rows, width)] * 2 + [shape(half, width)] * 2
    scratch = [pltpu.VMEM((CORES * rows, width), bf16)]
    if places is not None:
        outs.append(shape(2 * half // len(places[0]), width))
        scratch.insert(0, pltpu.VMEM((2 * half, width), f32))
    return pl.pallas_call(
        functools.partial(prior_kernel, places, devices),
        out_shape=tuple(outs),
        in_specs=[VMEM] * 7 + [ANY],
        out_specs=(VMEM,) * len(outs),
        scratch_shapes=scratch,
        compiler_params=PARAMS,
        cost_estimate=cost(16 * rows * half * width, 16 * rows * half),
        name="prior_pass",
    )(feats, turned, begun, part, got, own_cols, other_cols, later)


def step_kernel(halving, stage, under, devices, held, got, *refs):
    send = refs[-2] if halving else refs[-1]
    rows = send.shape[0] - under
    if halving:
        bit = where_am_i(devices)[1 + stage]
        for ref, which in ((send, 1 - bit), (refs[-1], bit)):
            at = rows_at(which, rows)
            ref[:rows, :] = held[at, :] + got[at, :]
    else:
        send[:rows, :] = held[:rows, :] + got[:rows, :]
    if under:
        sent, more = refs[:2]
        send[rows:, :] = sent[sent.shape[0] - under :, :] + more[more.shape[0] - under :, :]


def step_pass(halving, stage, devices, held, got, rows, riders=(), later=()):
    width = held.shape[1]
    under = RIDERS if riders else 0
    outs = [shape(rows // 2 + under, width), shape(rows // 2, width)] if halving else [shape(rows + under, width)]
    return pl.pallas_call(
        functools.partial(step_kernel, halving, stage, under, devices),
        out_shape=tuple(outs),
        in_specs=[VMEM] * (2 + len(riders)) + [ANY] * len(later),
        out_specs=(VMEM,) * len(outs),
        compiler_params=PARAMS,
        cost_estimate=cost(rows * width, 12 * rows * width),
        name="step_pass",
    )(held, got, *riders, *later)


def update_kernel(rate, held, got, sent, old, *refs):
    new, stats = refs[-2:]
    rows = old.shape[0]
    total = held[:rows, :] + got[:rows, :]
    before = old[...]
    new[...] = before + rate * (prior_prec * total - weight_decay * before)
    stats[...] = sent[sent.shape[0] - RIDERS :, :] + got[rows:, :]


def update_pass(rate, held, got, sent, old, later=()):
    return pl.pallas_call(
        functools.partial(update_kernel, rate),
        out_shape=(shape(*old.shape), shape(RIDERS, old.shape[1])),
        in_specs=[VMEM] * 4 + [ANY] * len(later),
        out_specs=(VMEM,) * 2,
        compiler_params=PARAMS,
        cost_estimate=cost(4 * old.size, 16 * old.size),
        name="update_pass",
    )(held, got, sent, old, *later)


def gather_kernel(slot, devices, part, got, *refs):
    both = refs[-1]
    rows = part.shape[0]
    bit = where_am_i(devices)[slot]
    both[pl.ds(pl.multiple_of(bit * rows, rows), rows), :] = part[...]
    both[pl.ds(pl.multiple_of((1 - bit) * rows, rows), rows), :] = got[...]


def gather_pass(stage, devices, part, got, later=()):
    rows, width = part.shape
    return pl.pallas_call(
        functools.partial(gather_kernel, 1 + stage, devices),
        out_shape=shape(2 * rows, width),
        in_specs=[VMEM, VMEM] + [ANY] * len(later),
        out_specs=VMEM,
        compiler_params=PARAMS,
        cost_estimate=cost(rows * width, 16 * rows * width),
        name="gather_pass",
    )(part, got, *later)


def split_kernel(devices, both, stats, mine, other):
    rows = mine.shape[0]
    core = where_am_i(devices)[0]
    mine[...] = both[rows_at(core, rows), :]
    other[:rows, :] = both[rows_at(1 - core, rows), :]
    other[rows:, :] = stats[...]


def split_pass(devices, both, stats):
    rows, width = both.shape
    rows = rows // CORES
    return pl.pallas_call(
        functools.partial(split_kernel, devices),
        out_shape=(shape(rows, width), shape(rows + RIDERS, width)),
        in_specs=[VMEM] * 2,
        out_specs=(VMEM,) * 2,
        compiler_params=PARAMS,
        name="split_pass",
    )(both, stats)


def renew(core, stats, base_u, grad_u, own_mean, other_mean, base_v, grad_v, users, *items):
    width = own_mean.shape[1]
    precision = precision_of(stats)
    precision = jnp.concatenate([precision] * CORES, 1)
    rows = base_v.shape[0] // len(items)
    for n, ref in enumerate(items):
        at = slice(n * rows, (n + 1) * rows)
        ref[...] = base_v[at, :] + precision * grad_v[at, :]
    new = base_u[...] + precision * grad_u[...]
    pull = step_size * prior_prec
    left = jnp.where(core == 0, own_mean[...], other_mean[...])
    right = jnp.where(core == 0, other_mean[...], own_mean[...])
    users[:, :width] = new[:, :width] + pull * left
    users[:, width:] = new[:, width:] + pull * right


def renew_kernel(devices, stats, more, *refs):
    core = where_am_i(devices)[0]
    renew(core, stats[...] + more[...], *refs[:-2])
    users = refs[6]
    for ref, which in zip(refs[-2:], (core, 1 - core), strict=True):
        ref[...] = half_of(users, which)


def renew_pass(devices, stats, more, base_u, grad_u, own_mean, *state):
    rows, rank = base_u.shape
    outs = [shape(rows, rank)] + [shape(rows // ITEM_PARTS, rank)] * ITEM_PARTS + [shape(*own_mean.shape)] * 2
    return pl.pallas_call(
        functools.partial(renew_kernel, devices),
        out_shape=tuple(outs),
        in_specs=[VMEM] * 8,
        out_specs=(VMEM,) * len(outs),
        compiler_params=PARAMS,
        cost_estimate=cost(8 * base_u.size, 32 * base_u.size),
        name="renew_pass",
    )(stats, more, base_u, grad_u, own_mean, *state)


def last_kernel(devices, stats, mine, got, *refs):
    core = where_am_i(devices)[0]
    weights = refs[-1]
    rows, width = mine.shape
    weights[:, rows_at(core, width)] = mine[...]
    weights[:, rows_at(1 - core, width)] = got[:rows, :]
    renew(core, stats[...] + got[rows:, :], *refs[:-1])


def last_pass(devices, stats, mine, got, base_u, *state):
    rows, width = mine.shape
    return pl.pallas_call(
        functools.partial(last_kernel, devices),
        out_shape=(shape(*base_u.shape),) * 2 + (shape(rows, CORES * width),),
        in_specs=[VMEM] * 9,
        out_specs=(VMEM,) * 3,
        compiler_params=PARAMS,
        cost_estimate=cost(8 * base_u.size, 32 * base_u.size),
        name="last_pass",
    )(stats, mine, got, base_u, *state)


def bit_order(devices, core):
    bits = devices.bit_length() - 1
    far = list(range(3, bits))
    return [2, 1] + far if core == 0 else [1, 2] + far[::-1]


def swap(array, devices):
    return lax.ppermute(array, "user", [(i, i ^ 1) for i in range(devices)])


def roll(array, devices):
    return lax.ppermute(array, "user", [(i, (i + 1) % devices) for i in range(devices)])


def exchange(array, devices, stage):
    orders = [bit_order(devices, core) for core in range(CORES)]
    pairs = [(i, i ^ (1 << orders[i & 1][stage])) for i in range(devices)]
    return lax.ppermute(array, "user", pairs)


def final_places(devices):
    bits = devices.bit_length() - 1
    return [
        [
            sum(
                ((place >> (bits - 2 - n)) & 1) << (bit - 1)
                for n, bit in enumerate(bit_order(devices, core))
            )
            for place in range(devices // 2)
        ]
        for core in range(CORES)
    ]


def local(
    ratings,
    tile_index,
    tile_count,
    side_features,
    user_factors,
    item_factors,
    prior_weights,
    user_noise,
    item_noise,
):
    devices = lax.axis_size("user")
    stages = devices.bit_length() - 2
    strata = ratings.shape[1]
    feat = prior_weights.shape[0]
    rate = rate_scale / (user_factors.shape[0] * devices)
    own_turned = turn_pass(side_features)
    own_mean, other_mean, send, offset, old = first_pass(
        devices, side_features, own_turned, prior_weights, user_factors
    )
    held = keep_pass(own_turned, offset)
    send, held = step_pass(True, 0, devices, held, swap(send, devices), feat)
    users, items = user_factors, [item_factors]
    for stratum in range(strata):
        last = stratum + 1 == strata
        got = exchange(send, devices, 0)
        later = send if stratum else own_turned
        err_b, stats = error_pass(stratum, tile_index, tile_count, ratings, users, later, *items)
        state = grad_pass(stratum, err_b, user_noise, item_noise, users, *items)
        riders = (stats, exchange(stats, devices, 0))
        send, held = step_pass(True, 1, devices, held, got, got.shape[0], riders)
        for stage in range(1, stages - 1):
            got = exchange(send, devices, stage)
            rows = got.shape[0] - RIDERS
            later = state[:1] if stage == 1 else ()
            if last:
                send, held = step_pass(True, stage + 1, devices, held, got, rows, (send, got), later)
            else:
                (send,) = step_pass(False, 0, devices, held, got, rows, (send, got), later)
                held = send
            if stratum == 0 and stage == 1:
                wide = [swap(part, devices) for part in widen_pass(side_features, send)]
                feats, turned = join_pass(side_features, own_turned, *wide)
        got = exchange(send, devices, stages - 1)
        part, stats = update_pass(rate, held, got, send, old)
        if last:
            break
        users, *items = renew_pass(
            devices, stats, swap(stats, devices), *state[:2], own_mean, other_mean, *state[2:]
        )
        old = part
        *items, own_cols, other_cols = items
        items = [roll(rows, devices) for rows in items]
        other_cols = swap(other_cols, devices)
        part = gather_pass(1, devices, part, exchange(part, devices, 1), [users])
        got = exchange(part, devices, 0)
        begun = part_pass(devices, feats, part)
        own_mean, other_mean, send, held, *olds = prior_pass(
            devices,
            feats,
            turned,
            begun,
            part,
            got,
            own_cols,
            other_cols,
            items[0],
            final_places(devices) if stratum + 2 == strata else None,
        )
        if olds:
            (old,) = olds
        other_mean = swap(other_mean, devices)
    mine, other = split_pass(devices, part, stats)
    return last_pass(
        devices, stats, mine, swap(other, devices), *state[:2], own_mean, other_mean, *state[2:]
    )


def solution(mesh):
    return jax.shard_map(
        local,
        mesh=mesh,
        in_specs=(
            P("user", None, None, None, None),
            P("user", None, None),
            P("user", None),
            P("user", None),
            P("user", None),
            P("user", None),
            P(),
            P(None, "user", None),
            P(None, "user", None),
        ),
        out_specs=(P("user", None), P("user", None), P("user", None)),
        check_vma=False,
    )
```

```python
import functools
import math

import jax
import jax.numpy as jnp
from jax import lax
from jax.experimental import pallas as pl
from jax.experimental.pallas import tpu as pltpu
from jax.sharding import PartitionSpec as P

step_size = 0.01
prior_prec = 8.0
item_prec = 1.0
weight_decay = 1.0
rate_scale = 0.04

CORES = 2
RIDERS = 8
ITEM_PARTS = 1
FEAT_PARTS = 3
NN = (((1,), (0,)), ((), ()))
NT = (((1,), (1,)), ((), ()))
TN = (((0,), (0,)), ((), ()))
VMEM = pl.BlockSpec(memory_space=pltpu.VMEM)
SMEM = pl.BlockSpec(memory_space=pltpu.SMEM)
ANY = pl.BlockSpec(memory_space=pl.ANY)
PARAMS = pltpu.CompilerParams(vmem_limit_bytes=8 << 20)
f32 = jnp.float32
bf16 = jnp.bfloat16


def dot(a, b, dims=NN):
    return lax.dot_general(a, b, dims, preferred_element_type=f32)


def shape(*dims, dtype=f32):
    return jax.ShapeDtypeStruct(dims, dtype)


def cost(flops, size):
    return pl.CostEstimate(flops=flops, bytes_accessed=size, transcendentals=0)


def where_am_i(devices):
    own = lax.axis_index("user")
    core = own & 1
    zero, one = (bit_order(devices, c) for c in range(CORES))
    bits = [jnp.where(core == 0, own >> z, own >> o) & 1 for z, o in zip(zero, one, strict=True)]
    return [core, *bits, own >> 1]


def rows_at(which, rows):
    start = which * rows
    return pl.ds(pl.multiple_of(start, rows) if rows % 8 == 0 else start, rows)


def half_of(ref, core):
    width = ref.shape[1] // CORES
    return ref[:, pl.ds(pl.multiple_of(core * width, width), width)]


def precision_of(stats):
    return (1.0 + stats[1:2, :] / 2.0) / (1.0 + stats[0:1, :] / 2.0)


def error_kernel(stratum, codes, count, ratings, users, *refs):
    items, (err_b, stats, pred) = refs[1:-3], refs[-3:]
    tile = ratings.shape[-1]
    grid = users.shape[0] // tile
    user_b = users[...].astype(bf16)
    start = 0
    for part in items:
        pred[:, start : start + part.shape[0]] = dot(user_b, part[...].astype(bf16), NT)
        start += part.shape[0]
    err_b[...] = jnp.zeros_like(err_b)
    live_slots = count[0, stratum]
    sse = jnp.zeros((tile, tile), f32)
    for slot in range(ratings.shape[2]):
        code = codes[0, stratum, slot]
        at_rows = rows_at(code // grid, tile)
        at_cols = rows_at(code % grid, tile)
        live = (slot < live_slots).astype(f32)
        err = (ratings[0, stratum, slot].astype(f32) - pred[at_rows, at_cols]) * live
        sse = sse + err * err
        err_b[at_rows, at_cols] = err.astype(bf16)
    total = jnp.sum(sse)
    counted = live_slots.astype(f32) * float(tile * tile)
    row = lax.broadcasted_iota(jnp.int32, stats.shape, 0)
    stats[...] = jnp.where(row == 0, total, jnp.where(row == 1, counted, 0.0))


def error_pass(stratum, codes, count, ratings, users, later, *items):
    rows, rank = users.shape
    return pl.pallas_call(
        functools.partial(error_kernel, stratum),
        out_shape=(shape(rows, rows, dtype=bf16), shape(RIDERS, rank // CORES)),
        in_specs=[SMEM] * 2 + [VMEM] * 2 + [ANY] + [VMEM] * len(items),
        out_specs=(VMEM,) * 2,
        scratch_shapes=[pltpu.VMEM((rows, rows), f32)],
        compiler_params=PARAMS,
        cost_estimate=cost(24 * rows * rows * rank, 64 * rows * rank),
        name="error_pass",
    )(codes, count, ratings, users, later, *items)


def grad_kernel(stratum, noise_scale, err_b, user_noise, item_noise, users, *refs):
    items, (base_u, grad_u, base_v, grad_v) = refs[:-4], refs[-4:]
    item_b = jnp.concatenate([part[...].astype(bf16) for part in items], 0)
    grad_u[...] = step_size * dot(err_b[...], item_b)
    grad_v[...] = step_size * dot(err_b[...], users[...].astype(bf16), TN)
    noise = noise_scale * user_noise[stratum].astype(f32)
    base_u[...] = (1.0 - step_size * prior_prec) * users[...] + noise
    start = 0
    for part in items:
        at = slice(start, start + part.shape[0])
        noise = noise_scale * item_noise[stratum, at].astype(f32)
        base_v[at, :] = (1.0 - step_size * item_prec) * part[...] + noise
        start += part.shape[0]


def grad_pass(stratum, err_b, user_noise, item_noise, users, *items):
    rows, rank = users.shape
    return pl.pallas_call(
        functools.partial(grad_kernel, stratum, math.sqrt(2.0 * step_size)),
        out_shape=(shape(rows, rank),) * 4,
        in_specs=[VMEM] * (4 + len(items)),
        out_specs=(VMEM,) * 4,
        compiler_params=PARAMS,
        cost_estimate=cost(4 * rows * rows * rank, 28 * rows * rank),
        name="grad_pass",
    )(err_b, user_noise, item_noise, users, *items)


def turn_kernel(feats, turned):
    turned[...] = feats[...].T


def turn_pass(feats):
    rows, feat = feats.shape
    return pl.pallas_call(
        turn_kernel,
        out_shape=shape(feat, rows, dtype=bf16),
        in_specs=[VMEM],
        out_specs=VMEM,
        compiler_params=PARAMS,
        cost_estimate=cost(rows * feat, 4 * rows * feat),
        name="turn_pass",
    )(feats)


def first_kernel(devices, feats, turned, weights, users, own_mean, other_mean, send, keep, old, mean):
    place = where_am_i(devices)
    here = place[0]
    mean[...] = dot(feats[...], weights[...].astype(bf16))
    for grad, means, which in ((send, other_mean, 1 - here), (keep, own_mean, here)):
        mean_now = half_of(mean, which)
        means[...] = mean_now
        offset = (half_of(users, which) - mean_now).astype(bf16)
        grad[...] = dot(turned[...], offset)
    rows, width = old.shape
    old[...] = weights[rows_at(2 * place[1] + place[2], rows), rows_at(here, width)]


def first_pass(devices, feats, turned, weights, users):
    rows, rank = users.shape
    feat = weights.shape[0]
    width = rank // CORES
    return pl.pallas_call(
        functools.partial(first_kernel, devices),
        out_shape=(shape(rows, width),) * 2 + (shape(feat, width),) * 2 + (shape(feat // 4, width),),
        in_specs=[VMEM] * 4,
        out_specs=(VMEM,) * 5,
        scratch_shapes=[pltpu.VMEM(users.shape, f32)],
        compiler_params=PARAMS,
        cost_estimate=cost(4 * rows * feat * rank, 8 * feat * rank),
        name="first_pass",
    )(feats, turned, weights, users)


def widen_kernel(narrow, later, *wide):
    rows = wide[0].shape[0]
    for n, ref in enumerate(wide):
        ref[...] = narrow[n * rows : (n + 1) * rows, :].astype(f32)


def widen_pass(narrow, later):
    rows, feat = narrow.shape
    return pl.pallas_call(
        widen_kernel,
        out_shape=(shape(rows // FEAT_PARTS, feat),) * FEAT_PARTS,
        in_specs=[VMEM, ANY],
        out_specs=(VMEM,) * FEAT_PARTS,
        compiler_params=PARAMS,
        name="widen_pass",
    )(narrow, later)


def join_kernel(own, own_turned, *refs):
    others, (both, turned) = refs[:-2], refs[-2:]
    rows = own.shape[0]
    both[:rows, :] = own[...]
    turned[:, :rows] = own_turned[...]
    for other in others:
        at = slice(rows, rows + other.shape[0])
        both[at, :] = other[...].astype(bf16)
        turned[:, at] = other[...].T.astype(bf16)
        rows += other.shape[0]


def join_pass(own, own_turned, *others):
    rows, feat = own.shape
    return pl.pallas_call(
        join_kernel,
        out_shape=(shape(CORES * rows, feat, dtype=bf16), shape(feat, CORES * rows, dtype=bf16)),
        in_specs=[VMEM] * (2 + len(others)),
        out_specs=(VMEM, VMEM),
        compiler_params=PARAMS,
        cost_estimate=cost(rows * feat, 12 * rows * feat),
        name="join_pass",
    )(own, own_turned, *others)


def part_kernel(devices, feats, part, mean):
    half = part.shape[0]
    bit = where_am_i(devices)[1]
    here = pl.ds(pl.multiple_of(bit * half, half), half)
    mean[...] = dot(feats[:, here], part[...].astype(bf16))


def part_pass(devices, feats, part):
    rows = feats.shape[0]
    half, width = part.shape
    return pl.pallas_call(
        functools.partial(part_kernel, devices),
        out_shape=shape(rows, width),
        in_specs=[VMEM, VMEM],
        out_specs=VMEM,
        compiler_params=PARAMS,
        cost_estimate=cost(2 * rows * half * width, 4 * rows * half),
        name="part_pass",
    )(feats, part)


def prior_kernel(places, devices, feats, turned, begun, part, got, own_cols, other_cols, later, own_mean, other_mean, send, keep, *refs):
    rows = own_cols.shape[0]
    half = keep.shape[0]
    place = where_am_i(devices)
    core, bit = place[0], place[1]
    here = pl.ds(pl.multiple_of(bit * half, half), half)
    there = pl.ds(pl.multiple_of((1 - bit) * half, half), half)
    offset = refs[-1]
    mean = begun[...] + dot(feats[:, there], got[...].astype(bf16))
    own_mean[...] = mean[:rows]
    other_mean[...] = mean[rows:]
    offset[:rows, :] = (own_cols[...] - mean[:rows]).astype(bf16)
    offset[rows:, :] = (other_cols[...] - mean[rows:]).astype(bf16)
    if places is None:
        send[...] = dot(turned[there, :], offset[...])
        keep[...] = dot(turned[here, :], offset[...])
        return
    old, full = refs[:2]
    full[here, :] = part[...]
    full[there, :] = got[...]
    start = place[-1] * old.shape[0]
    if old.shape[0] % 8 == 0:
        start = pl.multiple_of(start, old.shape[0])
    old[...] = full[pl.ds(start, old.shape[0]), :]
    full[...] = dot(turned[...], offset[...])
    blocks = len(places[0])
    block = 2 * half // blocks
    for ref, which in ((send, 1 - bit), (keep, bit)):
        for n in range(blocks // 2):
            source = jnp.int32(0)
            for c, order in enumerate(places):
                for b in range(2):
                    source = jnp.where((core == c) & (which == b), order[b * blocks // 2 + n], source)
            source = source * block
            if block % 8 == 0:
                source = pl.multiple_of(source, block)
            ref[n * block : (n + 1) * block, :] = full[pl.ds(source, block), :]


def prior_pass(devices, feats, turned, begun, part, got, own_cols, other_cols, later, places=None):
    rows, width = own_cols.shape
    half = part.shape[0]
    outs = [shape(rows, width)] * 2 + [shape(half, width)] * 2
    scratch = [pltpu.VMEM((CORES * rows, width), bf16)]
    if places is not None:
        outs.append(shape(2 * half // len(places[0]), width))
        scratch.insert(0, pltpu.VMEM((2 * half, width), f32))
    return pl.pallas_call(
        functools.partial(prior_kernel, places, devices),
        out_shape=tuple(outs),
        in_specs=[VMEM] * 7 + [ANY],
        out_specs=(VMEM,) * len(outs),
        scratch_shapes=scratch,
        compiler_params=PARAMS,
        cost_estimate=cost(16 * rows * half * width, 16 * rows * half),
        name="prior_pass",
    )(feats, turned, begun, part, got, own_cols, other_cols, later)


def step_kernel(halving, stage, under, devices, held, got, *refs):
    send = refs[-2] if halving else refs[-1]
    rows = send.shape[0] - under
    if halving:
        bit = where_am_i(devices)[1 + stage]
        for ref, which in ((send, 1 - bit), (refs[-1], bit)):
            at = rows_at(which, rows)
            ref[:rows, :] = held[at, :] + got[at, :]
    else:
        send[:rows, :] = held[:rows, :] + got[:rows, :]
    if under:
        sent, more = refs[:2]
        send[rows:, :] = sent[sent.shape[0] - under :, :] + more[more.shape[0] - under :, :]


def step_pass(halving, stage, devices, held, got, rows, riders=(), later=()):
    width = held.shape[1]
    under = RIDERS if riders else 0
    outs = [shape(rows // 2 + under, width), shape(rows // 2, width)] if halving else [shape(rows + under, width)]
    return pl.pallas_call(
        functools.partial(step_kernel, halving, stage, under, devices),
        out_shape=tuple(outs),
        in_specs=[VMEM] * (2 + len(riders)) + [ANY] * len(later),
        out_specs=(VMEM,) * len(outs),
        compiler_params=PARAMS,
        cost_estimate=cost(rows * width, 12 * rows * width),
        name="step_pass",
    )(held, got, *riders, *later)


def update_kernel(rate, held, got, sent, old, *refs):
    new, stats = refs[-2:]
    rows = old.shape[0]
    total = held[:rows, :] + got[:rows, :]
    before = old[...]
    new[...] = before + rate * (prior_prec * total - weight_decay * before)
    stats[...] = sent[sent.shape[0] - RIDERS :, :] + got[rows:, :]


def update_pass(rate, held, got, sent, old, later=()):
    return pl.pallas_call(
        functools.partial(update_kernel, rate),
        out_shape=(shape(*old.shape), shape(RIDERS, old.shape[1])),
        in_specs=[VMEM] * 4 + [ANY] * len(later),
        out_specs=(VMEM,) * 2,
        compiler_params=PARAMS,
        cost_estimate=cost(4 * old.size, 16 * old.size),
        name="update_pass",
    )(held, got, sent, old, *later)


def gather_kernel(slot, devices, part, got, *refs):
    both = refs[-1]
    rows = part.shape[0]
    bit = where_am_i(devices)[slot]
    both[pl.ds(pl.multiple_of(bit * rows, rows), rows), :] = part[...]
    both[pl.ds(pl.multiple_of((1 - bit) * rows, rows), rows), :] = got[...]


def gather_pass(stage, devices, part, got, later=()):
    rows, width = part.shape
    return pl.pallas_call(
        functools.partial(gather_kernel, 1 + stage, devices),
        out_shape=shape(2 * rows, width),
        in_specs=[VMEM, VMEM] + [ANY] * len(later),
        out_specs=VMEM,
        compiler_params=PARAMS,
        cost_estimate=cost(rows * width, 16 * rows * width),
        name="gather_pass",
    )(part, got, *later)


def split_kernel(devices, both, stats, mine, other):
    rows = mine.shape[0]
    core = where_am_i(devices)[0]
    mine[...] = both[rows_at(core, rows), :]
    other[:rows, :] = both[rows_at(1 - core, rows), :]
    other[rows:, :] = stats[...]


def split_pass(devices, both, stats):
    rows, width = both.shape
    rows = rows // CORES
    return pl.pallas_call(
        functools.partial(split_kernel, devices),
        out_shape=(shape(rows, width), shape(rows + RIDERS, width)),
        in_specs=[VMEM] * 2,
        out_specs=(VMEM,) * 2,
        compiler_params=PARAMS,
        name="split_pass",
    )(both, stats)


def renew(core, stats, base_u, grad_u, own_mean, other_mean, base_v, grad_v, users, *items):
    width = own_mean.shape[1]
    precision = precision_of(stats)
    precision = jnp.concatenate([precision] * CORES, 1)
    rows = base_v.shape[0] // len(items)
    for n, ref in enumerate(items):
        at = slice(n * rows, (n + 1) * rows)
        ref[...] = base_v[at, :] + precision * grad_v[at, :]
    new = base_u[...] + precision * grad_u[...]
    pull = step_size * prior_prec
    left = jnp.where(core == 0, own_mean[...], other_mean[...])
    right = jnp.where(core == 0, other_mean[...], own_mean[...])
    users[:, :width] = new[:, :width] + pull * left
    users[:, width:] = new[:, width:] + pull * right


def renew_kernel(devices, stats, more, *refs):
    core = where_am_i(devices)[0]
    renew(core, stats[...] + more[...], *refs[:-2])
    users = refs[6]
    for ref, which in zip(refs[-2:], (core, 1 - core), strict=True):
        ref[...] = half_of(users, which)


def renew_pass(devices, stats, more, base_u, grad_u, own_mean, *state):
    rows, rank = base_u.shape
    outs = [shape(rows, rank)] + [shape(rows // ITEM_PARTS, rank)] * ITEM_PARTS + [shape(*own_mean.shape)] * 2
    return pl.pallas_call(
        functools.partial(renew_kernel, devices),
        out_shape=tuple(outs),
        in_specs=[VMEM] * 8,
        out_specs=(VMEM,) * len(outs),
        compiler_params=PARAMS,
        cost_estimate=cost(8 * base_u.size, 32 * base_u.size),
        name="renew_pass",
    )(stats, more, base_u, grad_u, own_mean, *state)


def last_kernel(devices, stats, mine, got, *refs):
    core = where_am_i(devices)[0]
    weights = refs[-1]
    rows, width = mine.shape
    weights[:, rows_at(core, width)] = mine[...]
    weights[:, rows_at(1 - core, width)] = got[:rows, :]
    renew(core, stats[...] + got[rows:, :], *refs[:-1])


def last_pass(devices, stats, mine, got, base_u, *state):
    rows, width = mine.shape
    return pl.pallas_call(
        functools.partial(last_kernel, devices),
        out_shape=(shape(*base_u.shape),) * 2 + (shape(rows, CORES * width),),
        in_specs=[VMEM] * 9,
        out_specs=(VMEM,) * 3,
        compiler_params=PARAMS,
        cost_estimate=cost(8 * base_u.size, 32 * base_u.size),
        name="last_pass",
    )(stats, mine, got, base_u, *state)


def bit_order(devices, core):
    bits = devices.bit_length() - 1
    far = list(range(3, bits))
    return [1, 2] + far[::-1] if core == 0 else [2, 1] + far


def swap(array, devices):
    return lax.ppermute(array, "user", [(i, i ^ 1) for i in range(devices)])


def roll(array, devices):
    return lax.ppermute(array, "user", [(i, (i + 1) % devices) for i in range(devices)])


def exchange(array, devices, stage):
    orders = [bit_order(devices, core) for core in range(CORES)]
    pairs = [(i, i ^ (1 << orders[i & 1][stage])) for i in range(devices)]
    return lax.ppermute(array, "user", pairs)


def final_places(devices):
    bits = devices.bit_length() - 1
    return [
        [
            sum(
                ((place >> (bits - 2 - n)) & 1) << (bit - 1)
                for n, bit in enumerate(bit_order(devices, core))
            )
            for place in range(devices // 2)
        ]
        for core in range(CORES)
    ]


def local(
    ratings,
    tile_index,
    tile_count,
    side_features,
    user_factors,
    item_factors,
    prior_weights,
    user_noise,
    item_noise,
):
    devices = lax.axis_size("user")
    stages = devices.bit_length() - 2
    strata = ratings.shape[1]
    feat = prior_weights.shape[0]
    rate = rate_scale / (user_factors.shape[0] * devices)
    own_turned = turn_pass(side_features)
    own_mean, other_mean, send, held, old = first_pass(
        devices, side_features, own_turned, prior_weights, user_factors
    )
    send, held = step_pass(True, 0, devices, held, swap(send, devices), feat)
    users, items = user_factors, [item_factors]
    for stratum in range(strata):
        last = stratum + 1 == strata
        got = exchange(send, devices, 0)
        later = send if stratum else own_turned
        err_b, stats = error_pass(stratum, tile_index, tile_count, ratings, users, later, *items)
        state = grad_pass(stratum, err_b, user_noise, item_noise, users, *items)
        riders = (stats, exchange(stats, devices, 0))
        send, held = step_pass(True, 1, devices, held, got, got.shape[0], riders)
        for stage in range(1, stages - 1):
            got = exchange(send, devices, stage)
            rows = got.shape[0] - RIDERS
            later = state[:1] if stage == 1 else ()
            if last:
                send, held = step_pass(True, stage + 1, devices, held, got, rows, (send, got), later)
            else:
                (send,) = step_pass(False, 0, devices, held, got, rows, (send, got), later)
                held = send
            if stratum == 0 and stage == 1:
                wide = [swap(part, devices) for part in widen_pass(side_features, send)]
                feats, turned = join_pass(side_features, own_turned, *wide)
        got = exchange(send, devices, stages - 1)
        part, stats = update_pass(rate, held, got, send, old)
        if last:
            break
        users, *items = renew_pass(
            devices, stats, swap(stats, devices), *state[:2], own_mean, other_mean, *state[2:]
        )
        old = part
        *items, own_cols, other_cols = items
        items = [roll(rows, devices) for rows in items]
        other_cols = swap(other_cols, devices)
        part = gather_pass(1, devices, part, exchange(part, devices, 1), [users])
        got = exchange(part, devices, 0)
        begun = part_pass(devices, feats, part)
        own_mean, other_mean, send, held, *olds = prior_pass(
            devices,
            feats,
            turned,
            begun,
            part,
            got,
            own_cols,
            other_cols,
            items[0],
            final_places(devices) if stratum + 2 == strata else None,
        )
        if olds:
            (old,) = olds
        other_mean = swap(other_mean, devices)
    mine, other = split_pass(devices, part, stats)
    return last_pass(
        devices, stats, mine, swap(other, devices), *state[:2], own_mean, other_mean, *state[2:]
    )


def solution(mesh):
    return jax.shard_map(
        local,
        mesh=mesh,
        in_specs=(
            P("user", None, None, None, None),
            P("user", None, None),
            P("user", None),
            P("user", None),
            P("user", None),
            P("user", None),
            P(),
            P(None, "user", None),
            P(None, "user", None),
        ),
        out_specs=(P("user", None), P("user", None), P("user", None)),
        check_vma=False,
    )
```

```python
import functools
import math

import jax
import jax.numpy as jnp
from jax import lax
from jax.experimental import pallas as pl
from jax.experimental.pallas import tpu as pltpu
from jax.sharding import PartitionSpec as P

step_size = 0.01
prior_prec = 8.0
item_prec = 1.0
weight_decay = 1.0
rate_scale = 0.04

CORES = 2
RIDERS = 8
ITEM_PARTS = 1
FEAT_PARTS = 3
NN = (((1,), (0,)), ((), ()))
NT = (((1,), (1,)), ((), ()))
TN = (((0,), (0,)), ((), ()))
VMEM = pl.BlockSpec(memory_space=pltpu.VMEM)
SMEM = pl.BlockSpec(memory_space=pltpu.SMEM)
ANY = pl.BlockSpec(memory_space=pl.ANY)
PARAMS = pltpu.CompilerParams(vmem_limit_bytes=8 << 20)
f32 = jnp.float32
bf16 = jnp.bfloat16


def dot(a, b, dims=NN):
    return lax.dot_general(a, b, dims, preferred_element_type=f32)


def shape(*dims, dtype=f32):
    return jax.ShapeDtypeStruct(dims, dtype)


def cost(flops, size):
    return pl.CostEstimate(flops=flops, bytes_accessed=size, transcendentals=0)


def where_am_i(devices):
    own = lax.axis_index("user")
    core = own & 1
    zero, one = (bit_order(devices, c) for c in range(CORES))
    bits = [jnp.where(core == 0, own >> z, own >> o) & 1 for z, o in zip(zero, one, strict=True)]
    return [core, *bits, own >> 1]


def rows_at(which, rows):
    start = which * rows
    return pl.ds(pl.multiple_of(start, rows) if rows % 8 == 0 else start, rows)


def half_of(ref, core):
    width = ref.shape[1] // CORES
    return ref[:, pl.ds(pl.multiple_of(core * width, width), width)]


def precision_of(stats):
    return (1.0 + stats[1:2, :] / 2.0) / (1.0 + stats[0:1, :] / 2.0)


def error_kernel(stratum, codes, count, ratings, users, *refs):
    items, (err_b, stats, pred) = refs[1:-3], refs[-3:]
    tile = ratings.shape[-1]
    grid = users.shape[0] // tile
    user_b = users[...].astype(bf16)
    start = 0
    for part in items:
        pred[:, start : start + part.shape[0]] = dot(user_b, part[...].astype(bf16), NT)
        start += part.shape[0]
    err_b[...] = jnp.zeros_like(err_b)
    live_slots = count[0, stratum]
    sse = jnp.zeros((tile, tile), f32)
    for slot in range(ratings.shape[2]):
        code = codes[0, stratum, slot]
        at_rows = rows_at(code // grid, tile)
        at_cols = rows_at(code % grid, tile)
        live = (slot < live_slots).astype(f32)
        err = (ratings[0, stratum, slot].astype(f32) - pred[at_rows, at_cols]) * live
        sse = sse + err * err
        err_b[at_rows, at_cols] = err.astype(bf16)
    total = jnp.sum(sse)
    counted = live_slots.astype(f32) * float(tile * tile)
    row = lax.broadcasted_iota(jnp.int32, stats.shape, 0)
    stats[...] = jnp.where(row == 0, total, jnp.where(row == 1, counted, 0.0))


def error_pass(stratum, codes, count, ratings, users, later, *items):
    rows, rank = users.shape
    return pl.pallas_call(
        functools.partial(error_kernel, stratum),
        out_shape=(shape(rows, rows, dtype=bf16), shape(RIDERS, rank // CORES)),
        in_specs=[SMEM] * 2 + [VMEM] * 2 + [ANY] + [VMEM] * len(items),
        out_specs=(VMEM,) * 2,
        scratch_shapes=[pltpu.VMEM((rows, rows), f32)],
        compiler_params=PARAMS,
        cost_estimate=cost(24 * rows * rows * rank, 64 * rows * rank),
        name="error_pass",
    )(codes, count, ratings, users, later, *items)


def grad_kernel(stratum, noise_scale, err_b, user_noise, item_noise, users, *refs):
    items, (base_u, grad_u, base_v, grad_v) = refs[:-4], refs[-4:]
    item_b = jnp.concatenate([part[...].astype(bf16) for part in items], 0)
    grad_u[...] = step_size * dot(err_b[...], item_b)
    grad_v[...] = step_size * dot(err_b[...], users[...].astype(bf16), TN)
    noise = noise_scale * user_noise[stratum].astype(f32)
    base_u[...] = (1.0 - step_size * prior_prec) * users[...] + noise
    start = 0
    for part in items:
        at = slice(start, start + part.shape[0])
        noise = noise_scale * item_noise[stratum, at].astype(f32)
        base_v[at, :] = (1.0 - step_size * item_prec) * part[...] + noise
        start += part.shape[0]


def grad_pass(stratum, err_b, user_noise, item_noise, users, *items):
    rows, rank = users.shape
    return pl.pallas_call(
        functools.partial(grad_kernel, stratum, math.sqrt(2.0 * step_size)),
        out_shape=(shape(rows, rank),) * 4,
        in_specs=[VMEM] * (4 + len(items)),
        out_specs=(VMEM,) * 4,
        compiler_params=PARAMS,
        cost_estimate=cost(4 * rows * rows * rank, 28 * rows * rank),
        name="grad_pass",
    )(err_b, user_noise, item_noise, users, *items)


def turn_kernel(feats, turned):
    turned[...] = feats[...].T


def turn_pass(feats):
    rows, feat = feats.shape
    return pl.pallas_call(
        turn_kernel,
        out_shape=shape(feat, rows, dtype=bf16),
        in_specs=[VMEM],
        out_specs=VMEM,
        compiler_params=PARAMS,
        cost_estimate=cost(rows * feat, 4 * rows * feat),
        name="turn_pass",
    )(feats)


def first_kernel(devices, feats, turned, weights, users, own_mean, other_mean, send, offset, old, mean):
    place = where_am_i(devices)
    here = place[0]
    mean[...] = dot(feats[...], weights[...].astype(bf16))
    other_mean[...] = half_of(mean, 1 - here)
    send[...] = dot(turned[...], (half_of(users, 1 - here) - other_mean[...]).astype(bf16))
    own_mean[...] = half_of(mean, here)
    offset[...] = (half_of(users, here) - own_mean[...]).astype(bf16)
    rows, width = old.shape
    old[...] = weights[rows_at(2 * place[1] + place[2], rows), rows_at(here, width)]


def first_pass(devices, feats, turned, weights, users):
    rows, rank = users.shape
    feat = weights.shape[0]
    width = rank // CORES
    return pl.pallas_call(
        functools.partial(first_kernel, devices),
        out_shape=(shape(rows, width),) * 2
        + (shape(feat, width), shape(rows, width, dtype=bf16), shape(feat // 4, width)),
        in_specs=[VMEM] * 4,
        out_specs=(VMEM,) * 5,
        scratch_shapes=[pltpu.VMEM(users.shape, f32)],
        compiler_params=PARAMS,
        cost_estimate=cost(3 * rows * feat * rank, 8 * feat * rank),
        name="first_pass",
    )(feats, turned, weights, users)


def keep_kernel(turned, offset, grad):
    grad[...] = dot(turned[...], offset[...])


def keep_pass(turned, offset):
    feat, rows = turned.shape
    width = offset.shape[1]
    return pl.pallas_call(
        keep_kernel,
        out_shape=shape(feat, width),
        in_specs=[VMEM] * 2,
        out_specs=VMEM,
        compiler_params=PARAMS,
        cost_estimate=cost(2 * rows * feat * width, 4 * feat * width),
        name="keep_pass",
    )(turned, offset)


def widen_kernel(narrow, later, *wide):
    rows = wide[0].shape[0]
    for n, ref in enumerate(wide):
        ref[...] = narrow[n * rows : (n + 1) * rows, :].astype(f32)


def widen_pass(narrow, later):
    rows, feat = narrow.shape
    return pl.pallas_call(
        widen_kernel,
        out_shape=(shape(rows // FEAT_PARTS, feat),) * FEAT_PARTS,
        in_specs=[VMEM, ANY],
        out_specs=(VMEM,) * FEAT_PARTS,
        compiler_params=PARAMS,
        name="widen_pass",
    )(narrow, later)


def join_kernel(own, own_turned, *refs):
    others, (both, turned) = refs[:-2], refs[-2:]
    rows = own.shape[0]
    both[:rows, :] = own[...]
    turned[:, :rows] = own_turned[...]
    for other in others:
        at = slice(rows, rows + other.shape[0])
        both[at, :] = other[...].astype(bf16)
        turned[:, at] = other[...].T.astype(bf16)
        rows += other.shape[0]


def join_pass(own, own_turned, *others):
    rows, feat = own.shape
    return pl.pallas_call(
        join_kernel,
        out_shape=(shape(CORES * rows, feat, dtype=bf16), shape(feat, CORES * rows, dtype=bf16)),
        in_specs=[VMEM] * (2 + len(others)),
        out_specs=(VMEM, VMEM),
        compiler_params=PARAMS,
        cost_estimate=cost(rows * feat, 12 * rows * feat),
        name="join_pass",
    )(own, own_turned, *others)


def part_kernel(devices, feats, part, mean):
    half = part.shape[0]
    bit = where_am_i(devices)[1]
    here = pl.ds(pl.multiple_of(bit * half, half), half)
    mean[...] = dot(feats[:, here], part[...].astype(bf16))


def part_pass(devices, feats, part):
    rows = feats.shape[0]
    half, width = part.shape
    return pl.pallas_call(
        functools.partial(part_kernel, devices),
        out_shape=shape(rows, width),
        in_specs=[VMEM, VMEM],
        out_specs=VMEM,
        compiler_params=PARAMS,
        cost_estimate=cost(2 * rows * half * width, 4 * rows * half),
        name="part_pass",
    )(feats, part)


def prior_kernel(places, devices, feats, turned, begun, part, got, own_cols, other_cols, later, own_mean, other_mean, send, keep, *refs):
    rows = own_cols.shape[0]
    half = keep.shape[0]
    place = where_am_i(devices)
    core, bit = place[0], place[1]
    here = pl.ds(pl.multiple_of(bit * half, half), half)
    there = pl.ds(pl.multiple_of((1 - bit) * half, half), half)
    offset = refs[-1]
    mean = begun[...] + dot(feats[:, there], got[...].astype(bf16))
    own_mean[...] = mean[:rows]
    other_mean[...] = mean[rows:]
    offset[:rows, :] = (own_cols[...] - mean[:rows]).astype(bf16)
    offset[rows:, :] = (other_cols[...] - mean[rows:]).astype(bf16)
    if places is None:
        send[...] = dot(turned[there, :], offset[...])
        keep[...] = dot(turned[here, :], offset[...])
        return
    old, full = refs[:2]
    full[here, :] = part[...]
    full[there, :] = got[...]
    start = place[-1] * old.shape[0]
    if old.shape[0] % 8 == 0:
        start = pl.multiple_of(start, old.shape[0])
    old[...] = full[pl.ds(start, old.shape[0]), :]
    full[...] = dot(turned[...], offset[...])
    blocks = len(places[0])
    block = 2 * half // blocks
    for ref, which in ((send, 1 - bit), (keep, bit)):
        for n in range(blocks // 2):
            source = jnp.int32(0)
            for c, order in enumerate(places):
                for b in range(2):
                    source = jnp.where((core == c) & (which == b), order[b * blocks // 2 + n], source)
            source = source * block
            if block % 8 == 0:
                source = pl.multiple_of(source, block)
            ref[n * block : (n + 1) * block, :] = full[pl.ds(source, block), :]


def prior_pass(devices, feats, turned, begun, part, got, own_cols, other_cols, later, places=None):
    rows, width = own_cols.shape
    half = part.shape[0]
    outs = [shape(rows, width)] * 2 + [shape(half, width)] * 2
    scratch = [pltpu.VMEM((CORES * rows, width), bf16)]
    if places is not None:
        outs.append(shape(2 * half // len(places[0]), width))
        scratch.insert(0, pltpu.VMEM((2 * half, width), f32))
    return pl.pallas_call(
        functools.partial(prior_kernel, places, devices),
        out_shape=tuple(outs),
        in_specs=[VMEM] * 7 + [ANY],
        out_specs=(VMEM,) * len(outs),
        scratch_shapes=scratch,
        compiler_params=PARAMS,
        cost_estimate=cost(16 * rows * half * width, 16 * rows * half),
        name="prior_pass",
    )(feats, turned, begun, part, got, own_cols, other_cols, later)


def step_kernel(halving, stage, under, devices, held, got, *refs):
    send = refs[-2] if halving else refs[-1]
    rows = send.shape[0] - under
    if halving:
        bit = where_am_i(devices)[1 + stage]
        for ref, which in ((send, 1 - bit), (refs[-1], bit)):
            at = rows_at(which, rows)
            ref[:rows, :] = held[at, :] + got[at, :]
    else:
        send[:rows, :] = held[:rows, :] + got[:rows, :]
    if under:
        sent, more = refs[:2]
        send[rows:, :] = sent[sent.shape[0] - under :, :] + more[more.shape[0] - under :, :]


def step_pass(halving, stage, devices, held, got, rows, riders=(), later=()):
    width = held.shape[1]
    under = RIDERS if riders else 0
    outs = [shape(rows // 2 + under, width), shape(rows // 2, width)] if halving else [shape(rows + under, width)]
    return pl.pallas_call(
        functools.partial(step_kernel, halving, stage, under, devices),
        out_shape=tuple(outs),
        in_specs=[VMEM] * (2 + len(riders)) + [ANY] * len(later),
        out_specs=(VMEM,) * len(outs),
        compiler_params=PARAMS,
        cost_estimate=cost(rows * width, 12 * rows * width),
        name="step_pass",
    )(held, got, *riders, *later)


def update_kernel(rate, held, got, sent, old, *refs):
    new, stats = refs[-2:]
    rows = old.shape[0]
    total = held[:rows, :] + got[:rows, :]
    before = old[...]
    new[...] = before + rate * (prior_prec * total - weight_decay * before)
    stats[...] = sent[sent.shape[0] - RIDERS :, :] + got[rows:, :]


def update_pass(rate, held, got, sent, old, later=()):
    return pl.pallas_call(
        functools.partial(update_kernel, rate),
        out_shape=(shape(*old.shape), shape(RIDERS, old.shape[1])),
        in_specs=[VMEM] * 4 + [ANY] * len(later),
        out_specs=(VMEM,) * 2,
        compiler_params=PARAMS,
        cost_estimate=cost(4 * old.size, 16 * old.size),
        name="update_pass",
    )(held, got, sent, old, *later)


def gather_kernel(slot, devices, part, got, *refs):
    both = refs[-1]
    rows = part.shape[0]
    bit = where_am_i(devices)[slot]
    both[pl.ds(pl.multiple_of(bit * rows, rows), rows), :] = part[...]
    both[pl.ds(pl.multiple_of((1 - bit) * rows, rows), rows), :] = got[...]


def gather_pass(stage, devices, part, got, later=()):
    rows, width = part.shape
    return pl.pallas_call(
        functools.partial(gather_kernel, 1 + stage, devices),
        out_shape=shape(2 * rows, width),
        in_specs=[VMEM, VMEM] + [ANY] * len(later),
        out_specs=VMEM,
        compiler_params=PARAMS,
        cost_estimate=cost(rows * width, 16 * rows * width),
        name="gather_pass",
    )(part, got, *later)


def split_kernel(devices, both, stats, mine, other):
    rows = mine.shape[0]
    core = where_am_i(devices)[0]
    mine[...] = both[rows_at(core, rows), :]
    other[:rows, :] = both[rows_at(1 - core, rows), :]
    other[rows:, :] = stats[...]


def split_pass(devices, both, stats):
    rows, width = both.shape
    rows = rows // CORES
    return pl.pallas_call(
        functools.partial(split_kernel, devices),
        out_shape=(shape(rows, width), shape(rows + RIDERS, width)),
        in_specs=[VMEM] * 2,
        out_specs=(VMEM,) * 2,
        compiler_params=PARAMS,
        name="split_pass",
    )(both, stats)


def renew(core, stats, base_u, grad_u, own_mean, other_mean, base_v, grad_v, users, *items):
    width = own_mean.shape[1]
    precision = precision_of(stats)
    precision = jnp.concatenate([precision] * CORES, 1)
    rows = base_v.shape[0] // len(items)
    for n, ref in enumerate(items):
        at = slice(n * rows, (n + 1) * rows)
        ref[...] = base_v[at, :] + precision * grad_v[at, :]
    new = base_u[...] + precision * grad_u[...]
    pull = step_size * prior_prec
    left = jnp.where(core == 0, own_mean[...], other_mean[...])
    right = jnp.where(core == 0, other_mean[...], own_mean[...])
    users[:, :width] = new[:, :width] + pull * left
    users[:, width:] = new[:, width:] + pull * right


def renew_kernel(devices, stats, more, *refs):
    core = where_am_i(devices)[0]
    renew(core, stats[...] + more[...], *refs[:-2])
    users = refs[6]
    for ref, which in zip(refs[-2:], (core, 1 - core), strict=True):
        ref[...] = half_of(users, which)


def renew_pass(devices, stats, more, base_u, grad_u, own_mean, *state):
    rows, rank = base_u.shape
    outs = [shape(rows, rank)] + [shape(rows // ITEM_PARTS, rank)] * ITEM_PARTS + [shape(*own_mean.shape)] * 2
    return pl.pallas_call(
        functools.partial(renew_kernel, devices),
        out_shape=tuple(outs),
        in_specs=[VMEM] * 8,
        out_specs=(VMEM,) * len(outs),
        compiler_params=PARAMS,
        cost_estimate=cost(8 * base_u.size, 32 * base_u.size),
        name="renew_pass",
    )(stats, more, base_u, grad_u, own_mean, *state)


def last_kernel(devices, stats, mine, got, *refs):
    core = where_am_i(devices)[0]
    weights = refs[-1]
    rows, width = mine.shape
    weights[:, rows_at(core, width)] = mine[...]
    weights[:, rows_at(1 - core, width)] = got[:rows, :]
    renew(core, stats[...] + got[rows:, :], *refs[:-1])


def last_pass(devices, stats, mine, got, base_u, *state):
    rows, width = mine.shape
    return pl.pallas_call(
        functools.partial(last_kernel, devices),
        out_shape=(shape(*base_u.shape),) * 2 + (shape(rows, CORES * width),),
        in_specs=[VMEM] * 9,
        out_specs=(VMEM,) * 3,
        compiler_params=PARAMS,
        cost_estimate=cost(8 * base_u.size, 32 * base_u.size),
        name="last_pass",
    )(stats, mine, got, base_u, *state)


def bit_order(devices, core):
    bits = devices.bit_length() - 1
    far = list(range(3, bits))
    return [1, 2] + far if core == 0 else [2, 1] + far[::-1]


def swap(array, devices):
    return lax.ppermute(array, "user", [(i, i ^ 1) for i in range(devices)])


def roll(array, devices):
    return lax.ppermute(array, "user", [(i, (i + 1) % devices) for i in range(devices)])


def exchange(array, devices, stage):
    orders = [bit_order(devices, core) for core in range(CORES)]
    pairs = [(i, i ^ (1 << orders[i & 1][stage])) for i in range(devices)]
    return lax.ppermute(array, "user", pairs)


def final_places(devices):
    bits = devices.bit_length() - 1
    return [
        [
            sum(
                ((place >> (bits - 2 - n)) & 1) << (bit - 1)
                for n, bit in enumerate(bit_order(devices, core))
            )
            for place in range(devices // 2)
        ]
        for core in range(CORES)
    ]


def local(
    ratings,
    tile_index,
    tile_count,
    side_features,
    user_factors,
    item_factors,
    prior_weights,
    user_noise,
    item_noise,
):
    devices = lax.axis_size("user")
    stages = devices.bit_length() - 2
    strata = ratings.shape[1]
    feat = prior_weights.shape[0]
    rate = rate_scale / (user_factors.shape[0] * devices)
    own_turned = turn_pass(side_features)
    own_mean, other_mean, send, offset, old = first_pass(
        devices, side_features, own_turned, prior_weights, user_factors
    )
    held = keep_pass(own_turned, offset)
    send, held = step_pass(True, 0, devices, held, swap(send, devices), feat)
    users, items = user_factors, [item_factors]
    for stratum in range(strata):
        last = stratum + 1 == strata
        got = exchange(send, devices, 0)
        later = send if stratum else own_turned
        err_b, stats = error_pass(stratum, tile_index, tile_count, ratings, users, later, *items)
        state = grad_pass(stratum, err_b, user_noise, item_noise, users, *items)
        riders = (stats, exchange(stats, devices, 0))
        send, held = step_pass(True, 1, devices, held, got, got.shape[0], riders)
        for stage in range(1, stages - 1):
            got = exchange(send, devices, stage)
            rows = got.shape[0] - RIDERS
            later = state[:1] if stage == 1 else ()
            if last:
                send, held = step_pass(True, stage + 1, devices, held, got, rows, (send, got), later)
            else:
                (send,) = step_pass(False, 0, devices, held, got, rows, (send, got), later)
                held = send
            if stratum == 0 and stage == 1:
                wide = [swap(part, devices) for part in widen_pass(side_features, send)]
                feats, turned = join_pass(side_features, own_turned, *wide)
        got = exchange(send, devices, stages - 1)
        part, stats = update_pass(rate, held, got, send, old)
        if last:
            break
        users, *items = renew_pass(
            devices, stats, swap(stats, devices), *state[:2], own_mean, other_mean, *state[2:]
        )
        old = part
        *items, own_cols, other_cols = items
        items = [roll(rows, devices) for rows in items]
        other_cols = swap(other_cols, devices)
        part = gather_pass(1, devices, part, exchange(part, devices, 1), [users])
        got = exchange(part, devices, 0)
        begun = part_pass(devices, feats, part)
        own_mean, other_mean, send, held, *olds = prior_pass(
            devices,
            feats,
            turned,
            begun,
            part,
            got,
            own_cols,
            other_cols,
            items[0],
            final_places(devices) if stratum + 2 == strata else None,
        )
        if olds:
            (old,) = olds
        other_mean = swap(other_mean, devices)
    mine, other = split_pass(devices, part, stats)
    return last_pass(
        devices, stats, mine, swap(other, devices), *state[:2], own_mean, other_mean, *state[2:]
    )


def solution(mesh):
    return jax.shard_map(
        local,
        mesh=mesh,
        in_specs=(
            P("user", None, None, None, None),
            P("user", None, None),
            P("user", None),
            P("user", None),
            P("user", None),
            P("user", None),
            P(),
            P(None, "user", None),
            P(None, "user", None),
        ),
        out_specs=(P("user", None), P("user", None), P("user", None)),
        check_vma=False,
    )
```
